32 devices in a mesh: tx: 4 (over y, core), ty: 8 (over z, x).
Axes of the slice: x: 2, y: 2, z: 4, core: 2. Of those that a mesh axis runs over, the one named last changes fastest.
Arguments:
- schur_slab: bfloat16 [8192, 4096], P(('tx', 'ty')), may hold values from -2.5 to 2.5
- pivot_inverse: bfloat16 [4, 256, 256], replicated
- block_pattern: int32 [4, 2, 32], replicated, may hold values 0 or 1
- column_order: int32 [4, 32], replicated, may hold values from 0 to 31, each once within a row
- pivot_blocks: int32 [4, 32], replicated, may hold values from 0 to 31, each once within a row
Outputs:
- factored_slab: bfloat16 [8192, 4096], P(('tx', 'ty'))
The draws below stay inside these ranges and needn't reach their ends.
Inputs may be any that keep to these rules, and one draw needn't show every extreme that they name: `column_order`: each level's entry is a permutation of the column blocks. `pivot_blocks`: each level's entry is a permutation of the column blocks.
All inputs are finite; a program needn't handle non-finite values.
Results may differ from the reference program's by a relative error of at most 0.0095.
Values may be sent and summed in bfloat16 or wider, within the bound.
No kernel may reach another device: no remote copies, remote signals or barrier semaphores. Data moves between devices by JAX's collectives and lax.ppermute only.
A program may use at most 64 MiB of HBM per device.

```python
import math
import jax
import jax.numpy as jnp
from jax import lax

SEP = 4096
BLOCK = 128
PIVOTS = 256
ROWS = 256
LEVELS = 4
ALL_ROWS = 8192
N_TX = 4
N_TY = 8


def draw_pivot_inverse(key, part):
    key = jax.random.fold_in(key, 7)
    first_key, second_key = jax.random.split(key)
    diagonal = jax.random.uniform(first_key, (LEVELS, PIVOTS), jnp.float32, 0.6, 1.4)
    spread_part = jax.random.normal(second_key, (LEVELS, PIVOTS, PIVOTS), jnp.float32) * (0.35 / math.sqrt(PIVOTS))
    identity = jnp.eye(PIVOTS, dtype=jnp.float32)
    whole_matrix = (spread_part + identity[None] * diagonal[:, :, None]) * (0.5 / math.sqrt(PIVOTS))
    return whole_matrix.astype(jnp.bfloat16)


def plant(drawn, own_key, smallest, top_value):
    longest = drawn.shape.index(max(drawn.shape))
    spots = []
    for shift in (0, 1):
        where = [jax.random.randint(jax.random.fold_in(own_key, axis), (), 0, length) for axis, length in enumerate(drawn.shape)]
        where[longest] = (where[longest] + shift) % drawn.shape[longest]
        spots.append(tuple(where))
    return drawn.at[spots[0]].set(smallest).at[spots[1]].set(top_value)


def level_of(rng, dims, cuts, low, high):
    def one(axis_at, shards_of):
        steps = jax.random.uniform(jax.random.fold_in(jax.random.fold_in(rng, 6), axis_at), (shards_of,), jnp.float32, low / len(cuts), high / len(cuts))
        return jnp.repeat(jnp.exp(steps), dims[axis_at] // shards_of).reshape((-1,) + (1,) * (len(dims) - axis_at - 1))

    loudness = one(*cuts[0])
    for cut in cuts[1:]:
        loudness = loudness * one(*cut)
    return loudness


def bell_draw(key, dims, spread, limit, cuts=(), kind=jnp.bfloat16):
    entries = spread * jax.random.normal(key, dims, jnp.float32)
    if cuts:
        entries = entries * level_of(key, dims, cuts, -0.22, 0.18)
    return jnp.clip(entries, -limit, limit).astype(kind)


def setup_inputs(seed: int = 0) -> dict:
    arg_keys = jax.random.split(jax.random.key(seed), 6)
    schur_slab = bell_draw(arg_keys[0], (ALL_ROWS, SEP), 0.3, 2.5, ((0, 32),))
    pivot_inverse = draw_pivot_inverse(jax.random.fold_in(arg_keys[5], 71), 0)
    block_pattern = plant((jax.random.randint(arg_keys[2], (LEVELS, PIVOTS // BLOCK, SEP // BLOCK), 0, 4) < 3).astype(jnp.int32), jax.random.fold_in(arg_keys[2], 1), 0, 1)
    column_order = jax.vmap(lambda own: jax.random.permutation(own, SEP // BLOCK))(jax.random.split(arg_keys[3], LEVELS)).reshape((LEVELS, SEP // BLOCK)).astype(jnp.int32)
    pivot_blocks = jax.vmap(lambda own: jax.random.permutation(own, SEP // BLOCK))(jax.random.split(arg_keys[4], LEVELS)).reshape((LEVELS, SEP // BLOCK)).astype(jnp.int32)
    return {"schur_slab": schur_slab, "pivot_inverse": pivot_inverse, "block_pattern": block_pattern, "column_order": column_order, "pivot_blocks": pivot_blocks}


def member_table(count, high_bits, offsets_list):
    base = jnp.arange(count, dtype=jnp.int32)
    keep_mask = (count >> high_bits) - 1
    cleared = jnp.bitwise_and(base, jnp.int32(keep_mask))
    offsets = jnp.array(offsets_list, dtype=jnp.int32)
    return cleared[:, None] + offsets[None, :]


def reference(schur_slab, pivot_inverse, block_pattern, column_order, pivot_blocks):
    block_count = SEP // BLOCK
    pivot_count = PIVOTS // BLOCK
    current = schur_slab.reshape(N_TX, N_TY, ROWS, SEP)
    for tier_index in range(LEVELS):
        if tier_index % 2 == 0:
            flipper = N_TX >> (1 + tier_index // 2)
            partner = current[jnp.bitwise_xor(jnp.arange(N_TX, dtype=jnp.int32), flipper)]
        else:
            flipper = N_TY >> (1 + tier_index // 2)
            partner = current[:, jnp.bitwise_xor(jnp.arange(N_TY, dtype=jnp.int32), flipper)]
        group_size = 2 ** (tier_index + 1)
        share = PIVOTS // group_size
        block_order = column_order[tier_index]
        chosen_blocks = pivot_blocks[tier_index, :pivot_count]
        mask_rows = jnp.repeat(block_pattern[tier_index], BLOCK, axis=0).astype(jnp.bfloat16)
        inverse_now = pivot_inverse[tier_index]
        x_offsets = []
        y_offsets = []
        for rank in range(group_size):
            x_part = 0
            y_part = 0
            for step in range(tier_index + 1):
                if (rank >> step) & 1:
                    if step % 2 == 0:
                        x_part += N_TX >> (1 + step // 2)
                    else:
                        y_part += N_TY >> (1 + step // 2)
            x_offsets.append(x_part)
            y_offsets.append(y_part)
        x_bits = tier_index // 2 + 1
        y_bits = (tier_index + 1) // 2
        member_a = member_table(N_TX, x_bits, x_offsets)
        member_b = member_table(N_TY, y_bits, y_offsets)
        moved_top = partner[:, :, :share].reshape(N_TX, N_TY, share, block_count, BLOCK)[:, :, :, block_order]
        top_rows = (current[:, :, :share].astype(jnp.float32) + moved_top.reshape(N_TX, N_TY, share, SEP).astype(jnp.float32)).astype(jnp.bfloat16)

        def merge_line(pair):
            own_slab, other_slab, line_members = pair
            moved = other_slab.reshape(N_TY, ROWS, block_count, BLOCK)[:, :, block_order]
            merged = own_slab.astype(jnp.float32) + moved.reshape(N_TY, ROWS, SEP).astype(jnp.float32)
            panel = top_rows[line_members[None, :], member_b]
            panel = panel.reshape(N_TY, PIVOTS, block_count, BLOCK) * mask_rows[None, :, :, None]
            panel = panel.reshape(N_TY, PIVOTS, SEP)
            coupling = merged.reshape(N_TY, ROWS, block_count, BLOCK)[:, :, chosen_blocks]
            coupling = coupling.reshape(N_TY * ROWS, PIVOTS).astype(jnp.bfloat16)
            weights = jnp.dot(coupling, inverse_now, preferred_element_type=jnp.float32).astype(jnp.bfloat16)
            weights = weights.reshape(N_TY, ROWS, PIVOTS)
            update = jnp.einsum("brp,bps->brs", weights.astype(jnp.float32), panel.astype(jnp.float32))
            result = merged - update
            return result.astype(jnp.bfloat16)

        current = lax.map(merge_line, (current, partner, member_a))
    return current.reshape(N_TX * N_TY * ROWS, SEP)
```

```python
import functools

import jax
import jax.numpy as jnp
from jax import lax
from jax.experimental import pallas as pl
from jax.experimental.pallas import tpu as pltpu
from jax.sharding import PartitionSpec as P

BLOCK = 128
LEVELS = 4
TILE = 2 * BLOCK
F32 = jnp.float32
BF16 = jnp.bfloat16


def stride_bit(axis, level):
    return lax.axis_size(axis).bit_length() - 2 - level // 2


def level_axis(level):
    return "tx" if level % 2 == 0 else "ty"


def trade(block, level):
    axis = level_axis(level)
    flip = 1 << stride_bit(axis, level)
    return lax.ppermute(block, axis, [(i, i ^ flip) for i in range(lax.axis_size(axis))])


def my_bit(level):
    axis = level_axis(level)
    place = lax.axis_index(axis).astype(jnp.int32)
    return jnp.bitwise_and(jnp.right_shift(place, stride_bit(axis, level)), 1)


def cut(pieces, start, rows):
    for ref, low, count in pieces:
        if start < count:
            assert start + rows <= count
            return ref, low + start
        start -= count
    raise ValueError


def segments(one, other):
    edges = {0}
    for pieces in (one, other):
        at = 0
        for _, _, count in pieces:
            at += count
            edges.add(at)
    edges = sorted(edges)
    return [(a, b - a) for a, b in zip(edges[:-1], edges[1:])]


def level_kernel(meta, *refs, base, blocks, n_in, top, pairs, outs, keeps):
    ins, out_refs, rest = refs[:n_in], refs[n_in : n_in + len(outs)], refs[n_in + len(outs) :]
    width = blocks * BLOCK

    def stack(spec):
        return [(ins[i], low, count) for i, low, count in spec]

    def at(j):
        return pl.ds(pl.multiple_of(j * BLOCK, BLOCK), BLOCK)

    def read(pieces, start, rows, j):
        ref, low = cut(pieces, start, rows)
        return ref[pl.ds(low, rows), at(j)].astype(F32)

    def order(j):
        return meta[base + j]

    if top is not None:
        inv, (panel, inv_rel, merged) = ins[0], rest
        a, b = stack(top[0]), stack(top[1])
        half = sum(count for _, _, count in a)
        shift = meta[base + 4 * blocks]
        row_id = lax.broadcasted_iota(jnp.int32, inv.shape, 0)
        col_id = lax.broadcasted_iota(jnp.int32, inv.shape, 1)
        swap = jnp.where(row_id == jnp.bitwise_xor(col_id, shift), 1.0, 0.0).astype(BF16)
        inv_rel[...] = jnp.dot(inv[...], swap, preferred_element_type=F32).astype(BF16)

        def merge_block(j, carry):
            other = order(j)
            keep_a = meta[base + blocks + j].astype(F32)
            keep_b = meta[base + 2 * blocks + j].astype(F32)
            for start, rows in segments(a, b):
                from_a = read(a, start, rows, j) + read(b, start, rows, other)
                from_b = read(b, start, rows, j) + read(a, start, rows, other)
                low, high = pl.ds(start, rows), pl.ds(half + start, rows)
                merged[low, at(j)] = from_a
                merged[high, at(j)] = from_b
                panel[low, at(j)] = (from_a * keep_a).astype(BF16)
                panel[high, at(j)] = (from_b * keep_b).astype(BF16)
            return carry

        lax.fori_loop(0, blocks, merge_block, 0, unroll=4)
    else:
        panel, inv_rel = ins[0], ins[1]

    def columns(job, j):
        source, start, rows = job
        if source == "top":
            return merged[pl.ds(start, rows), at(j)]
        a, b = (stack(s) for s in pairs[source])
        return read(a, start, rows, j) + read(b, start, rows, order(j))

    jobs = [job for dest in outs for job in dest]
    pivots = [meta[base + 3 * blocks + i] for i in range(inv_rel.shape[0] // BLOCK)]
    coupling = jnp.concatenate(
        [jnp.concatenate([columns(job, p) for p in pivots], axis=1).astype(BF16) for job in jobs],
        axis=0,
    )
    weights = jnp.dot(coupling, inv_rel[...], preferred_element_type=F32).astype(BF16)

    def finish_tile(t, carry):
        lanes = pl.ds(pl.multiple_of(t * TILE, TILE), TILE)
        update = jnp.dot(weights, panel[:, lanes], preferred_element_type=F32)
        done = 0
        for out, dest in zip(out_refs, outs):
            put = 0
            for job in dest:
                rows = job[2]
                for i in range(TILE // BLOCK):
                    j = (TILE // BLOCK) * t + i
                    part = update[done : done + rows, i * BLOCK : (i + 1) * BLOCK]
                    out[pl.ds(put, rows), at(j)] = (columns(job, j) - part).astype(BF16)
                put += rows
                done += rows
        return carry

    lax.fori_loop(0, width // TILE, finish_tile, 0, unroll=4)


def run_level(level, meta, held, outs, pairs=(), top=None, keeps=False):
    arrays = list(held)

    def spec(stack):
        named = []
        for x, low, rows in stack:
            found = [i for i, seen in enumerate(arrays) if seen is x]
            if not found:
                arrays.append(x)
            named.append((found[0] if found else len(arrays) - 1, low, rows))
        return tuple(named)

    top_spec = None if top is None else (spec(top[0]), spec(top[1]))
    pair_specs = tuple((spec(a), spec(b)) for a, b in pairs)
    width = arrays[-1].shape[1]
    size = held[-1].shape[0]
    shapes = [jax.ShapeDtypeStruct((sum(job[2] for job in dest), width), BF16) for dest in outs]
    rows = sum(shape.shape[0] for shape in shapes)
    scratch = []
    if top is not None:
        tails = [(size, width), (size, size)]
        if keeps:
            shapes += [jax.ShapeDtypeStruct(s, BF16) for s in tails]
        else:
            scratch += [pltpu.VMEM(s, BF16) for s in tails]
        scratch.append(pltpu.VMEM((size, width), F32))
    blocks = width // BLOCK
    kernel = functools.partial(
        level_kernel,
        base=level * meta.shape[0] // LEVELS,
        blocks=blocks,
        n_in=len(arrays),
        top=top_spec,
        pairs=pair_specs,
        outs=tuple(tuple(dest) for dest in outs),
        keeps=keeps,
    )
    return pl.pallas_call(
        kernel,
        out_shape=shapes,
        in_specs=[pl.BlockSpec(memory_space=pltpu.SMEM)]
        + [pl.BlockSpec(memory_space=pltpu.VMEM)] * len(arrays),
        out_specs=[pl.BlockSpec(memory_space=pltpu.VMEM)] * len(shapes),
        scratch_shapes=scratch,
        compiler_params=pltpu.CompilerParams(vmem_limit_bytes=30 * 2**20),
        cost_estimate=pl.CostEstimate(
            flops=2 * rows * size * (width + size),
            bytes_accessed=sum(x.size * 2 for x in arrays) + sum(s.size * 2 for s in shapes),
            transcendentals=0,
        ),
        name=f"level{level}_rows{rows}",
    )(meta, *arrays)


def on_device(schur_slab, pivot_inverse, block_pattern, column_order, pivot_blocks):
    size = pivot_inverse.shape[1]
    blocks = schur_slab.shape[1] // BLOCK
    half = size // 2
    quarter = half // 2
    eighth = quarter // 2
    rank = jnp.int32(0)
    meta = []
    for level in range(LEVELS):
        bit = my_bit(level)
        rank = rank + bit * (1 << level)
        shift = rank * (size >> (level + 1))
        meta += [
            column_order[level],
            jnp.where(bit == 0, block_pattern[level, 0], block_pattern[level, 1]),
            jnp.where(bit == 0, block_pattern[level, 1], block_pattern[level, 0]),
            pivot_blocks[level],
            jnp.zeros((blocks,), jnp.int32) + shift,
        ]
    meta = jnp.concatenate(meta)

    first = schur_slab[:half]
    first_1, first_2 = schur_slab[:quarter], schur_slab[quarter:half]
    rest_1, rest_2 = schur_slab[half : half + quarter], schur_slab[half + quarter :]

    first_y = trade(first, 0)
    first_z1 = trade(first_1, 1)
    first_z2 = trade(first_2, 1)
    first_yz1 = trade(first_z1, 0)
    rest_y1 = trade(rest_1, 0)
    first_yz2 = trade(first_z2, 0)
    rest_y2 = trade(rest_2, 0)

    tops = [("top", 0, quarter), ("top", half, quarter)]
    near, near_x, panel, inv = run_level(
        0,
        meta,
        (pivot_inverse[0],),
        [tops, [("top", quarter, quarter)]],
        top=([(first, 0, half)], [(first_y, 0, half)]),
        keeps=True,
    )
    (after_1,) = run_level(
        0, meta, (panel, inv), [[(0, 0, quarter)]], pairs=[([(rest_1, 0, quarter)], [(rest_y1, 0, quarter)])]
    )
    (after_2,) = run_level(
        0, meta, (panel, inv), [[(0, 0, quarter)]], pairs=[([(rest_2, 0, quarter)], [(rest_y2, 0, quarter)])]
    )
    far, far_x = run_level(
        0,
        meta,
        (pivot_inverse[0],),
        [tops, [("top", quarter, quarter)]],
        top=(
            [(first_z1, 0, quarter), (first_z2, 0, quarter)],
            [(first_yz1, 0, quarter), (first_yz2, 0, quarter)],
        ),
    )

    after_z1 = trade(after_1, 1)
    after_z2 = trade(after_2, 1)
    tops = [("top", low, eighth) for low in range(0, size, quarter)]
    head, panel, inv = run_level(
        1,
        meta,
        (pivot_inverse[1],),
        [tops + [("top", eighth, eighth), (0, 0, quarter)]],
        top=([(near, 0, half)], [(far, 0, half)]),
        pairs=[([(near_x, 0, quarter)], [(far_x, 0, quarter)])],
        keeps=True,
    )
    (next_1,) = run_level(
        1, meta, (panel, inv), [[(0, 0, quarter)]], pairs=[([(after_1, 0, quarter)], [(after_z1, 0, quarter)])]
    )
    (next_2,) = run_level(
        1, meta, (panel, inv), [[(0, 0, quarter)]], pairs=[([(after_2, 0, quarter)], [(after_z2, 0, quarter)])]
    )

    head_c = trade(head, 2)
    next_c1 = trade(next_1, 2)
    next_c2 = trade(next_2, 2)
    more = head.shape[0] - half
    share = eighth // 2
    tops_a = [("top", low, share) for low in range(0, half, eighth)]
    tops_b = [("top", half + low, share) for low in range(0, half, eighth)]
    lead, other_tops, panel, inv = run_level(
        2,
        meta,
        (pivot_inverse[2],),
        [tops_a + [("top", share, share), (0, 0, more)], tops_b],
        top=([(head, 0, half)], [(head_c, 0, half)]),
        pairs=[([(head, half, more)], [(head_c, half, more)])],
        keeps=True,
    )
    (last_1,) = run_level(
        2, meta, (panel, inv), [[(0, 0, quarter)]], pairs=[([(next_1, 0, quarter)], [(next_c1, 0, quarter)])]
    )
    (last_2,) = run_level(
        2, meta, (panel, inv), [[(0, 0, quarter)]], pairs=[([(next_2, 0, quarter)], [(next_c2, 0, quarter)])]
    )

    lead_w = trade(lead, 3)
    tops_cw = trade(lead_w[:quarter], 2)
    last_w1 = trade(last_1, 3)
    last_w2 = trade(last_2, 3)
    more = lead.shape[0] - quarter
    (out,) = run_level(
        3,
        meta,
        (pivot_inverse[3],),
        [[("top", 0, share), (0, 0, more), (1, 0, quarter), (2, 0, quarter)]],
        top=([(lead, 0, quarter), (other_tops, 0, quarter)], [(lead_w, 0, quarter), (tops_cw, 0, quarter)]),
        pairs=[
            ([(lead, quarter, more)], [(lead_w, quarter, more)]),
            ([(last_1, 0, quarter)], [(last_w1, 0, quarter)]),
            ([(last_2, 0, quarter)], [(last_w2, 0, quarter)]),
        ],
    )
    return out


def solution(mesh):
    return jax.shard_map(
        on_device,
        mesh=mesh,
        in_specs=(P(("tx", "ty"), None), P(), P(), P(), P()),
        out_specs=P(("tx", "ty"), None),
        check_vma=False,
    )
```

```python
import functools

import jax
import jax.numpy as jnp
from jax import lax
from jax.experimental import pallas as pl
from jax.experimental.pallas import tpu as pltpu
from jax.sharding import PartitionSpec as P

BLOCK = 128
LEVELS = 4
TILE = 2 * BLOCK
F32 = jnp.float32
BF16 = jnp.bfloat16


def stride_bit(axis, level):
    return lax.axis_size(axis).bit_length() - 2 - level // 2


def level_axis(level):
    return "tx" if level % 2 == 0 else "ty"


def trade(block, level):
    axis = level_axis(level)
    flip = 1 << stride_bit(axis, level)
    return lax.ppermute(block, axis, [(i, i ^ flip) for i in range(lax.axis_size(axis))])


def my_bit(level):
    axis = level_axis(level)
    place = lax.axis_index(axis).astype(jnp.int32)
    return jnp.bitwise_and(jnp.right_shift(place, stride_bit(axis, level)), 1)


def after(x, *others):
    return lax.optimization_barrier((x, *others))


def cut(pieces, start, rows):
    for ref, low, count in pieces:
        if start < count:
            assert start + rows <= count
            return ref, low + start
        start -= count
    raise ValueError


def segments(one, other):
    edges = {0}
    for pieces in (one, other):
        at = 0
        for _, _, count in pieces:
            at += count
            edges.add(at)
    edges = sorted(edges)
    return [(a, b - a) for a, b in zip(edges[:-1], edges[1:])]


def reorder_kernel(meta, inv, out, *, step):
    for level in range(LEVELS):
        shape = inv.shape[1:]
        row_id = lax.broadcasted_iota(jnp.int32, shape, 0)
        col_id = lax.broadcasted_iota(jnp.int32, shape, 1)
        source = jnp.bitwise_xor(col_id, meta[step * (level + 1) - 1])
        swap = jnp.where(row_id == source, 1.0, 0.0).astype(BF16)
        out[level] = jnp.dot(inv[level], swap, preferred_element_type=F32).astype(BF16)


def level_kernel(meta, *refs, base, level, blocks, n_in, top, pairs, outs, n_hidden):
    ins, rest = refs[:n_in], refs[n_in + n_hidden :]
    out_refs, rest = rest[: len(outs)], rest[len(outs) :]
    width = blocks * BLOCK

    def stack(spec):
        return [(ins[i], low, count) for i, low, count in spec]

    def at(j):
        return pl.ds(pl.multiple_of(j * BLOCK, BLOCK), BLOCK)

    def read(pieces, start, rows, j):
        ref, low = cut(pieces, start, rows)
        return ref[pl.ds(low, rows), at(j)].astype(F32)

    def order(j):
        return meta[base + j]

    inv = ins[0]
    if top is not None:
        panel, merged = rest
        a, b = stack(top[0]), stack(top[1])
        half = sum(count for _, _, count in a)

        def merge_block(j, carry):
            other = order(j)
            keep_a = meta[base + blocks + j].astype(F32)
            keep_b = meta[base + 2 * blocks + j].astype(F32)
            for start, rows in segments(a, b):
                from_a = read(a, start, rows, j) + read(b, start, rows, other)
                from_b = read(b, start, rows, j) + read(a, start, rows, other)
                low, high = pl.ds(start, rows), pl.ds(half + start, rows)
                merged[low, at(j)] = from_a
                merged[high, at(j)] = from_b
                panel[low, at(j)] = (from_a * keep_a).astype(BF16)
                panel[high, at(j)] = (from_b * keep_b).astype(BF16)
            return carry

        lax.fori_loop(0, blocks, merge_block, 0, unroll=4)
    else:
        panel = ins[1]

    def columns(job, j):
        source, start, rows = job
        if source == "top":
            return merged[pl.ds(start, rows), at(j)]
        a, b = (stack(s) for s in pairs[source])
        return read(a, start, rows, j) + read(b, start, rows, order(j))

    jobs = [job for dest in outs for job in dest]
    pivots = [meta[base + 3 * blocks + i] for i in range(inv.shape[1] // BLOCK)]
    coupling = jnp.concatenate(
        [jnp.concatenate([columns(job, p) for p in pivots], axis=1).astype(BF16) for job in jobs],
        axis=0,
    )
    weights = jnp.dot(coupling, inv[level], preferred_element_type=F32).astype(BF16)

    def finish_tile(t, carry):
        lanes = pl.ds(pl.multiple_of(t * TILE, TILE), TILE)
        update = jnp.dot(weights, panel[:, lanes], preferred_element_type=F32)
        done = 0
        for out, dest in zip(out_refs, outs):
            put = 0
            for job in dest:
                rows = job[2]
                for i in range(TILE // BLOCK):
                    j = (TILE // BLOCK) * t + i
                    part = update[done : done + rows, i * BLOCK : (i + 1) * BLOCK]
                    out[pl.ds(put, rows), at(j)] = (columns(job, j) - part).astype(BF16)
                put += rows
                done += rows
        return carry

    lax.fori_loop(0, width // TILE, finish_tile, 0, unroll=4)


def run_level(level, meta, held, outs, pairs=(), top=None, keeps=False, part=None, cost=0):
    arrays = list(held)

    def spec(stack):
        named = []
        for x, low, rows in stack:
            found = [i for i, seen in enumerate(arrays) if seen is x]
            if not found:
                arrays.append(x)
            named.append((found[0] if found else len(arrays) - 1, low, rows))
        return tuple(named)

    top_spec = None if top is None else (spec(top[0]), spec(top[1]))
    pair_specs = tuple((spec(a), spec(b)) for a, b in pairs)
    n_in = len(arrays)
    width = arrays[-1].shape[1]
    size = held[0].shape[1]
    counts = [sum(job[2] for job in dest) for dest in outs]
    shapes = [jax.ShapeDtypeStruct((rows, width), BF16) for rows in counts]
    whole = pl.BlockSpec(memory_space=pltpu.VMEM)
    in_specs = [pl.BlockSpec(memory_space=pltpu.SMEM)] + [whole] * n_in
    out_specs = [whole] * len(shapes)
    aliases = {}
    hidden = []
    if part is not None:
        all_rows, block, old = part
        shapes[0] = jax.ShapeDtypeStruct((all_rows, width), BF16)
        out_specs[0] = pl.BlockSpec((counts[0], width), lambda i: (block, 0))
        if old is not None:
            hidden = [old]
            in_specs.append(pl.BlockSpec(memory_space=pl.ANY))
            aliases = {1 + n_in: 0}
    scratch = []
    if top is not None:
        if keeps:
            shapes.append(jax.ShapeDtypeStruct((size, width), BF16))
            out_specs.append(whole)
        else:
            scratch.append(pltpu.VMEM((size, width), BF16))
        scratch.append(pltpu.VMEM((size, width), F32))
    kernel = functools.partial(
        level_kernel,
        base=level * meta.shape[0] // LEVELS,
        level=level,
        blocks=width // BLOCK,
        n_in=n_in,
        top=top_spec,
        pairs=pair_specs,
        outs=tuple(tuple(dest) for dest in outs),
        n_hidden=len(hidden),
    )
    return pl.pallas_call(
        kernel,
        grid=(1,) if part is not None else (),
        out_shape=shapes,
        in_specs=in_specs,
        out_specs=out_specs,
        scratch_shapes=scratch,
        input_output_aliases=aliases,
        compiler_params=pltpu.CompilerParams(vmem_limit_bytes=30 * 2**20),
        cost_estimate=pl.CostEstimate(flops=cost, bytes_accessed=0, transcendentals=0),
        name=f"level{level}_rows{sum(counts)}",
    )(meta, *arrays, *hidden)


def reorder(meta, pivot_inverse):
    step = meta.shape[0] // LEVELS
    return pl.pallas_call(
        functools.partial(reorder_kernel, step=step),
        out_shape=jax.ShapeDtypeStruct(pivot_inverse.shape, BF16),
        in_specs=[pl.BlockSpec(memory_space=pltpu.SMEM), pl.BlockSpec(memory_space=pltpu.VMEM)],
        out_specs=pl.BlockSpec(memory_space=pltpu.VMEM),
        compiler_params=pltpu.CompilerParams(vmem_limit_bytes=30 * 2**20),
        cost_estimate=pl.CostEstimate(flops=0, bytes_accessed=0, transcendentals=0),
        name="reorder",
    )(meta, pivot_inverse)


def make_meta(size, block_pattern, column_order, pivot_blocks):
    blocks = column_order.shape[1]
    rank = jnp.int32(0)
    meta = []
    for level in range(LEVELS):
        bit = my_bit(level)
        rank = rank + bit * (1 << level)
        shift = rank * (size >> (level + 1))
        meta += [
            column_order[level],
            jnp.where(bit == 0, block_pattern[level, 0], block_pattern[level, 1]),
            jnp.where(bit == 0, block_pattern[level, 1], block_pattern[level, 0]),
            pivot_blocks[level],
            jnp.zeros((blocks,), jnp.int32) + shift,
        ]
    return jnp.concatenate(meta)


def on_device(schur_slab, pivot_inverse, block_pattern, column_order, pivot_blocks):
    all_rows = schur_slab.shape[0]
    size = pivot_inverse.shape[1]
    half, quarter, eighth, share = size // 2, size // 4, size // 8, size // 16
    meta = make_meta(size, block_pattern, column_order, pivot_blocks)

    def rows_of(x):
        return [(x, 0, x.shape[0])]

    def chunk(level, panel, own, other, **more):
        (out,) = run_level(
            level, meta, (inv, panel), [[(0, 0, own.shape[0])]], pairs=[(rows_of(own), rows_of(other))], **more
        )
        return out

    first_1 = schur_slab[:quarter]
    first_z1 = trade(first_1, 1)
    slab, first_1 = after(schur_slab, first_1)
    first = slab[:half]
    first_y = trade(first, 0)
    slab, first = after(slab, first)
    first_2 = slab[quarter:half]
    rest_1, rest_2 = slab[half : half + quarter], slab[half + quarter :]
    inv = reorder(meta, pivot_inverse)

    first_yz1 = trade(first_z1, 0)
    first_2, first_z1 = after(first_2, first_z1)
    first_z2 = trade(first_2, 1)
    rest_1, first_y = after(rest_1, first_y)
    rest_y1 = trade(rest_1, 0)

    tops = [("top", 0, quarter), ("top", half, quarter)]
    near, near_x, panel_0 = run_level(
        0, meta, (inv,), [tops, [("top", quarter, quarter)]], top=(rows_of(first), rows_of(first_y)), keeps=True
    )
    after_1 = chunk(0, panel_0, rest_1, rest_y1)
    first_z2, after_1, first_yz1 = after(first_z2, after_1, first_yz1)
    first_yz2 = trade(first_z2, 0)
    after_z1 = trade(after_1, 1)
    rest_2, first_yz2 = after(rest_2, first_yz2)
    rest_y2 = trade(rest_2, 0)
    far, far_x = run_level(
        0,
        meta,
        (inv,),
        [tops, [("top", quarter, quarter)]],
        top=(rows_of(first_z1) + rows_of(first_z2), rows_of(first_yz1) + rows_of(first_yz2)),
    )

    tops = [("top", low, eighth) for low in range(0, size, quarter)]
    head, panel_1 = run_level(1, meta, (inv,), [tops], top=(rows_of(near), rows_of(far)), keeps=True)
    head_c = trade(head, 2)
    rest_y2, after_z1 = after(rest_y2, after_z1)
    after_2 = chunk(0, panel_0, rest_2, rest_y2, cost=10**10)
    after_z2 = trade(after_2, 1)
    head_c, after_2 = after(head_c, after_2)

    tops = [("top", low, share) for low in range(0, size, eighth)]
    mine, others, panel_2 = run_level(
        2,
        meta,
        (inv,),
        [[tops[0], tops[2]], [tops[i] for i in (1, 3, 4, 5, 6, 7)]],
        top=(rows_of(head), rows_of(head_c)),
        keeps=True,
    )
    mine_w = trade(mine, 3)
    after_z1, mine = after(after_z1, mine)
    (next_1,) = run_level(
        1,
        meta,
        (inv, panel_1),
        [[(0, 0, eighth), (1, 0, quarter), (2, 0, quarter)]],
        pairs=[
            ([(near, eighth, eighth)], [(far, eighth, eighth)]),
            (rows_of(near_x), rows_of(far_x)),
            (rows_of(after_1), rows_of(after_z1)),
        ],
    )
    next_c1 = trade(next_1, 2)
    (last_1,) = run_level(
        2,
        meta,
        (inv, panel_2),
        [[(0, 0, share), (1, 0, next_1.shape[0])]],
        pairs=[
            ([(head, share, share)], [(head_c, share, share)]),
            (rows_of(next_1), rows_of(next_c1)),
        ],
    )
    last_w1 = trade(last_1, 3)
    mine_wy = trade(mine_w, 0)
    mine_wc = trade(mine_w, 2)
    after_z2, mine_w, last_1 = after(after_z2, mine_w, last_1)
    next_2 = chunk(1, panel_1, after_2, after_z2)
    last_2 = chunk(2, panel_2, next_2, trade(next_2, 2))
    last_w2 = trade(last_2, 3)
    mine_wy, last_2 = after(mine_wy, last_2)
    mine_wyc = trade(mine_wy, 2)

    last_w1, mine_wyc, last_2 = after(last_w1, mine_wyc, last_2)
    tops = [(mine, 0, share), (others, 0, share), (mine, share, share)]
    tops += [(others, share * i, share) for i in range(1, 6)]
    tops_w = [(x, low, share) for low in (0, share) for x in (mine_w, mine_wy)]
    tops_w += [(x, low, share) for low in (0, share) for x in (mine_wc, mine_wyc)]
    out, panel_3 = run_level(
        3,
        meta,
        (inv,),
        [[("top", 0, share), (0, 0, last_1.shape[0])]],
        top=(tops, tops_w),
        pairs=[(rows_of(last_1), rows_of(last_w1))],
        keeps=True,
        part=(all_rows, 0, None),
    )
    return chunk(3, panel_3, last_2, last_w2, part=(all_rows, all_rows // quarter - 1, out))


def solution(mesh):
    return jax.shard_map(
        on_device,
        mesh=mesh,
        in_specs=(P(("tx", "ty"), None), P(), P(), P(), P()),
        out_specs=P(("tx", "ty"), None),
        check_vma=False,
    )
```

```python
import functools

import jax
import jax.numpy as jnp
from jax import lax
from jax.experimental import pallas as pl
from jax.experimental.pallas import tpu as pltpu
from jax.sharding import PartitionSpec as P

BLOCK = 128
LEVELS = 4
TILE = 2 * BLOCK
F32 = jnp.float32
BF16 = jnp.bfloat16


def stride_bit(axis, level):
    return lax.axis_size(axis).bit_length() - 2 - level // 2


def level_axis(level):
    return "tx" if level % 2 == 0 else "ty"


def trade(block, level):
    axis = level_axis(level)
    flip = 1 << stride_bit(axis, level)
    return lax.ppermute(block, axis, [(i, i ^ flip) for i in range(lax.axis_size(axis))])


def my_bit(level):
    axis = level_axis(level)
    place = lax.axis_index(axis).astype(jnp.int32)
    return jnp.bitwise_and(jnp.right_shift(place, stride_bit(axis, level)), 1)


def after(x, *others):
    return lax.optimization_barrier((x, *others))


def cut(pieces, start, rows):
    for ref, low, count in pieces:
        if start < count:
            assert start + rows <= count
            return ref, low + start
        start -= count
    raise ValueError


def segments(one, other):
    edges = {0}
    for pieces in (one, other):
        at = 0
        for _, _, count in pieces:
            at += count
            edges.add(at)
    edges = sorted(edges)
    return [(a, b - a) for a, b in zip(edges[:-1], edges[1:])]


def reorder_kernel(meta, inv, out, *, step):
    for level in range(LEVELS):
        shape = inv.shape[1:]
        row_id = lax.broadcasted_iota(jnp.int32, shape, 0)
        col_id = lax.broadcasted_iota(jnp.int32, shape, 1)
        source = jnp.bitwise_xor(col_id, meta[step * (level + 1) - 1])
        swap = jnp.where(row_id == source, 1.0, 0.0).astype(BF16)
        out[level] = jnp.dot(inv[level], swap, preferred_element_type=F32).astype(BF16)


def level_kernel(meta, *refs, base, level, blocks, n_in, top, pairs, outs, n_hidden):
    ins, rest = refs[:n_in], refs[n_in + n_hidden :]
    out_refs, rest = rest[: len(outs)], rest[len(outs) :]
    width = blocks * BLOCK

    def stack(spec):
        return [(ins[i], low, count) for i, low, count in spec]

    def at(j):
        return pl.ds(pl.multiple_of(j * BLOCK, BLOCK), BLOCK)

    def read(pieces, start, rows, j):
        ref, low = cut(pieces, start, rows)
        return ref[pl.ds(low, rows), at(j)].astype(F32)

    def order(j):
        return meta[base + j]

    inv = ins[0]
    if top is not None:
        panel, merged = rest
        a, b = stack(top[0]), stack(top[1])
        half = sum(count for _, _, count in a)

        def merge_block(j, carry):
            other = order(j)
            keep_a = meta[base + blocks + j].astype(F32)
            keep_b = meta[base + 2 * blocks + j].astype(F32)
            for start, rows in segments(a, b):
                from_a = read(a, start, rows, j) + read(b, start, rows, other)
                from_b = read(b, start, rows, j) + read(a, start, rows, other)
                low, high = pl.ds(start, rows), pl.ds(half + start, rows)
                merged[low, at(j)] = from_a
                merged[high, at(j)] = from_b
                panel[low, at(j)] = (from_a * keep_a).astype(BF16)
                panel[high, at(j)] = (from_b * keep_b).astype(BF16)
            return carry

        lax.fori_loop(0, blocks, merge_block, 0, unroll=4)
    else:
        panel = ins[1]

    def columns(job, j):
        source, start, rows = job
        if source == "top":
            return merged[pl.ds(start, rows), at(j)]
        a, b = (stack(s) for s in pairs[source])
        return read(a, start, rows, j) + read(b, start, rows, order(j))

    jobs = [job for dest in outs for job in dest]
    pivots = [meta[base + 3 * blocks + i] for i in range(inv.shape[1] // BLOCK)]
    coupling = jnp.concatenate(
        [jnp.concatenate([columns(job, p) for p in pivots], axis=1).astype(BF16) for job in jobs],
        axis=0,
    )
    weights = jnp.dot(coupling, inv[level], preferred_element_type=F32).astype(BF16)

    def finish_tile(t, carry):
        lanes = pl.ds(pl.multiple_of(t * TILE, TILE), TILE)
        update = jnp.dot(weights, panel[:, lanes], preferred_element_type=F32)
        done = 0
        for out, dest in zip(out_refs, outs):
            put = 0
            for job in dest:
                rows = job[2]
                for i in range(TILE // BLOCK):
                    j = (TILE // BLOCK) * t + i
                    part = update[done : done + rows, i * BLOCK : (i + 1) * BLOCK]
                    out[pl.ds(put, rows), at(j)] = (columns(job, j) - part).astype(BF16)
                put += rows
                done += rows
        return carry

    lax.fori_loop(0, width // TILE, finish_tile, 0, unroll=4)


def run_level(level, meta, held, outs, pairs=(), top=None, keeps=False, part=None, cost=0):
    arrays = list(held)

    def spec(stack):
        named = []
        for x, low, rows in stack:
            found = [i for i, seen in enumerate(arrays) if seen is x]
            if not found:
                arrays.append(x)
            named.append((found[0] if found else len(arrays) - 1, low, rows))
        return tuple(named)

    top_spec = None if top is None else (spec(top[0]), spec(top[1]))
    pair_specs = tuple((spec(a), spec(b)) for a, b in pairs)
    n_in = len(arrays)
    width = arrays[-1].shape[1]
    size = held[0].shape[1]
    counts = [sum(job[2] for job in dest) for dest in outs]
    shapes = [jax.ShapeDtypeStruct((rows, width), BF16) for rows in counts]
    whole = pl.BlockSpec(memory_space=pltpu.VMEM)
    in_specs = [pl.BlockSpec(memory_space=pltpu.SMEM)] + [whole] * n_in
    out_specs = [whole] * len(shapes)
    aliases = {}
    hidden = []
    if part is not None:
        all_rows, block, old = part
        shapes[0] = jax.ShapeDtypeStruct((all_rows, width), BF16)
        out_specs[0] = pl.BlockSpec((counts[0], width), lambda i: (block, 0))
        if old is not None:
            hidden = [old]
            in_specs.append(pl.BlockSpec(memory_space=pl.ANY))
            aliases = {1 + n_in: 0}
    scratch = []
    if top is not None:
        if keeps:
            shapes.append(jax.ShapeDtypeStruct((size, width), BF16))
            out_specs.append(whole)
        else:
            scratch.append(pltpu.VMEM((size, width), BF16))
        scratch.append(pltpu.VMEM((size, width), F32))
    kernel = functools.partial(
        level_kernel,
        base=level * meta.shape[0] // LEVELS,
        level=level,
        blocks=width // BLOCK,
        n_in=n_in,
        top=top_spec,
        pairs=pair_specs,
        outs=tuple(tuple(dest) for dest in outs),
        n_hidden=len(hidden),
    )
    return pl.pallas_call(
        kernel,
        grid=(1,) if part is not None else (),
        out_shape=shapes,
        in_specs=in_specs,
        out_specs=out_specs,
        scratch_shapes=scratch,
        input_output_aliases=aliases,
        compiler_params=pltpu.CompilerParams(vmem_limit_bytes=30 * 2**20),
        cost_estimate=pl.CostEstimate(flops=cost, bytes_accessed=0, transcendentals=0),
        name=f"level{level}_rows{sum(counts)}",
    )(meta, *arrays, *hidden)


def reorder(meta, pivot_inverse):
    step = meta.shape[0] // LEVELS
    return pl.pallas_call(
        functools.partial(reorder_kernel, step=step),
        out_shape=jax.ShapeDtypeStruct(pivot_inverse.shape, BF16),
        in_specs=[pl.BlockSpec(memory_space=pltpu.SMEM), pl.BlockSpec(memory_space=pltpu.VMEM)],
        out_specs=pl.BlockSpec(memory_space=pltpu.VMEM),
        compiler_params=pltpu.CompilerParams(vmem_limit_bytes=30 * 2**20),
        cost_estimate=pl.CostEstimate(flops=0, bytes_accessed=0, transcendentals=0),
        name="reorder",
    )(meta, pivot_inverse)


def make_meta(size, block_pattern, column_order, pivot_blocks):
    blocks = column_order.shape[1]
    rank = jnp.int32(0)
    meta = []
    for level in range(LEVELS):
        bit = my_bit(level)
        rank = rank + bit * (1 << level)
        shift = rank * (size >> (level + 1))
        meta += [
            column_order[level],
            jnp.where(bit == 0, block_pattern[level, 0], block_pattern[level, 1]),
            jnp.where(bit == 0, block_pattern[level, 1], block_pattern[level, 0]),
            pivot_blocks[level],
            jnp.zeros((blocks,), jnp.int32) + shift,
        ]
    return jnp.concatenate(meta)


def on_device(schur_slab, pivot_inverse, block_pattern, column_order, pivot_blocks):
    all_rows = schur_slab.shape[0]
    size = pivot_inverse.shape[1]
    half, quarter, eighth, share = size // 2, size // 4, size // 8, size // 16
    meta = make_meta(size, block_pattern, column_order, pivot_blocks)

    def rows_of(x):
        return [(x, 0, x.shape[0])]

    def chunk(level, panel, own, other, **more):
        (out,) = run_level(
            level, meta, (inv, panel), [[(0, 0, own.shape[0])]], pairs=[(rows_of(own), rows_of(other))], **more
        )
        return out

    first_1 = schur_slab[:quarter]
    first_z1 = trade(first_1, 1)
    slab, first_1 = after(schur_slab, first_1)
    first = slab[:half]
    first_y = trade(first, 0)
    slab, first = after(slab, first)
    first_2 = slab[quarter:half]
    rest_1, rest_2 = slab[half : half + quarter], slab[half + quarter :]
    inv = reorder(meta, pivot_inverse)

    first_yz1 = trade(first_z1, 0)
    first_2, first_z1 = after(first_2, first_z1)
    first_z2 = trade(first_2, 1)
    rest_1, first_y = after(rest_1, first_y)
    rest_y1 = trade(rest_1, 0)

    tops = [("top", 0, quarter), ("top", half, quarter)]
    near, near_x, panel_0 = run_level(
        0, meta, (inv,), [tops, [("top", quarter, quarter)]], top=(rows_of(first), rows_of(first_y)), keeps=True
    )
    after_1 = chunk(0, panel_0, rest_1, rest_y1)
    first_z2, after_1, first_yz1 = after(first_z2, after_1, first_yz1)
    first_yz2 = trade(first_z2, 0)
    after_z1 = trade(after_1, 1)
    rest_2, first_yz2 = after(rest_2, first_yz2)
    rest_y2 = trade(rest_2, 0)
    far, far_x = run_level(
        0,
        meta,
        (inv,),
        [tops, [("top", quarter, quarter)]],
        top=(rows_of(first_z1) + rows_of(first_z2), rows_of(first_yz1) + rows_of(first_yz2)),
    )

    tops = [("top", low, eighth) for low in range(0, size, quarter)]
    head, panel_1 = run_level(
        1,
        meta,
        (inv,),
        [tops + [("top", eighth, eighth), (0, 0, quarter)]],
        top=(rows_of(near), rows_of(far)),
        pairs=[(rows_of(near_x), rows_of(far_x))],
        keeps=True,
    )
    head_c = trade(head, 2)
    rest_y2, after_z1 = after(rest_y2, after_z1)
    after_2 = chunk(0, panel_0, rest_2, rest_y2, cost=3 * 10**10)
    after_z2 = trade(after_2, 1)
    head_c, after_2 = after(head_c, after_2)

    more = head.shape[0] - half
    tops = [("top", low, share) for low in range(0, size, eighth)]
    lead, others, panel_2 = run_level(
        2,
        meta,
        (inv,),
        [
            [tops[0], tops[2], ("top", share, share), (0, 0, more)],
            [tops[i] for i in (1, 3, 4, 5, 6, 7)],
        ],
        top=([(head, 0, half)], [(head_c, 0, half)]),
        pairs=[([(head, half, more)], [(head_c, half, more)])],
        keeps=True,
    )
    lead_w = trade(lead, 3)
    after_z1, lead = after(after_z1, lead)
    next_1a, next_1b = run_level(
        1,
        meta,
        (inv, panel_1),
        [[(0, 0, eighth)], [(0, eighth, eighth)]],
        pairs=[(rows_of(after_1), rows_of(after_z1))],
    )
    (last_1,) = run_level(
        2,
        meta,
        (inv, panel_2),
        [[(0, 0, eighth), (1, 0, eighth)]],
        pairs=[(rows_of(x), rows_of(trade(x, 2))) for x in (next_1a, next_1b)],
    )
    last_w1 = trade(last_1, 3)
    after_z2, last_1 = after(after_z2, last_1)
    next_2 = chunk(1, panel_1, after_2, after_z2, cost=25 * 10**8)
    last_2 = chunk(2, panel_2, next_2, trade(next_2, 2))
    last_w2 = trade(last_2, 3)
    lead_w, last_2 = after(lead_w, last_2)
    tops_w = lead_w[:eighth]
    tops_wc = trade(tops_w, 2)
    tops_wy = trade(tops_w, 0)
    tops_wyc = trade(tops_wy, 2)

    more = lead.shape[0] - eighth
    tops = [(lead, 0, share), (others, 0, share), (lead, share, share)]
    tops += [(others, share * i, share) for i in range(1, 6)]
    tops_other = [(x, low, share) for low in (0, share) for x in (tops_w, tops_wy)]
    tops_other += [(x, low, share) for low in (0, share) for x in (tops_wc, tops_wyc)]
    out, panel_3 = run_level(
        3,
        meta,
        (inv,),
        [[("top", 0, share), (0, 0, more), (1, 0, quarter)]],
        top=(tops, tops_other),
        pairs=[([(lead, eighth, more)], [(lead_w, eighth, more)]), (rows_of(last_1), rows_of(last_w1))],
        keeps=True,
        part=(all_rows, 0, None),
    )
    return chunk(3, panel_3, last_2, last_w2, part=(all_rows, all_rows // quarter - 1, out))


def solution(mesh):
    return jax.shard_map(
        on_device,
        mesh=mesh,
        in_specs=(P(("tx", "ty"), None), P(), P(), P(), P()),
        out_specs=P(("tx", "ty"), None),
        check_vma=False,
    )
```

```python
import functools

import jax
import jax.numpy as jnp
from jax import lax
from jax.experimental import pallas as pl
from jax.experimental.pallas import tpu as pltpu
from jax.sharding import PartitionSpec as P

BLOCK = 128
LEVELS = 4
TILE = 2 * BLOCK
F32 = jnp.float32
BF16 = jnp.bfloat16


def stride_bit(axis, level):
    return lax.axis_size(axis).bit_length() - 2 - level // 2


def level_axis(level):
    return "tx" if level % 2 == 0 else "ty"


def trade(block, level):
    axis = level_axis(level)
    flip = 1 << stride_bit(axis, level)
    return lax.ppermute(block, axis, [(i, i ^ flip) for i in range(lax.axis_size(axis))])


def my_bit(level):
    axis = level_axis(level)
    place = lax.axis_index(axis).astype(jnp.int32)
    return jnp.bitwise_and(jnp.right_shift(place, stride_bit(axis, level)), 1)


def after(x, *others):
    return lax.optimization_barrier((x, *others))


def cut(pieces, start, rows):
    for ref, low, count in pieces:
        if start < count:
            assert start + rows <= count
            return ref, low + start
        start -= count
    raise ValueError


def segments(one, other):
    edges = {0}
    for pieces in (one, other):
        at = 0
        for _, _, count in pieces:
            at += count
            edges.add(at)
    edges = sorted(edges)
    return [(a, b - a) for a, b in zip(edges[:-1], edges[1:])]


def reorder_kernel(meta, inv, out, *, step):
    for level in range(LEVELS):
        shape = inv.shape[1:]
        row_id = lax.broadcasted_iota(jnp.int32, shape, 0)
        col_id = lax.broadcasted_iota(jnp.int32, shape, 1)
        source = jnp.bitwise_xor(col_id, meta[step * (level + 1) - 1])
        swap = jnp.where(row_id == source, 1.0, 0.0).astype(BF16)
        out[level] = jnp.dot(inv[level], swap, preferred_element_type=F32).astype(BF16)


def eliminate(meta, inv, panel, merged, top, pairs, outs, level, blocks):
    width = blocks * BLOCK
    base = level * meta.shape[0] // LEVELS

    def at(j):
        return pl.ds(pl.multiple_of(j * BLOCK, BLOCK), BLOCK)

    def read(pieces, start, rows, j):
        ref, low = cut(pieces, start, rows)
        return ref[pl.ds(low, rows), at(j)].astype(F32)

    def order(j):
        return meta[base + j]

    if top is not None:
        a, b = top
        half = sum(count for _, _, count in a)

        def merge_block(j, carry):
            other = order(j)
            keep_a = meta[base + blocks + j].astype(F32)
            keep_b = meta[base + 2 * blocks + j].astype(F32)
            for start, rows in segments(a, b):
                from_a = read(a, start, rows, j) + read(b, start, rows, other)
                from_b = read(b, start, rows, j) + read(a, start, rows, other)
                low, high = pl.ds(start, rows), pl.ds(half + start, rows)
                merged[low, at(j)] = from_a
                merged[high, at(j)] = from_b
                panel[low, at(j)] = (from_a * keep_a).astype(BF16)
                panel[high, at(j)] = (from_b * keep_b).astype(BF16)
            return carry

        lax.fori_loop(0, blocks, merge_block, 0, unroll=4)

    def columns(job, j):
        source, start, rows = job
        if source == "top":
            return merged[pl.ds(start, rows), at(j)]
        a, b = pairs[source]
        return read(a, start, rows, j) + read(b, start, rows, order(j))

    jobs = [job for _, dest in outs for job in dest]
    pivots = [meta[base + 3 * blocks + i] for i in range(inv.shape[1] // BLOCK)]
    coupling = jnp.concatenate(
        [jnp.concatenate([columns(job, p) for p in pivots], axis=1).astype(BF16) for job in jobs],
        axis=0,
    )
    weights = jnp.dot(coupling, inv[level], preferred_element_type=F32).astype(BF16)

    def finish_tile(t, carry):
        lanes = pl.ds(pl.multiple_of(t * TILE, TILE), TILE)
        update = jnp.dot(weights, panel[:, lanes], preferred_element_type=F32)
        done = 0
        for out, dest in outs:
            put = 0
            for job in dest:
                rows = job[2]
                for i in range(TILE // BLOCK):
                    j = (TILE // BLOCK) * t + i
                    part = update[done : done + rows, i * BLOCK : (i + 1) * BLOCK]
                    out[pl.ds(put, rows), at(j)] = (columns(job, j) - part).astype(BF16)
                put += rows
                done += rows
        return carry

    lax.fori_loop(0, width // TILE, finish_tile, 0, unroll=4)


def level_kernel(meta, *refs, level, blocks, n_in, top, pairs, outs, n_hidden):
    ins, rest = refs[:n_in], refs[n_in + n_hidden :]
    out_refs, rest = rest[: len(outs)], rest[len(outs) :]

    def stack(spec):
        return [(ins[i], low, count) for i, low, count in spec]

    panel, merged = rest if top is not None else (ins[1], None)
    eliminate(
        meta,
        ins[0],
        panel,
        merged,
        None if top is None else tuple(stack(s) for s in top),
        [tuple(stack(s) for s in pair) for pair in pairs],
        list(zip(out_refs, outs)),
        level,
        blocks,
    )


def two_level_kernel(meta, inv, *refs, blocks, counts, first_outs, second_outs):
    n = len(counts)
    ours, theirs, (near, near_x, out, panel, other_panel, merged, far, far_x) = (
        refs[:n],
        refs[n : 2 * n],
        refs[2 * n :],
    )
    stacks = tuple([(ref, 0, count) for ref, count in zip(group, counts)] for group in (ours, theirs))
    made = list(zip((far, far_x), first_outs))
    eliminate(meta, inv, other_panel, merged, stacks, [], made, 0, blocks)

    def whole(ref):
        return [(ref, 0, ref.shape[0])]

    pair = [(whole(near_x), whole(far_x))]
    eliminate(
        meta, inv, panel, merged, (whole(near), whole(far)), pair, [(out, second_outs)], 1, blocks
    )


def split_kernel(slab, *refs, starts):
    outs, sems = refs[:-1], refs[-1]
    copies = [
        pltpu.make_async_copy(slab.at[pl.ds(start, out.shape[0])], out, sems.at[i])
        for i, (start, out) in enumerate(zip(starts, outs))
    ]
    for copy in copies:
        copy.start()
    for copy in copies:
        copy.wait()


def split(slab, pieces):
    return pl.pallas_call(
        functools.partial(split_kernel, starts=[start for start, _ in pieces]),
        out_shape=[jax.ShapeDtypeStruct((rows, slab.shape[1]), BF16) for _, rows in pieces],
        in_specs=[pl.BlockSpec(memory_space=pltpu.HBM)],
        out_specs=[pl.BlockSpec(memory_space=pltpu.HBM)] * len(pieces),
        scratch_shapes=[pltpu.SemaphoreType.DMA((len(pieces),))],
        compiler_params=pltpu.CompilerParams(vmem_limit_bytes=60 * 2**20),
        cost_estimate=pl.CostEstimate(flops=0, bytes_accessed=0, transcendentals=0),
        name="split",
    )(slab)


def run_level(level, meta, held, outs, pairs=(), top=None, keeps=False, part=None, cost=0):
    arrays = list(held)

    def spec(stack):
        named = []
        for x, low, rows in stack:
            found = [i for i, seen in enumerate(arrays) if seen is x]
            if not found:
                arrays.append(x)
            named.append((found[0] if found else len(arrays) - 1, low, rows))
        return tuple(named)

    top_spec = None if top is None else (spec(top[0]), spec(top[1]))
    pair_specs = tuple((spec(a), spec(b)) for a, b in pairs)
    n_in = len(arrays)
    width = arrays[-1].shape[1]
    size = held[0].shape[1]
    counts = [sum(job[2] for job in dest) for dest in outs]
    shapes = [jax.ShapeDtypeStruct((rows, width), BF16) for rows in counts]
    whole = pl.BlockSpec(memory_space=pltpu.VMEM)
    in_specs = [pl.BlockSpec(memory_space=pltpu.SMEM)] + [whole] * n_in
    out_specs = [whole] * len(shapes)
    aliases = {}
    hidden = []
    if part is not None:
        all_rows, block, old = part
        shapes[0] = jax.ShapeDtypeStruct((all_rows, width), BF16)
        out_specs[0] = pl.BlockSpec((counts[0], width), lambda i: (block, 0))
        if old is not None:
            hidden = [old]
            in_specs.append(pl.BlockSpec(memory_space=pl.ANY))
            aliases = {1 + n_in: 0}
    scratch = []
    if top is not None:
        if keeps:
            shapes.append(jax.ShapeDtypeStruct((size, width), BF16))
            out_specs.append(whole)
        else:
            scratch.append(pltpu.VMEM((size, width), BF16))
        scratch.append(pltpu.VMEM((size, width), F32))
    kernel = functools.partial(
        level_kernel,
        level=level,
        blocks=width // BLOCK,
        n_in=n_in,
        top=top_spec,
        pairs=pair_specs,
        outs=tuple(tuple(dest) for dest in outs),
        n_hidden=len(hidden),
    )
    return pl.pallas_call(
        kernel,
        grid=(1,) if part is not None else (),
        out_shape=shapes,
        in_specs=in_specs,
        out_specs=out_specs,
        scratch_shapes=scratch,
        input_output_aliases=aliases,
        compiler_params=pltpu.CompilerParams(vmem_limit_bytes=30 * 2**20),
        cost_estimate=pl.CostEstimate(flops=cost, bytes_accessed=0, transcendentals=0),
        name=f"level{level}_rows{sum(counts)}",
    )(meta, *arrays, *hidden)


def run_two_levels(meta, inv, ours, theirs, near, near_x, first_outs, second_outs):
    width, size = near.shape[1], inv.shape[1]
    rows = sum(job[2] for job in second_outs)
    vmem = pl.BlockSpec(memory_space=pltpu.VMEM)
    kernel = functools.partial(
        two_level_kernel,
        blocks=width // BLOCK,
        counts=tuple(x.shape[0] for x in ours),
        first_outs=first_outs,
        second_outs=second_outs,
    )
    return pl.pallas_call(
        kernel,
        out_shape=[jax.ShapeDtypeStruct((n, width), BF16) for n in (rows, size)],
        in_specs=[pl.BlockSpec(memory_space=pltpu.SMEM)] + [vmem] * (3 + 2 * len(ours)),
        out_specs=[vmem, vmem],
        scratch_shapes=[
            pltpu.VMEM((size, width), BF16),
            pltpu.VMEM((size, width), F32),
            pltpu.VMEM(near.shape, BF16),
            pltpu.VMEM(near_x.shape, BF16),
        ],
        compiler_params=pltpu.CompilerParams(vmem_limit_bytes=30 * 2**20),
        cost_estimate=pl.CostEstimate(flops=0, bytes_accessed=0, transcendentals=0),
        name="level0_level1",
    )(meta, inv, *ours, *theirs, near, near_x)


def reorder(meta, pivot_inverse):
    step = meta.shape[0] // LEVELS
    return pl.pallas_call(
        functools.partial(reorder_kernel, step=step),
        out_shape=jax.ShapeDtypeStruct(pivot_inverse.shape, BF16),
        in_specs=[pl.BlockSpec(memory_space=pltpu.SMEM), pl.BlockSpec(memory_space=pltpu.VMEM)],
        out_specs=pl.BlockSpec(memory_space=pltpu.VMEM),
        compiler_params=pltpu.CompilerParams(vmem_limit_bytes=30 * 2**20),
        cost_estimate=pl.CostEstimate(flops=0, bytes_accessed=0, transcendentals=0),
        name="reorder",
    )(meta, pivot_inverse)


def make_meta(size, block_pattern, column_order, pivot_blocks):
    blocks = column_order.shape[1]
    rank = jnp.int32(0)
    meta = []
    for level in range(LEVELS):
        bit = my_bit(level)
        rank = rank + bit * (1 << level)
        shift = rank * (size >> (level + 1))
        meta += [
            column_order[level],
            jnp.where(bit == 0, block_pattern[level, 0], block_pattern[level, 1]),
            jnp.where(bit == 0, block_pattern[level, 1], block_pattern[level, 0]),
            pivot_blocks[level],
            jnp.zeros((blocks,), jnp.int32) + shift,
        ]
    return jnp.concatenate(meta)


def on_device(schur_slab, pivot_inverse, block_pattern, column_order, pivot_blocks):
    all_rows = schur_slab.shape[0]
    size = pivot_inverse.shape[1]
    half, quarter, eighth, share = size // 2, size // 4, size // 8, size // 16
    meta = make_meta(size, block_pattern, column_order, pivot_blocks)

    def rows_of(x):
        return [(x, 0, x.shape[0])]

    def chunk(level, panel, own, other, **more):
        (out,) = run_level(
            level, meta, (inv, panel), [[(0, 0, own.shape[0])]], pairs=[(rows_of(own), rows_of(other))], **more
        )
        return out

    cut_1 = quarter + share
    first_1, begin = split(schur_slab, [(0, cut_1), (0, half + quarter)])
    first_z1 = trade(first_1, 1)
    begin_y = trade(begin, 0)
    slab, begin = after(schur_slab, begin)
    first_2, rest_2 = slab[cut_1:half], slab[half + quarter :]
    inv = reorder(meta, pivot_inverse)

    first_yz1 = trade(first_z1, 0)
    first_2, first_z1 = after(first_2, first_z1)
    first_z2 = trade(first_2, 1)

    tops = [("top", 0, quarter), ("top", half, quarter)]
    near, near_x, after_1, panel_0 = run_level(
        0,
        meta,
        (inv,),
        [tops, [("top", quarter, quarter)], [(0, 0, quarter)]],
        top=([(begin, 0, half)], [(begin_y, 0, half)]),
        pairs=[([(begin, half, quarter)], [(begin_y, half, quarter)])],
        keeps=True,
    )
    first_z2, after_1, first_yz1 = after(first_z2, after_1, first_yz1)
    first_yz2 = trade(first_z2, 0)
    after_z1 = trade(after_1, 1)
    rest_2, first_yz2 = after(rest_2, first_yz2)
    rest_y2 = trade(rest_2, 0)

    head, panel_1 = run_two_levels(
        meta,
        inv,
        (first_z1, first_z2),
        (first_yz1, first_yz2),
        near,
        near_x,
        (tuple(tops), (("top", quarter, quarter),)),
        tuple([("top", low, eighth) for low in range(0, size, quarter)] + [("top", eighth, eighth), (0, 0, quarter)]),
    )
    head_c = trade(head, 2)
    rest_y2, after_z1 = after(rest_y2, after_z1)
    after_2 = chunk(0, panel_0, rest_2, rest_y2, cost=3 * 10**10)
    after_z2 = trade(after_2, 1)
    head_c, after_2 = after(head_c, after_2)

    more = head.shape[0] - half
    tops = [("top", low, share) for low in range(0, size, eighth)]
    lead, others, panel_2 = run_level(
        2,
        meta,
        (inv,),
        [
            [tops[0], tops[2], ("top", share, share), (0, 0, more)],
            [tops[i] for i in (1, 3, 4, 5, 6, 7)],
        ],
        top=([(head, 0, half)], [(head_c, 0, half)]),
        pairs=[([(head, half, more)], [(head_c, half, more)])],
        keeps=True,
    )
    lead_w = trade(lead, 3)
    after_z1, lead = after(after_z1, lead)
    next_1a, next_1b = run_level(
        1,
        meta,
        (inv, panel_1),
        [[(0, 0, eighth)], [(0, eighth, eighth)]],
        pairs=[(rows_of(after_1), rows_of(after_z1))],
    )
    (last_1,) = run_level(
        2,
        meta,
        (inv, panel_2),
        [[(0, 0, eighth), (1, 0, eighth)]],
        pairs=[(rows_of(x), rows_of(trade(x, 2))) for x in (next_1a, next_1b)],
    )
    last_w1 = trade(last_1, 3)
    after_z2, last_1 = after(after_z2, last_1)
    next_2 = chunk(1, panel_1, after_2, after_z2, cost=25 * 10**8)
    last_2 = chunk(2, panel_2, next_2, trade(next_2, 2))
    last_w2 = trade(last_2, 3)
    lead_w, last_2 = after(lead_w, last_2)
    tops_w = lead_w[:eighth]
    tops_wc = trade(tops_w, 2)
    tops_wy = trade(tops_w, 0)
    tops_wyc = trade(tops_wy, 2)

    more = lead.shape[0] - eighth
    tops = [(lead, 0, share), (others, 0, share), (lead, share, share)]
    tops += [(others, share * i, share) for i in range(1, 6)]
    tops_other = [(x, low, share) for low in (0, share) for x in (tops_w, tops_wy)]
    tops_other += [(x, low, share) for low in (0, share) for x in (tops_wc, tops_wyc)]
    out, panel_3 = run_level(
        3,
        meta,
        (inv,),
        [[("top", 0, share), (0, 0, more), (1, 0, quarter)]],
        top=(tops, tops_other),
        pairs=[([(lead, eighth, more)], [(lead_w, eighth, more)]), (rows_of(last_1), rows_of(last_w1))],
        keeps=True,
        part=(all_rows, 0, None),
    )
    return chunk(3, panel_3, last_2, last_w2, part=(all_rows, all_rows // quarter - 1, out))


def solution(mesh):
    return jax.shard_map(
        on_device,
        mesh=mesh,
        in_specs=(P(("tx", "ty"), None), P(), P(), P(), P()),
        out_specs=P(("tx", "ty"), None),
        check_vma=False,
    )
```

```python
import functools

import jax
import jax.numpy as jnp
from jax import lax
from jax.experimental import pallas as pl
from jax.experimental.pallas import tpu as pltpu
from jax.sharding import PartitionSpec as P

BLOCK = 128
LEVELS = 4
TILE = 2 * BLOCK
F32 = jnp.float32
BF16 = jnp.bfloat16


def stride_bit(axis, level):
    return lax.axis_size(axis).bit_length() - 2 - level // 2


def level_axis(level):
    return "tx" if level % 2 == 0 else "ty"


def trade(block, level):
    axis = level_axis(level)
    flip = 1 << stride_bit(axis, level)
    return lax.ppermute(block, axis, [(i, i ^ flip) for i in range(lax.axis_size(axis))])


def my_bit(level):
    axis = level_axis(level)
    place = lax.axis_index(axis).astype(jnp.int32)
    return jnp.bitwise_and(jnp.right_shift(place, stride_bit(axis, level)), 1)


def after(x, *others):
    return lax.optimization_barrier((x, *others))


def cut(pieces, start, rows):
    for ref, low, count in pieces:
        if start < count:
            assert start + rows <= count
            return ref, low + start
        start -= count
    raise ValueError


def segments(one, other):
    edges = {0}
    for pieces in (one, other):
        at = 0
        for _, _, count in pieces:
            at += count
            edges.add(at)
    edges = sorted(edges)
    return [(a, b - a) for a, b in zip(edges[:-1], edges[1:])]


def reorder_kernel(meta, inv, out, *, step):
    for level in range(LEVELS):
        shape = inv.shape[1:]
        row_id = lax.broadcasted_iota(jnp.int32, shape, 0)
        col_id = lax.broadcasted_iota(jnp.int32, shape, 1)
        source = jnp.bitwise_xor(col_id, meta[step * (level + 1) - 1])
        swap = jnp.where(row_id == source, 1.0, 0.0).astype(BF16)
        out[level] = jnp.dot(inv[level], swap, preferred_element_type=F32).astype(BF16)


def eliminate(meta, inv, panel, merged, top, pairs, outs, level, blocks):
    width = blocks * BLOCK
    base = level * meta.shape[0] // LEVELS

    def at(j):
        return pl.ds(pl.multiple_of(j * BLOCK, BLOCK), BLOCK)

    def read(pieces, start, rows, j):
        ref, low = cut(pieces, start, rows)
        return ref[pl.ds(low, rows), at(j)].astype(F32)

    def order(j):
        return meta[base + j]

    if top is not None:
        a, b = top
        half = sum(count for _, _, count in a)

        def merge_block(j, carry):
            other = order(j)
            keep_a = meta[base + blocks + j].astype(F32)
            keep_b = meta[base + 2 * blocks + j].astype(F32)
            for start, rows in segments(a, b):
                from_a = read(a, start, rows, j) + read(b, start, rows, other)
                from_b = read(b, start, rows, j) + read(a, start, rows, other)
                low, high = pl.ds(start, rows), pl.ds(half + start, rows)
                merged[low, at(j)] = from_a
                merged[high, at(j)] = from_b
                panel[low, at(j)] = (from_a * keep_a).astype(BF16)
                panel[high, at(j)] = (from_b * keep_b).astype(BF16)
            return carry

        lax.fori_loop(0, blocks, merge_block, 0, unroll=4)

    def columns(job, j):
        source, start, rows = job
        if source == "top":
            return merged[pl.ds(start, rows), at(j)]
        a, b = pairs[source]
        return read(a, start, rows, j) + read(b, start, rows, order(j))

    jobs = [job for _, dest in outs for job in dest]
    pivots = [meta[base + 3 * blocks + i] for i in range(inv.shape[1] // BLOCK)]
    coupling = jnp.concatenate(
        [jnp.concatenate([columns(job, p) for p in pivots], axis=1).astype(BF16) for job in jobs],
        axis=0,
    )
    weights = jnp.dot(coupling, inv[level], preferred_element_type=F32).astype(BF16)

    def finish_tile(t, carry):
        lanes = pl.ds(pl.multiple_of(t * TILE, TILE), TILE)
        update = jnp.dot(weights, panel[:, lanes], preferred_element_type=F32)
        done = 0
        for out, dest in outs:
            put = 0
            for job in dest:
                rows = job[2]
                for i in range(TILE // BLOCK):
                    j = (TILE // BLOCK) * t + i
                    part = update[done : done + rows, i * BLOCK : (i + 1) * BLOCK]
                    out[pl.ds(put, rows), at(j)] = (columns(job, j) - part).astype(BF16)
                put += rows
                done += rows
        return carry

    lax.fori_loop(0, width // TILE, finish_tile, 0, unroll=4)


def level_kernel(meta, *refs, level, blocks, n_in, top, pairs, outs, n_hidden):
    ins, rest = refs[:n_in], refs[n_in + n_hidden :]
    out_refs, rest = rest[: len(outs)], rest[len(outs) :]

    def stack(spec):
        return [(ins[i], low, count) for i, low, count in spec]

    panel, merged = rest if top is not None else (ins[1], None)
    eliminate(
        meta,
        ins[0],
        panel,
        merged,
        None if top is None else tuple(stack(s) for s in top),
        [tuple(stack(s) for s in pair) for pair in pairs],
        list(zip(out_refs, outs)),
        level,
        blocks,
    )


def two_level_kernel(meta, inv, *refs, blocks, counts, first_outs, second_outs):
    n = len(counts)
    ours, theirs, near, far, far_x = refs[:n], refs[n : 2 * n], *refs[2 * n : 2 * n + 3]
    outs, panel, other_panel, merged = refs[2 * n + 3 : -3], *refs[-3:]
    stacks = tuple([(ref, 0, count) for ref, count in zip(group, counts)] for group in (ours, theirs))
    made = list(zip((far, far_x), first_outs))
    eliminate(meta, inv, other_panel, merged, stacks, [], made, 0, blocks)
    top = tuple([(ref, 0, ref.shape[0])] for ref in (near, far))
    eliminate(meta, inv, panel, merged, top, [], list(zip(outs, second_outs)), 1, blocks)


def run_level(level, meta, held, outs, pairs=(), top=None, keeps=False, part=None, cost=0):
    arrays = list(held)

    def spec(stack):
        named = []
        for x, low, rows in stack:
            found = [i for i, seen in enumerate(arrays) if seen is x]
            if not found:
                arrays.append(x)
            named.append((found[0] if found else len(arrays) - 1, low, rows))
        return tuple(named)

    top_spec = None if top is None else (spec(top[0]), spec(top[1]))
    pair_specs = tuple((spec(a), spec(b)) for a, b in pairs)
    n_in = len(arrays)
    width = arrays[-1].shape[1]
    size = held[0].shape[1]
    counts = [sum(job[2] for job in dest) for dest in outs]
    shapes = [jax.ShapeDtypeStruct((rows, width), BF16) for rows in counts]
    whole = pl.BlockSpec(memory_space=pltpu.VMEM)
    in_specs = [pl.BlockSpec(memory_space=pltpu.SMEM)] + [whole] * n_in
    out_specs = [whole] * len(shapes)
    aliases = {}
    hidden = []
    if part is not None:
        all_rows, block, old = part
        shapes[0] = jax.ShapeDtypeStruct((all_rows, width), BF16)
        out_specs[0] = pl.BlockSpec((counts[0], width), lambda i: (block, 0))
        if old is not None:
            hidden = [old]
            in_specs.append(pl.BlockSpec(memory_space=pl.ANY))
            aliases = {1 + n_in: 0}
    scratch = []
    if top is not None:
        if keeps:
            shapes.append(jax.ShapeDtypeStruct((size, width), BF16))
            out_specs.append(whole)
        else:
            scratch.append(pltpu.VMEM((size, width), BF16))
        scratch.append(pltpu.VMEM((size, width), F32))
    kernel = functools.partial(
        level_kernel,
        level=level,
        blocks=width // BLOCK,
        n_in=n_in,
        top=top_spec,
        pairs=pair_specs,
        outs=tuple(tuple(dest) for dest in outs),
        n_hidden=len(hidden),
    )
    return pl.pallas_call(
        kernel,
        grid=(1,) if part is not None else (),
        out_shape=shapes,
        in_specs=in_specs,
        out_specs=out_specs,
        scratch_shapes=scratch,
        input_output_aliases=aliases,
        compiler_params=pltpu.CompilerParams(vmem_limit_bytes=30 * 2**20),
        cost_estimate=pl.CostEstimate(flops=cost, bytes_accessed=0, transcendentals=0),
        name=f"level{level}_rows{sum(counts)}",
    )(meta, *arrays, *hidden)


def run_two_levels(meta, inv, ours, theirs, near, first_outs, second_outs):
    width, size = near.shape[1], inv.shape[1]
    rows = [sum(job[2] for job in dest) for dest in (*first_outs, *second_outs)] + [size]
    vmem = pl.BlockSpec(memory_space=pltpu.VMEM)
    kernel = functools.partial(
        two_level_kernel,
        blocks=width // BLOCK,
        counts=tuple(x.shape[0] for x in ours),
        first_outs=first_outs,
        second_outs=second_outs,
    )
    return pl.pallas_call(
        kernel,
        out_shape=[jax.ShapeDtypeStruct((n, width), BF16) for n in rows],
        in_specs=[pl.BlockSpec(memory_space=pltpu.SMEM)] + [vmem] * (2 + 2 * len(ours)),
        out_specs=[vmem] * len(rows),
        scratch_shapes=[pltpu.VMEM((size, width), BF16), pltpu.VMEM((size, width), F32)],
        compiler_params=pltpu.CompilerParams(vmem_limit_bytes=30 * 2**20),
        cost_estimate=pl.CostEstimate(flops=0, bytes_accessed=0, transcendentals=0),
        name="level0_level1",
    )(meta, inv, *ours, *theirs, near)


def reorder(meta, pivot_inverse):
    step = meta.shape[0] // LEVELS
    return pl.pallas_call(
        functools.partial(reorder_kernel, step=step),
        out_shape=jax.ShapeDtypeStruct(pivot_inverse.shape, BF16),
        in_specs=[pl.BlockSpec(memory_space=pltpu.SMEM), pl.BlockSpec(memory_space=pltpu.VMEM)],
        out_specs=pl.BlockSpec(memory_space=pltpu.VMEM),
        compiler_params=pltpu.CompilerParams(vmem_limit_bytes=30 * 2**20),
        cost_estimate=pl.CostEstimate(flops=0, bytes_accessed=0, transcendentals=0),
        name="reorder",
    )(meta, pivot_inverse)


def make_meta(size, block_pattern, column_order, pivot_blocks):
    blocks = column_order.shape[1]
    rank = jnp.int32(0)
    meta = []
    for level in range(LEVELS):
        bit = my_bit(level)
        rank = rank + bit * (1 << level)
        shift = rank * (size >> (level + 1))
        meta += [
            column_order[level],
            jnp.where(bit == 0, block_pattern[level, 0], block_pattern[level, 1]),
            jnp.where(bit == 0, block_pattern[level, 1], block_pattern[level, 0]),
            pivot_blocks[level],
            jnp.zeros((blocks,), jnp.int32) + shift,
        ]
    return jnp.concatenate(meta)


def on_device(schur_slab, pivot_inverse, block_pattern, column_order, pivot_blocks):
    all_rows = schur_slab.shape[0]
    size = pivot_inverse.shape[1]
    half, quarter, eighth, share = size // 2, size // 4, size // 8, size // 16
    meta = make_meta(size, block_pattern, column_order, pivot_blocks)

    def rows_of(x):
        return [(x, 0, x.shape[0])]

    def chunk(level, panel, own, other, **more):
        (out,) = run_level(
            level, meta, (inv, panel), [[(0, 0, own.shape[0])]], pairs=[(rows_of(own), rows_of(other))], **more
        )
        return out

    three = half - eighth
    begin_1 = schur_slab[:three]
    first_z1 = trade(begin_1, 1)
    begin_y1 = trade(begin_1, 0)
    slab, begin_1 = after(schur_slab, begin_1)
    begin_2 = slab[three : 2 * three]
    begin_y2 = trade(begin_2, 0)
    slab, begin_2 = after(slab, begin_2)
    first_2, rest_2 = slab[three:half], slab[2 * three :]
    inv = reorder(meta, pivot_inverse)

    first_yz1 = trade(first_z1, 0)
    first_2, first_z1 = after(first_2, first_z1)
    first_z2 = trade(first_2, 1)

    tops = [("top", 0, quarter), ("top", half, quarter)]
    begun = ((begin_1, begin_2), (begin_y1, begin_y2))
    near, near_x, after_1, panel_0 = run_level(
        0,
        meta,
        (inv,),
        [tops, [("top", quarter, quarter)], [(0, 0, quarter)]],
        top=tuple([(x, 0, three), (y, 0, eighth)] for x, y in begun),
        pairs=[tuple([(y, eighth, quarter)] for _, y in begun)],
        keeps=True,
    )
    first_z2, after_1, first_yz1 = after(first_z2, after_1, first_yz1)
    first_yz2 = trade(first_z2, 0)
    after_z1 = trade(after_1, 1)
    rest_2, first_yz2 = after(rest_2, first_yz2)
    rest_y2 = trade(rest_2, 0)

    e, y, z, yz = (("top", low, eighth) for low in range(0, size, quarter))
    jobs = [[e, (*y[:2], share)], [("top", quarter + share, share), z], [yz]]
    far, far_x, *head, panel_1 = run_two_levels(
        meta,
        inv,
        (first_z1, first_z2),
        (first_yz1, first_yz2),
        near,
        (tuple(tops), (("top", quarter, quarter),)),
        jobs,
    )
    head_c = [trade(x, 2) for x in head]

    tops = [("top", low, share) for low in range(0, size, eighth)]
    lead, others, panel_2 = run_level(
        2,
        meta,
        (inv,),
        [[tops[0], tops[2], ("top", share, share)], [tops[i] for i in (1, 3, 4, 5, 6, 7)]],
        top=tuple(sum((rows_of(x) for x in group), []) for group in (head, head_c)),
        keeps=True,
    )
    rest_y2, after_z1, far_x, lead = after(rest_y2, after_z1, far_x, lead)
    after_2 = chunk(0, panel_0, rest_2, rest_y2, cost=0)
    after_z2 = trade(after_2, 1)
    (next_0,) = run_level(
        1,
        meta,
        (inv, panel_1),
        [[(0, 0, eighth), (1, 0, quarter)]],
        pairs=[
            ([(near, eighth, eighth)], [(far, eighth, eighth)]),
            (rows_of(near_x), rows_of(far_x)),
        ],
    )
    lead_w = trade(lead, 3)
    after_z1, after_2 = after(after_z1, after_2)
    next_1 = run_level(
        1,
        meta,
        (inv, panel_1),
        [[(0, 0, eighth)], [(0, eighth, eighth)]],
        pairs=[(rows_of(after_1), rows_of(after_z1))],
    )
    next_1 = [next_0, *next_1]
    (last_1,) = run_level(
        2,
        meta,
        (inv, panel_2),
        [[(i, 0, x.shape[0]) for i, x in enumerate(next_1)]],
        pairs=[(rows_of(x), rows_of(trade(x, 2))) for x in next_1],
    )
    last_w1 = trade(last_1, 3)
    after_z2, last_1, lead_w = after(after_z2, last_1, lead_w)
    next_2 = chunk(1, panel_1, after_2, after_z2, cost=15 * 10**8)
    last_2 = chunk(2, panel_2, next_2, trade(next_2, 2))
    last_w2 = trade(last_2, 3)
    lead_w, last_2 = after(lead_w, last_2)
    tops_w = lead_w[:eighth]
    tops_wc = trade(tops_w, 2)
    tops_wy = trade(tops_w, 0)
    tops_wyc = trade(tops_wy, 2)

    more = lead.shape[0] - eighth
    tops = [(lead, 0, share), (others, 0, share), (lead, share, share)]
    tops += [(others, share * i, share) for i in range(1, 6)]
    tops_other = [(x, low, share) for low in (0, share) for x in (tops_w, tops_wy)]
    tops_other += [(x, low, share) for low in (0, share) for x in (tops_wc, tops_wyc)]
    out, panel_3 = run_level(
        3,
        meta,
        (inv,),
        [[("top", 0, share), (0, 0, more), (1, 0, last_1.shape[0])]],
        top=(tops, tops_other),
        pairs=[([(lead, eighth, more)], [(lead_w, eighth, more)]), (rows_of(last_1), rows_of(last_w1))],
        keeps=True,
        part=(all_rows, 0, None),
    )
    return chunk(3, panel_3, last_2, last_w2, part=(all_rows, all_rows // quarter - 1, out))


def solution(mesh):
    return jax.shard_map(
        on_device,
        mesh=mesh,
        in_specs=(P(("tx", "ty"), None), P(), P(), P(), P()),
        out_specs=P(("tx", "ty"), None),
        check_vma=False,
    )
```

```python
import functools

import jax
import jax.numpy as jnp
from jax import lax
from jax.experimental import pallas as pl
from jax.experimental.pallas import tpu as pltpu
from jax.sharding import PartitionSpec as P

BLOCK = 128
LEVELS = 4
TILE = 2 * BLOCK
F32 = jnp.float32
BF16 = jnp.bfloat16


def stride_bit(axis, level):
    return lax.axis_size(axis).bit_length() - 2 - level // 2


def level_axis(level):
    return "tx" if level % 2 == 0 else "ty"


def trade(block, level):
    axis = level_axis(level)
    flip = 1 << stride_bit(axis, level)
    return lax.ppermute(block, axis, [(i, i ^ flip) for i in range(lax.axis_size(axis))])


def my_bit(level):
    axis = level_axis(level)
    place = lax.axis_index(axis).astype(jnp.int32)
    return jnp.bitwise_and(jnp.right_shift(place, stride_bit(axis, level)), 1)


def after(x, *others):
    return lax.optimization_barrier((x, *others))


def cut(pieces, start, rows):
    for ref, low, count in pieces:
        if start < count:
            assert start + rows <= count
            return ref, low + start
        start -= count
    raise ValueError


def segments(one, other):
    edges = {0}
    for pieces in (one, other):
        at = 0
        for _, _, count in pieces:
            at += count
            edges.add(at)
    edges = sorted(edges)
    return [(a, b - a) for a, b in zip(edges[:-1], edges[1:])]


def reorder_kernel(meta, inv, out, *, step):
    for level in range(LEVELS):
        shape = inv.shape[1:]
        row_id = lax.broadcasted_iota(jnp.int32, shape, 0)
        col_id = lax.broadcasted_iota(jnp.int32, shape, 1)
        source = jnp.bitwise_xor(col_id, meta[step * (level + 1) - 1])
        swap = jnp.where(row_id == source, 1.0, 0.0).astype(BF16)
        out[level] = jnp.dot(inv[level], swap, preferred_element_type=F32).astype(BF16)


def eliminate(meta, inv, panel, merged, top, pairs, outs, level, blocks):
    width = blocks * BLOCK
    base = level * meta.shape[0] // LEVELS

    def at(j):
        return pl.ds(pl.multiple_of(j * BLOCK, BLOCK), BLOCK)

    def read(pieces, start, rows, j):
        ref, low = cut(pieces, start, rows)
        return ref[pl.ds(low, rows), at(j)].astype(F32)

    def order(j):
        return meta[base + j]

    if top is not None:
        a, b = top
        half = sum(count for _, _, count in a)

        def merge_block(j, carry):
            other = order(j)
            keep_a = meta[base + blocks + j].astype(F32)
            keep_b = meta[base + 2 * blocks + j].astype(F32)
            for start, rows in segments(a, b):
                from_a = read(a, start, rows, j) + read(b, start, rows, other)
                from_b = read(b, start, rows, j) + read(a, start, rows, other)
                low, high = pl.ds(start, rows), pl.ds(half + start, rows)
                merged[low, at(j)] = from_a
                merged[high, at(j)] = from_b
                panel[low, at(j)] = (from_a * keep_a).astype(BF16)
                panel[high, at(j)] = (from_b * keep_b).astype(BF16)
            return carry

        lax.fori_loop(0, blocks, merge_block, 0, unroll=4)

    def columns(job, j):
        source, start, rows = job
        if source == "top":
            return merged[pl.ds(start, rows), at(j)]
        a, b = pairs[source]
        return read(a, start, rows, j) + read(b, start, rows, order(j))

    jobs = [job for _, dest in outs for job in dest]
    pivots = [meta[base + 3 * blocks + i] for i in range(inv.shape[1] // BLOCK)]
    coupling = jnp.concatenate(
        [jnp.concatenate([columns(job, p) for p in pivots], axis=1).astype(BF16) for job in jobs],
        axis=0,
    )
    weights = jnp.dot(coupling, inv[level], preferred_element_type=F32).astype(BF16)

    def finish_tile(t, carry):
        lanes = pl.ds(pl.multiple_of(t * TILE, TILE), TILE)
        update = jnp.dot(weights, panel[:, lanes], preferred_element_type=F32)
        done = 0
        for out, dest in outs:
            put = 0
            for job in dest:
                rows = job[2]
                for i in range(TILE // BLOCK):
                    j = (TILE // BLOCK) * t + i
                    part = update[done : done + rows, i * BLOCK : (i + 1) * BLOCK]
                    out[pl.ds(put, rows), at(j)] = (columns(job, j) - part).astype(BF16)
                put += rows
                done += rows
        return carry

    lax.fori_loop(0, width // TILE, finish_tile, 0, unroll=4)


def level_kernel(meta, *refs, level, blocks, n_in, top, pairs, outs, n_hidden):
    ins, rest = refs[:n_in], refs[n_in + n_hidden :]
    out_refs, rest = rest[: len(outs)], rest[len(outs) :]

    def stack(spec):
        return [(ins[i], low, count) for i, low, count in spec]

    panel, merged = rest if top is not None else (ins[1], None)
    eliminate(
        meta,
        ins[0],
        panel,
        merged,
        None if top is None else tuple(stack(s) for s in top),
        [tuple(stack(s) for s in pair) for pair in pairs],
        list(zip(out_refs, outs)),
        level,
        blocks,
    )


def two_level_kernel(meta, inv, *refs, blocks, counts, first_outs, second_outs):
    n = len(counts)
    ours, theirs, near, far, far_x = refs[:n], refs[n : 2 * n], *refs[2 * n : 2 * n + 3]
    outs, panel, other_panel, merged = refs[2 * n + 3 : -3], *refs[-3:]
    stacks = tuple([(ref, 0, count) for ref, count in zip(group, counts)] for group in (ours, theirs))
    made = list(zip((far, far_x), first_outs))
    eliminate(meta, inv, other_panel, merged, stacks, [], made, 0, blocks)
    top = tuple([(ref, 0, ref.shape[0])] for ref in (near, far))
    eliminate(meta, inv, panel, merged, top, [], list(zip(outs, second_outs)), 1, blocks)


def run_level(level, meta, held, outs, pairs=(), top=None, keeps=False, part=None, cost=0):
    arrays = list(held)

    def spec(stack):
        named = []
        for x, low, rows in stack:
            found = [i for i, seen in enumerate(arrays) if seen is x]
            if not found:
                arrays.append(x)
            named.append((found[0] if found else len(arrays) - 1, low, rows))
        return tuple(named)

    top_spec = None if top is None else (spec(top[0]), spec(top[1]))
    pair_specs = tuple((spec(a), spec(b)) for a, b in pairs)
    n_in = len(arrays)
    width = arrays[-1].shape[1]
    size = held[0].shape[1]
    counts = [sum(job[2] for job in dest) for dest in outs]
    shapes = [jax.ShapeDtypeStruct((rows, width), BF16) for rows in counts]
    whole = pl.BlockSpec(memory_space=pltpu.VMEM)
    in_specs = [pl.BlockSpec(memory_space=pltpu.SMEM)] + [whole] * n_in
    out_specs = [whole] * len(shapes)
    aliases = {}
    hidden = []
    if part is not None:
        all_rows, block, old = part
        shapes[0] = jax.ShapeDtypeStruct((all_rows, width), BF16)
        out_specs[0] = pl.BlockSpec((counts[0], width), lambda i: (block, 0))
        if old is not None:
            hidden = [old]
            in_specs.append(pl.BlockSpec(memory_space=pl.ANY))
            aliases = {1 + n_in: 0}
    scratch = []
    if top is not None:
        if keeps:
            shapes.append(jax.ShapeDtypeStruct((size, width), BF16))
            out_specs.append(whole)
        else:
            scratch.append(pltpu.VMEM((size, width), BF16))
        scratch.append(pltpu.VMEM((size, width), F32))
    kernel = functools.partial(
        level_kernel,
        level=level,
        blocks=width // BLOCK,
        n_in=n_in,
        top=top_spec,
        pairs=pair_specs,
        outs=tuple(tuple(dest) for dest in outs),
        n_hidden=len(hidden),
    )
    return pl.pallas_call(
        kernel,
        grid=(1,) if part is not None else (),
        out_shape=shapes,
        in_specs=in_specs,
        out_specs=out_specs,
        scratch_shapes=scratch,
        input_output_aliases=aliases,
        compiler_params=pltpu.CompilerParams(vmem_limit_bytes=30 * 2**20),
        cost_estimate=pl.CostEstimate(flops=cost, bytes_accessed=0, transcendentals=0),
        name=f"level{level}_rows{sum(counts)}",
    )(meta, *arrays, *hidden)


def run_two_levels(meta, inv, ours, theirs, near, first_outs, second_outs):
    width, size = near.shape[1], inv.shape[1]
    rows = [sum(job[2] for job in dest) for dest in (*first_outs, *second_outs)] + [size]
    vmem = pl.BlockSpec(memory_space=pltpu.VMEM)
    kernel = functools.partial(
        two_level_kernel,
        blocks=width // BLOCK,
        counts=tuple(x.shape[0] for x in ours),
        first_outs=first_outs,
        second_outs=second_outs,
    )
    return pl.pallas_call(
        kernel,
        out_shape=[jax.ShapeDtypeStruct((n, width), BF16) for n in rows],
        in_specs=[pl.BlockSpec(memory_space=pltpu.SMEM)] + [vmem] * (2 + 2 * len(ours)),
        out_specs=[vmem] * len(rows),
        scratch_shapes=[pltpu.VMEM((size, width), BF16), pltpu.VMEM((size, width), F32)],
        compiler_params=pltpu.CompilerParams(vmem_limit_bytes=30 * 2**20),
        cost_estimate=pl.CostEstimate(flops=0, bytes_accessed=0, transcendentals=0),
        name="level0_level1",
    )(meta, inv, *ours, *theirs, near)


def reorder(meta, pivot_inverse):
    step = meta.shape[0] // LEVELS
    return pl.pallas_call(
        functools.partial(reorder_kernel, step=step),
        out_shape=jax.ShapeDtypeStruct(pivot_inverse.shape, BF16),
        in_specs=[pl.BlockSpec(memory_space=pltpu.SMEM), pl.BlockSpec(memory_space=pltpu.VMEM)],
        out_specs=pl.BlockSpec(memory_space=pltpu.VMEM),
        compiler_params=pltpu.CompilerParams(vmem_limit_bytes=30 * 2**20),
        cost_estimate=pl.CostEstimate(flops=0, bytes_accessed=0, transcendentals=0),
        name="reorder",
    )(meta, pivot_inverse)


def make_meta(size, block_pattern, column_order, pivot_blocks):
    blocks = column_order.shape[1]
    rank = jnp.int32(0)
    meta = []
    for level in range(LEVELS):
        bit = my_bit(level)
        rank = rank + bit * (1 << level)
        shift = rank * (size >> (level + 1))
        meta += [
            column_order[level],
            jnp.where(bit == 0, block_pattern[level, 0], block_pattern[level, 1]),
            jnp.where(bit == 0, block_pattern[level, 1], block_pattern[level, 0]),
            pivot_blocks[level],
            jnp.zeros((blocks,), jnp.int32) + shift,
        ]
    return jnp.concatenate(meta)


def on_device(schur_slab, pivot_inverse, block_pattern, column_order, pivot_blocks):
    all_rows = schur_slab.shape[0]
    size = pivot_inverse.shape[1]
    half, quarter, eighth, share = size // 2, size // 4, size // 8, size // 16
    meta = make_meta(size, block_pattern, column_order, pivot_blocks)

    def rows_of(x):
        return [(x, 0, x.shape[0])]

    def chunk(level, panel, own, other, **more):
        (out,) = run_level(
            level, meta, (inv, panel), [[(0, 0, own.shape[0])]], pairs=[(rows_of(own), rows_of(other))], **more
        )
        return out

    cut_1 = quarter + share
    cut_2 = half + quarter
    begin_1 = schur_slab[:cut_1]
    first_z1 = trade(begin_1, 1)
    begin_y1 = trade(begin_1, 0)
    slab, begin_1 = after(schur_slab, begin_1)
    begin_2, begin_3, rest_2 = slab[cut_1:half], slab[half:cut_2], slab[cut_2:]
    begin_y2, begin_y3 = trade(begin_2, 0), trade(begin_3, 0)
    inv = reorder(meta, pivot_inverse)

    first_yz1 = trade(first_z1, 0)
    first_2, first_z1 = after(begin_2, first_z1)
    first_z2 = trade(first_2, 1)
    rest_2, begin_y3 = after(rest_2, begin_y3)

    tops = [("top", 0, quarter), ("top", half, quarter)]
    begun = ((begin_1, begin_2, begin_3), (begin_y1, begin_y2, begin_y3))
    near, near_x, after_1, panel_0 = run_level(
        0,
        meta,
        (inv,),
        [tops, [("top", quarter, quarter)], [(0, 0, quarter)]],
        top=tuple(rows_of(x) + rows_of(y) for x, y, _ in begun),
        pairs=[tuple(rows_of(x) for *_, x in begun)],
        keeps=True,
    )
    first_z2, after_1 = after(first_z2, after_1)
    after_z1 = trade(after_1, 1)
    first_z2, first_yz1 = after(first_z2, first_yz1)
    first_yz2 = trade(first_z2, 0)
    rest_2, first_yz2 = after(rest_2, first_yz2)
    rest_y2 = trade(rest_2, 0)

    e, y, z, yz = (("top", low, eighth) for low in range(0, size, quarter))
    jobs = [[e, (*y[:2], share)], [("top", quarter + share, share), z], [yz]]
    far, far_x, *head, panel_1 = run_two_levels(
        meta,
        inv,
        (first_z1, first_z2),
        (first_yz1, first_yz2),
        near,
        (tuple(tops), (("top", quarter, quarter),)),
        jobs,
    )
    head_c = [trade(x, 2) for x in head]

    tops = [("top", low, share) for low in range(0, size, eighth)]
    lead, others, panel_2 = run_level(
        2,
        meta,
        (inv,),
        [[tops[0], tops[2], ("top", share, share)], [tops[i] for i in (1, 3, 4, 5, 6, 7)]],
        top=tuple(sum((rows_of(x) for x in group), []) for group in (head, head_c)),
        keeps=True,
    )
    rest_y2, after_z1, far_x, lead = after(rest_y2, after_z1, far_x, lead)
    after_2 = chunk(0, panel_0, rest_2, rest_y2, cost=0)
    after_z2 = trade(after_2, 1)
    (next_0,) = run_level(
        1,
        meta,
        (inv, panel_1),
        [[(0, 0, eighth), (1, 0, quarter)]],
        pairs=[
            ([(near, eighth, eighth)], [(far, eighth, eighth)]),
            (rows_of(near_x), rows_of(far_x)),
        ],
    )
    lead_w = trade(lead, 3)
    after_z1, after_2 = after(after_z1, after_2)
    next_1 = run_level(
        1,
        meta,
        (inv, panel_1),
        [[(0, 0, eighth)], [(0, eighth, eighth)]],
        pairs=[(rows_of(after_1), rows_of(after_z1))],
    )
    next_1 = [next_0, *next_1]
    (last_1,) = run_level(
        2,
        meta,
        (inv, panel_2),
        [[(i, 0, x.shape[0]) for i, x in enumerate(next_1)]],
        pairs=[(rows_of(x), rows_of(trade(x, 2))) for x in next_1],
    )
    last_w1 = trade(last_1, 3)
    after_z2, last_1, lead_w = after(after_z2, last_1, lead_w)
    next_2 = chunk(1, panel_1, after_2, after_z2, cost=15 * 10**8)
    last_2 = chunk(2, panel_2, next_2, trade(next_2, 2))
    last_w2 = trade(last_2, 3)
    lead_w, last_2 = after(lead_w, last_2)
    tops_w = lead_w[:eighth]
    tops_wc = trade(tops_w, 2)
    tops_wy = trade(tops_w, 0)
    tops_wyc = trade(tops_wy, 2)

    more = lead.shape[0] - eighth
    tops = [(lead, 0, share), (others, 0, share), (lead, share, share)]
    tops += [(others, share * i, share) for i in range(1, 6)]
    tops_other = [(x, low, share) for low in (0, share) for x in (tops_w, tops_wy)]
    tops_other += [(x, low, share) for low in (0, share) for x in (tops_wc, tops_wyc)]
    out, panel_3 = run_level(
        3,
        meta,
        (inv,),
        [[("top", 0, share), (0, 0, more), (1, 0, last_1.shape[0])]],
        top=(tops, tops_other),
        pairs=[([(lead, eighth, more)], [(lead_w, eighth, more)]), (rows_of(last_1), rows_of(last_w1))],
        keeps=True,
        part=(all_rows, 0, None),
    )
    return chunk(3, panel_3, last_2, last_w2, part=(all_rows, all_rows // quarter - 1, out))


def solution(mesh):
    return jax.shard_map(
        on_device,
        mesh=mesh,
        in_specs=(P(("tx", "ty"), None), P(), P(), P(), P()),
        out_specs=P(("tx", "ty"), None),
        check_vma=False,
    )
```

```python
import functools

import jax
import jax.numpy as jnp
from jax import lax
from jax.experimental import pallas as pl
from jax.experimental.pallas import tpu as pltpu
from jax.sharding import PartitionSpec as P

BLOCK = 128
LEVELS = 4
TILE = 2 * BLOCK
F32 = jnp.float32
BF16 = jnp.bfloat16


def stride_bit(axis, level):
    return lax.axis_size(axis).bit_length() - 2 - level // 2


def level_axis(level):
    return "tx" if level % 2 == 0 else "ty"


def trade(block, level):
    axis = level_axis(level)
    flip = 1 << stride_bit(axis, level)
    return lax.ppermute(block, axis, [(i, i ^ flip) for i in range(lax.axis_size(axis))])


def my_bit(level):
    axis = level_axis(level)
    place = lax.axis_index(axis).astype(jnp.int32)
    return jnp.bitwise_and(jnp.right_shift(place, stride_bit(axis, level)), 1)


def after(x, *others):
    return lax.optimization_barrier((x, *others))


def cut(pieces, start, rows):
    for ref, low, count in pieces:
        if start < count:
            assert start + rows <= count
            return ref, low + start
        start -= count
    raise ValueError


def segments(one, other):
    edges = {0}
    for pieces in (one, other):
        at = 0
        for _, _, count in pieces:
            at += count
            edges.add(at)
    edges = sorted(edges)
    return [(a, b - a) for a, b in zip(edges[:-1], edges[1:])]


def reorder_kernel(meta, inv, out, *, step):
    for level in range(LEVELS):
        shape = inv.shape[1:]
        row_id = lax.broadcasted_iota(jnp.int32, shape, 0)
        col_id = lax.broadcasted_iota(jnp.int32, shape, 1)
        source = jnp.bitwise_xor(col_id, meta[step * (level + 1) - 1])
        swap = jnp.where(row_id == source, 1.0, 0.0).astype(BF16)
        out[level] = jnp.dot(inv[level], swap, preferred_element_type=F32).astype(BF16)


def eliminate(meta, inv, panel, merged, top, pairs, outs, level, blocks):
    width = blocks * BLOCK
    base = level * meta.shape[0] // LEVELS

    def at(j):
        return pl.ds(pl.multiple_of(j * BLOCK, BLOCK), BLOCK)

    def read(pieces, start, rows, j):
        ref, low = cut(pieces, start, rows)
        return ref[pl.ds(low, rows), at(j)].astype(F32)

    def order(j):
        return meta[base + j]

    if top is not None:
        a, b = top
        half = sum(count for _, _, count in a)

        def merge_block(j, carry):
            other = order(j)
            keep_a = meta[base + blocks + j].astype(F32)
            keep_b = meta[base + 2 * blocks + j].astype(F32)
            for start, rows in segments(a, b):
                from_a = read(a, start, rows, j) + read(b, start, rows, other)
                from_b = read(b, start, rows, j) + read(a, start, rows, other)
                low, high = pl.ds(start, rows), pl.ds(half + start, rows)
                merged[low, at(j)] = from_a
                merged[high, at(j)] = from_b
                panel[low, at(j)] = (from_a * keep_a).astype(BF16)
                panel[high, at(j)] = (from_b * keep_b).astype(BF16)
            return carry

        lax.fori_loop(0, blocks, merge_block, 0, unroll=4)

    def columns(job, j):
        source, start, rows = job
        if source == "top":
            return merged[pl.ds(start, rows), at(j)]
        a, b = pairs[source]
        return read(a, start, rows, j) + read(b, start, rows, order(j))

    jobs = [job for _, dest in outs for job in dest]
    pivots = [meta[base + 3 * blocks + i] for i in range(inv.shape[1] // BLOCK)]
    coupling = jnp.concatenate(
        [jnp.concatenate([columns(job, p) for p in pivots], axis=1).astype(BF16) for job in jobs],
        axis=0,
    )
    weights = jnp.dot(coupling, inv[level], preferred_element_type=F32).astype(BF16)

    def finish_tile(t, carry):
        lanes = pl.ds(pl.multiple_of(t * TILE, TILE), TILE)
        update = jnp.dot(weights, panel[:, lanes], preferred_element_type=F32)
        done = 0
        for out, dest in outs:
            put = 0
            for job in dest:
                rows = job[2]
                for i in range(TILE // BLOCK):
                    j = (TILE // BLOCK) * t + i
                    part = update[done : done + rows, i * BLOCK : (i + 1) * BLOCK]
                    out[pl.ds(put, rows), at(j)] = (columns(job, j) - part).astype(BF16)
                put += rows
                done += rows
        return carry

    lax.fori_loop(0, width // TILE, finish_tile, 0, unroll=4)


def level_kernel(meta, *refs, level, blocks, n_in, top, pairs, outs, n_hidden):
    ins, rest = refs[:n_in], refs[n_in + n_hidden :]
    out_refs, rest = rest[: len(outs)], rest[len(outs) :]

    def stack(spec):
        return [(ins[i], low, count) for i, low, count in spec]

    panel, merged = rest if top is not None else (ins[1], None)
    eliminate(
        meta,
        ins[0],
        panel,
        merged,
        None if top is None else tuple(stack(s) for s in top),
        [tuple(stack(s) for s in pair) for pair in pairs],
        list(zip(out_refs, outs)),
        level,
        blocks,
    )


def two_level_kernel(meta, inv, *refs, blocks, counts, first_outs, second_outs, pairs):
    n = len(counts)
    ours, theirs, near, near_x = refs[:n], refs[n : 2 * n], *refs[2 * n : 2 * n + 2]
    outs, panel, other_panel, merged, far, far_x = refs[2 * n + 2 : -5], *refs[-5:]
    stacks = tuple([(ref, 0, count) for ref, count in zip(group, counts)] for group in (ours, theirs))
    eliminate(meta, inv, other_panel, merged, stacks, [], list(zip((far, far_x), first_outs)), 0, blocks)
    held = ((near, far), (near_x, far_x))
    top = tuple([(ref, 0, ref.shape[0])] for ref in (near, far))
    stacked = [tuple([(ref, low, rows)] for ref in held[i]) for i, low, rows in pairs]
    eliminate(meta, inv, panel, merged, top, stacked, list(zip(outs, second_outs)), 1, blocks)


def run_level(level, meta, held, outs, pairs=(), top=None, keeps=False, part=None, cost=0):
    arrays = list(held)

    def spec(stack):
        named = []
        for x, low, rows in stack:
            found = [i for i, seen in enumerate(arrays) if seen is x]
            if not found:
                arrays.append(x)
            named.append((found[0] if found else len(arrays) - 1, low, rows))
        return tuple(named)

    top_spec = None if top is None else (spec(top[0]), spec(top[1]))
    pair_specs = tuple((spec(a), spec(b)) for a, b in pairs)
    n_in = len(arrays)
    width = arrays[-1].shape[1]
    size = held[0].shape[1]
    counts = [sum(job[2] for job in dest) for dest in outs]
    shapes = [jax.ShapeDtypeStruct((rows, width), BF16) for rows in counts]
    whole = pl.BlockSpec(memory_space=pltpu.VMEM)
    in_specs = [pl.BlockSpec(memory_space=pltpu.SMEM)] + [whole] * n_in
    out_specs = [whole] * len(shapes)
    aliases = {}
    hidden = []
    if part is not None:
        all_rows, block, old = part
        shapes[0] = jax.ShapeDtypeStruct((all_rows, width), BF16)
        out_specs[0] = pl.BlockSpec((counts[0], width), lambda i: (block, 0))
        if old is not None:
            hidden = [old]
            in_specs.append(pl.BlockSpec(memory_space=pl.ANY))
            aliases = {1 + n_in: 0}
    scratch = []
    if top is not None:
        if keeps:
            shapes.append(jax.ShapeDtypeStruct((size, width), BF16))
            out_specs.append(whole)
        else:
            scratch.append(pltpu.VMEM((size, width), BF16))
        scratch.append(pltpu.VMEM((size, width), F32))
    kernel = functools.partial(
        level_kernel,
        level=level,
        blocks=width // BLOCK,
        n_in=n_in,
        top=top_spec,
        pairs=pair_specs,
        outs=tuple(tuple(dest) for dest in outs),
        n_hidden=len(hidden),
    )
    return pl.pallas_call(
        kernel,
        grid=(1,) if part is not None else (),
        out_shape=shapes,
        in_specs=in_specs,
        out_specs=out_specs,
        scratch_shapes=scratch,
        input_output_aliases=aliases,
        compiler_params=pltpu.CompilerParams(vmem_limit_bytes=30 * 2**20),
        cost_estimate=pl.CostEstimate(flops=cost, bytes_accessed=0, transcendentals=0),
        name=f"level{level}_rows{sum(counts)}",
    )(meta, *arrays, *hidden)


def run_two_levels(meta, inv, ours, theirs, near, near_x, first_outs, second_outs, pairs):
    width, size = near.shape[1], inv.shape[1]
    rows = [sum(job[2] for job in dest) for dest in second_outs] + [size]
    vmem = pl.BlockSpec(memory_space=pltpu.VMEM)
    kernel = functools.partial(
        two_level_kernel,
        blocks=width // BLOCK,
        counts=tuple(x.shape[0] for x in ours),
        first_outs=first_outs,
        second_outs=second_outs,
        pairs=pairs,
    )
    return pl.pallas_call(
        kernel,
        out_shape=[jax.ShapeDtypeStruct((n, width), BF16) for n in rows],
        in_specs=[pl.BlockSpec(memory_space=pltpu.SMEM)] + [vmem] * (3 + 2 * len(ours)),
        out_specs=[vmem] * len(rows),
        scratch_shapes=[
            pltpu.VMEM((size, width), BF16),
            pltpu.VMEM((size, width), F32),
            pltpu.VMEM(near.shape, BF16),
            pltpu.VMEM(near_x.shape, BF16),
        ],
        compiler_params=pltpu.CompilerParams(vmem_limit_bytes=30 * 2**20),
        cost_estimate=pl.CostEstimate(flops=0, bytes_accessed=0, transcendentals=0),
        name="level0_level1",
    )(meta, inv, *ours, *theirs, near, near_x)


def reorder(meta, pivot_inverse):
    step = meta.shape[0] // LEVELS
    return pl.pallas_call(
        functools.partial(reorder_kernel, step=step),
        out_shape=jax.ShapeDtypeStruct(pivot_inverse.shape, BF16),
        in_specs=[pl.BlockSpec(memory_space=pltpu.SMEM), pl.BlockSpec(memory_space=pltpu.VMEM)],
        out_specs=pl.BlockSpec(memory_space=pltpu.VMEM),
        compiler_params=pltpu.CompilerParams(vmem_limit_bytes=30 * 2**20),
        cost_estimate=pl.CostEstimate(flops=0, bytes_accessed=0, transcendentals=0),
        name="reorder",
    )(meta, pivot_inverse)


def make_meta(size, block_pattern, column_order, pivot_blocks):
    blocks = column_order.shape[1]
    rank = jnp.int32(0)
    meta = []
    for level in range(LEVELS):
        bit = my_bit(level)
        rank = rank + bit * (1 << level)
        shift = rank * (size >> (level + 1))
        meta += [
            column_order[level],
            jnp.where(bit == 0, block_pattern[level, 0], block_pattern[level, 1]),
            jnp.where(bit == 0, block_pattern[level, 1], block_pattern[level, 0]),
            pivot_blocks[level],
            jnp.zeros((blocks,), jnp.int32) + shift,
        ]
    return jnp.concatenate(meta)


def on_device(schur_slab, pivot_inverse, block_pattern, column_order, pivot_blocks):
    all_rows = schur_slab.shape[0]
    size = pivot_inverse.shape[1]
    half, quarter, eighth, share = size // 2, size // 4, size // 8, size // 16
    meta = make_meta(size, block_pattern, column_order, pivot_blocks)

    def rows_of(x):
        return [(x, 0, x.shape[0])]

    def chunk(level, panel, own, other, **more):
        (out,) = run_level(
            level, meta, (inv, panel), [[(0, 0, own.shape[0])]], pairs=[(rows_of(own), rows_of(other))], **more
        )
        return out

    cut_1 = quarter + share
    cut_2 = half + quarter
    begin_1 = schur_slab[:cut_1]
    first_z1 = trade(begin_1, 1)
    begin_y1 = trade(begin_1, 0)
    slab, begin_1 = after(schur_slab, begin_1)
    begin_2, begin_3, rest_2 = slab[cut_1:half], slab[half:cut_2], slab[cut_2:]
    begin_y2, begin_y3 = trade(begin_2, 0), trade(begin_3, 0)
    inv = reorder(meta, pivot_inverse)

    first_yz1 = trade(first_z1, 0)
    first_2, first_z1 = after(begin_2, first_z1)
    first_z2 = trade(first_2, 1)
    rest_2, begin_y3 = after(rest_2, begin_y3)

    tops = [("top", 0, quarter), ("top", half, quarter)]
    begun = ((begin_1, begin_2, begin_3), (begin_y1, begin_y2, begin_y3))
    near, near_x, after_1, panel_0 = run_level(
        0,
        meta,
        (inv,),
        [tops, [("top", quarter, quarter)], [(0, 0, quarter)]],
        top=tuple(rows_of(x) + rows_of(y) for x, y, _ in begun),
        pairs=[tuple(rows_of(x) for *_, x in begun)],
        keeps=True,
    )
    first_z2, after_1 = after(first_z2, after_1)
    after_z1 = trade(after_1, 1)
    first_z2, first_yz1 = after(first_z2, first_yz1)
    first_yz2 = trade(first_z2, 0)
    e, y, z, yz = (("top", low, eighth) for low in range(0, size, quarter))
    jobs = [[e, (*y[:2], share)], [("top", quarter + share, share), z], [yz]]
    jobs.append([(0, 0, eighth), (1, 0, quarter)])
    *head, next_0, panel_1 = run_two_levels(
        meta,
        inv,
        (first_z1, first_z2),
        (first_yz1, first_yz2),
        near,
        near_x,
        (tuple(tops), (("top", quarter, quarter),)),
        jobs,
        ((0, eighth, eighth), (1, 0, quarter)),
    )
    head_c = [trade(x, 2) for x in head]

    tops = [("top", low, share) for low in range(0, size, eighth)]
    lead, others, panel_2 = run_level(
        2,
        meta,
        (inv,),
        [[tops[0], tops[2], ("top", share, share)], [tops[i] for i in (1, 3, 4, 5, 6, 7)]],
        top=tuple(sum((rows_of(x) for x in group), []) for group in (head, head_c)),
        keeps=True,
    )
    lead_w = trade(lead, 3)
    after_z1, rest_2, lead = after(after_z1, rest_2, lead)
    rest_y2 = trade(rest_2, 0)
    next_1 = run_level(
        1,
        meta,
        (inv, panel_1),
        [[(0, 0, eighth)], [(0, eighth, eighth)]],
        pairs=[(rows_of(after_1), rows_of(after_z1))],
        cost=10**9,
    )
    next_1 = [next_0, *next_1]
    (last_1,) = run_level(
        2,
        meta,
        (inv, panel_2),
        [[(i, 0, x.shape[0]) for i, x in enumerate(next_1)]],
        pairs=[(rows_of(x), rows_of(trade(x, 2))) for x in next_1],
    )
    rest_y2, lead_w, last_1 = after(rest_y2, lead_w, last_1)
    after_2 = chunk(0, panel_0, rest_2, rest_y2, cost=3 * 10**9)
    after_z2 = trade(after_2, 1)
    last_w1 = trade(last_1, 3)
    tops_w = lead_w[:eighth]
    tops_wc = trade(tops_w, 2)
    tops_wy = trade(tops_w, 0)
    after_z2, tops_wy = after(after_z2, tops_wy)
    tops_wyc = trade(tops_wy, 2)
    next_2 = chunk(1, panel_1, after_2, after_z2, cost=0)
    last_2 = chunk(2, panel_2, next_2, trade(next_2, 2))
    last_w2 = trade(last_2, 3)
    more = lead.shape[0] - eighth
    tops = [(lead, 0, share), (others, 0, share), (lead, share, share)]
    tops += [(others, share * i, share) for i in range(1, 6)]
    tops_other = [(x, low, share) for low in (0, share) for x in (tops_w, tops_wy)]
    tops_other += [(x, low, share) for low in (0, share) for x in (tops_wc, tops_wyc)]
    out, panel_3 = run_level(
        3,
        meta,
        (inv,),
        [[("top", 0, share), (0, 0, more), (1, 0, last_1.shape[0])]],
        top=(tops, tops_other),
        pairs=[([(lead, eighth, more)], [(lead_w, eighth, more)]), (rows_of(last_1), rows_of(last_w1))],
        keeps=True,
        part=(all_rows, 0, None),
        cost=5 * 10**9,
    )
    return chunk(3, panel_3, last_2, last_w2, part=(all_rows, all_rows // quarter - 1, out))


def solution(mesh):
    return jax.shard_map(
        on_device,
        mesh=mesh,
        in_specs=(P(("tx", "ty"), None), P(), P(), P(), P()),
        out_specs=P(("tx", "ty"), None),
        check_vma=False,
    )
```

```python
import functools

import jax
import jax.numpy as jnp
from jax import lax
from jax.experimental import pallas as pl
from jax.experimental.pallas import tpu as pltpu
from jax.sharding import PartitionSpec as P

BLOCK = 128
LEVELS = 4
TILE = 2 * BLOCK
F32 = jnp.float32
BF16 = jnp.bfloat16


def stride_bit(axis, level):
    return lax.axis_size(axis).bit_length() - 2 - level // 2


def level_axis(level):
    return "tx" if level % 2 == 0 else "ty"


def trade(block, level):
    axis = level_axis(level)
    flip = 1 << stride_bit(axis, level)
    return lax.ppermute(block, axis, [(i, i ^ flip) for i in range(lax.axis_size(axis))])


def my_bit(level):
    axis = level_axis(level)
    place = lax.axis_index(axis).astype(jnp.int32)
    return jnp.bitwise_and(jnp.right_shift(place, stride_bit(axis, level)), 1)


def after(x, *others):
    return lax.optimization_barrier((x, *others))


def cut(pieces, start, rows):
    for ref, low, count in pieces:
        if start < count:
            assert start + rows <= count
            return ref, low + start
        start -= count
    raise ValueError


def segments(one, other):
    edges = {0}
    for pieces in (one, other):
        at = 0
        for _, _, count in pieces:
            at += count
            edges.add(at)
    edges = sorted(edges)
    return [(a, b - a) for a, b in zip(edges[:-1], edges[1:])]


def reorder_kernel(meta, inv, out, *, step):
    for level in range(LEVELS):
        shape = inv.shape[1:]
        row_id = lax.broadcasted_iota(jnp.int32, shape, 0)
        col_id = lax.broadcasted_iota(jnp.int32, shape, 1)
        source = jnp.bitwise_xor(col_id, meta[step * (level + 1) - 1])
        swap = jnp.where(row_id == source, 1.0, 0.0).astype(BF16)
        out[level] = jnp.dot(inv[level], swap, preferred_element_type=F32).astype(BF16)


def eliminate(meta, inv, panel, merged, top, pairs, outs, level, blocks):
    width = blocks * BLOCK
    base = level * meta.shape[0] // LEVELS

    def at(j):
        return pl.ds(pl.multiple_of(j * BLOCK, BLOCK), BLOCK)

    def read(pieces, start, rows, j):
        ref, low = cut(pieces, start, rows)
        return ref[pl.ds(low, rows), at(j)].astype(F32)

    def order(j):
        return meta[base + j]

    if top is not None:
        a, b = top
        half = sum(count for _, _, count in a)

        def merge_block(j, carry):
            other = order(j)
            keep_a = meta[base + blocks + j].astype(F32)
            keep_b = meta[base + 2 * blocks + j].astype(F32)
            for start, rows in segments(a, b):
                from_a = read(a, start, rows, j) + read(b, start, rows, other)
                from_b = read(b, start, rows, j) + read(a, start, rows, other)
                low, high = pl.ds(start, rows), pl.ds(half + start, rows)
                merged[low, at(j)] = from_a
                merged[high, at(j)] = from_b
                panel[low, at(j)] = (from_a * keep_a).astype(BF16)
                panel[high, at(j)] = (from_b * keep_b).astype(BF16)
            return carry

        lax.fori_loop(0, blocks, merge_block, 0, unroll=4)

    def columns(job, j):
        source, start, rows = job
        if source == "top":
            return merged[pl.ds(start, rows), at(j)]
        a, b = pairs[source]
        return read(a, start, rows, j) + read(b, start, rows, order(j))

    jobs = [job for _, dest in outs for job in dest]
    pivots = [meta[base + 3 * blocks + i] for i in range(inv.shape[1] // BLOCK)]
    coupling = jnp.concatenate(
        [jnp.concatenate([columns(job, p) for p in pivots], axis=1).astype(BF16) for job in jobs],
        axis=0,
    )
    weights = jnp.dot(coupling, inv[level], preferred_element_type=F32).astype(BF16)

    def finish_tile(t, carry):
        lanes = pl.ds(pl.multiple_of(t * TILE, TILE), TILE)
        update = jnp.dot(weights, panel[:, lanes], preferred_element_type=F32)
        done = 0
        for out, dest in outs:
            put = 0
            for job in dest:
                rows = job[2]
                for i in range(TILE // BLOCK):
                    j = (TILE // BLOCK) * t + i
                    part = update[done : done + rows, i * BLOCK : (i + 1) * BLOCK]
                    out[pl.ds(put, rows), at(j)] = (columns(job, j) - part).astype(BF16)
                put += rows
                done += rows
        return carry

    lax.fori_loop(0, width // TILE, finish_tile, 0, unroll=4)


def level_kernel(meta, *refs, level, blocks, n_in, top, pairs, outs, n_hidden):
    ins, rest = refs[:n_in], refs[n_in + n_hidden :]
    out_refs, rest = rest[: len(outs)], rest[len(outs) :]

    def stack(spec):
        return [(ins[i], low, count) for i, low, count in spec]

    panel, merged = rest if top is not None else (ins[1], None)
    eliminate(
        meta,
        ins[0],
        panel,
        merged,
        None if top is None else tuple(stack(s) for s in top),
        [tuple(stack(s) for s in pair) for pair in pairs],
        list(zip(out_refs, outs)),
        level,
        blocks,
    )


def two_level_kernel(meta, inv, *refs, blocks, counts, first_outs, second_outs, pairs):
    n = len(counts)
    ours, theirs, near, near_x = refs[:n], refs[n : 2 * n], *refs[2 * n : 2 * n + 2]
    outs, panel, other_panel, merged, far, far_x = refs[2 * n + 2 : -5], *refs[-5:]
    stacks = tuple([(ref, 0, count) for ref, count in zip(group, counts)] for group in (ours, theirs))
    eliminate(meta, inv, other_panel, merged, stacks, [], list(zip((far, far_x), first_outs)), 0, blocks)
    held = ((near, far), (near_x, far_x))
    top = tuple([(ref, 0, ref.shape[0])] for ref in (near, far))
    stacked = [tuple([(ref, low, rows)] for ref in held[i]) for i, low, rows in pairs]
    eliminate(meta, inv, panel, merged, top, stacked, list(zip(outs, second_outs)), 1, blocks)


def run_level(level, meta, held, outs, pairs=(), top=None, keeps=False, part=None, cost=0):
    arrays = list(held)

    def spec(stack):
        named = []
        for x, low, rows in stack:
            found = [i for i, seen in enumerate(arrays) if seen is x]
            if not found:
                arrays.append(x)
            named.append((found[0] if found else len(arrays) - 1, low, rows))
        return tuple(named)

    top_spec = None if top is None else (spec(top[0]), spec(top[1]))
    pair_specs = tuple((spec(a), spec(b)) for a, b in pairs)
    n_in = len(arrays)
    width = arrays[-1].shape[1]
    size = held[0].shape[1]
    counts = [sum(job[2] for job in dest) for dest in outs]
    shapes = [jax.ShapeDtypeStruct((rows, width), BF16) for rows in counts]
    whole = pl.BlockSpec(memory_space=pltpu.VMEM)
    in_specs = [pl.BlockSpec(memory_space=pltpu.SMEM)] + [whole] * n_in
    out_specs = [whole] * len(shapes)
    aliases = {}
    hidden = []
    if part is not None:
        all_rows, block, old = part
        shapes[0] = jax.ShapeDtypeStruct((all_rows, width), BF16)
        out_specs[0] = pl.BlockSpec((counts[0], width), lambda i: (block, 0))
        if old is not None:
            hidden = [old]
            in_specs.append(pl.BlockSpec(memory_space=pl.ANY))
            aliases = {1 + n_in: 0}
    scratch = []
    if top is not None:
        if keeps:
            shapes.append(jax.ShapeDtypeStruct((size, width), BF16))
            out_specs.append(whole)
        else:
            scratch.append(pltpu.VMEM((size, width), BF16))
        scratch.append(pltpu.VMEM((size, width), F32))
    kernel = functools.partial(
        level_kernel,
        level=level,
        blocks=width // BLOCK,
        n_in=n_in,
        top=top_spec,
        pairs=pair_specs,
        outs=tuple(tuple(dest) for dest in outs),
        n_hidden=len(hidden),
    )
    return pl.pallas_call(
        kernel,
        grid=(1,) if part is not None else (),
        out_shape=shapes,
        in_specs=in_specs,
        out_specs=out_specs,
        scratch_shapes=scratch,
        input_output_aliases=aliases,
        compiler_params=pltpu.CompilerParams(vmem_limit_bytes=30 * 2**20),
        cost_estimate=pl.CostEstimate(flops=cost, bytes_accessed=0, transcendentals=0),
        name=f"level{level}_rows{sum(counts)}",
    )(meta, *arrays, *hidden)


def run_two_levels(meta, inv, ours, theirs, near, near_x, first_outs, second_outs, pairs):
    width, size = near.shape[1], inv.shape[1]
    rows = [sum(job[2] for job in dest) for dest in second_outs] + [size]
    vmem = pl.BlockSpec(memory_space=pltpu.VMEM)
    kernel = functools.partial(
        two_level_kernel,
        blocks=width // BLOCK,
        counts=tuple(x.shape[0] for x in ours),
        first_outs=first_outs,
        second_outs=second_outs,
        pairs=pairs,
    )
    return pl.pallas_call(
        kernel,
        out_shape=[jax.ShapeDtypeStruct((n, width), BF16) for n in rows],
        in_specs=[pl.BlockSpec(memory_space=pltpu.SMEM)] + [vmem] * (3 + 2 * len(ours)),
        out_specs=[vmem] * len(rows),
        scratch_shapes=[
            pltpu.VMEM((size, width), BF16),
            pltpu.VMEM((size, width), F32),
            pltpu.VMEM(near.shape, BF16),
            pltpu.VMEM(near_x.shape, BF16),
        ],
        compiler_params=pltpu.CompilerParams(vmem_limit_bytes=30 * 2**20),
        cost_estimate=pl.CostEstimate(flops=0, bytes_accessed=0, transcendentals=0),
        name="level0_level1",
    )(meta, inv, *ours, *theirs, near, near_x)


def reorder(meta, pivot_inverse):
    step = meta.shape[0] // LEVELS
    return pl.pallas_call(
        functools.partial(reorder_kernel, step=step),
        out_shape=jax.ShapeDtypeStruct(pivot_inverse.shape, BF16),
        in_specs=[pl.BlockSpec(memory_space=pltpu.SMEM), pl.BlockSpec(memory_space=pltpu.VMEM)],
        out_specs=pl.BlockSpec(memory_space=pltpu.VMEM),
        compiler_params=pltpu.CompilerParams(vmem_limit_bytes=30 * 2**20),
        cost_estimate=pl.CostEstimate(flops=0, bytes_accessed=0, transcendentals=0),
        name="reorder",
    )(meta, pivot_inverse)


def make_meta(size, block_pattern, column_order, pivot_blocks):
    blocks = column_order.shape[1]
    rank = jnp.int32(0)
    meta = []
    for level in range(LEVELS):
        bit = my_bit(level)
        rank = rank + bit * (1 << level)
        shift = rank * (size >> (level + 1))
        meta += [
            column_order[level],
            jnp.where(bit == 0, block_pattern[level, 0], block_pattern[level, 1]),
            jnp.where(bit == 0, block_pattern[level, 1], block_pattern[level, 0]),
            pivot_blocks[level],
            jnp.zeros((blocks,), jnp.int32) + shift,
        ]
    return jnp.concatenate(meta)


def on_device(schur_slab, pivot_inverse, block_pattern, column_order, pivot_blocks):
    all_rows = schur_slab.shape[0]
    size = pivot_inverse.shape[1]
    half, quarter, eighth, share = size // 2, size // 4, size // 8, size // 16
    meta = make_meta(size, block_pattern, column_order, pivot_blocks)

    def rows_of(x):
        return [(x, 0, x.shape[0])]

    def chunk(level, panel, own, other, **more):
        (out,) = run_level(
            level, meta, (inv, panel), [[(0, 0, own.shape[0])]], pairs=[(rows_of(own), rows_of(other))], **more
        )
        return out

    cut_1 = quarter + share
    cut_2 = half + quarter
    begin_1 = schur_slab[:cut_1]
    first_z1 = trade(begin_1, 1)
    begin_y1 = trade(begin_1, 0)
    slab, begin_1 = after(schur_slab, begin_1)
    begin_2, begin_3, rest_2 = slab[cut_1:half], slab[half:cut_2], slab[cut_2:]
    begin_y2, begin_y3 = trade(begin_2, 0), trade(begin_3, 0)
    inv = reorder(meta, pivot_inverse)

    first_yz1 = trade(first_z1, 0)
    first_2, first_z1 = after(begin_2, first_z1)
    first_z2 = trade(first_2, 1)
    rest_2, begin_y3 = after(rest_2, begin_y3)

    tops = [("top", 0, quarter), ("top", half, quarter)]
    begun = ((begin_1, begin_2, begin_3), (begin_y1, begin_y2, begin_y3))
    near, near_x, after_1, panel_0 = run_level(
        0,
        meta,
        (inv,),
        [tops, [("top", quarter, quarter)], [(0, 0, quarter)]],
        top=tuple(rows_of(x) + rows_of(y) for x, y, _ in begun),
        pairs=[tuple(rows_of(x) for *_, x in begun)],
        keeps=True,
    )
    first_z2, after_1 = after(first_z2, after_1)
    after_z1 = trade(after_1, 1)
    first_z2, first_yz1 = after(first_z2, first_yz1)
    first_yz2 = trade(first_z2, 0)
    rest_2, first_yz2 = after(rest_2, first_yz2)
    rest_y2 = trade(rest_2, 0)

    e, y, z, yz = (("top", low, eighth) for low in range(0, size, quarter))
    jobs = [[e, (*y[:2], share)], [("top", quarter + share, share), z], [yz]]
    jobs.append([(0, 0, eighth), (1, 0, quarter)])
    *head, next_0, panel_1 = run_two_levels(
        meta,
        inv,
        (first_z1, first_z2),
        (first_yz1, first_yz2),
        near,
        near_x,
        (tuple(tops), (("top", quarter, quarter),)),
        jobs,
        ((0, eighth, eighth), (1, 0, quarter)),
    )
    head_c = [trade(x, 2) for x in head]

    tops = [("top", low, share) for low in range(0, size, eighth)]
    lead, others, panel_2 = run_level(
        2,
        meta,
        (inv,),
        [[tops[0], tops[2], ("top", share, share)], [tops[i] for i in (1, 3, 4, 5, 6, 7)]],
        top=tuple(sum((rows_of(x) for x in group), []) for group in (head, head_c)),
        keeps=True,
    )
    lead_w = trade(lead, 3)
    after_z1, rest_y2, lead = after(after_z1, rest_y2, lead)
    next_1 = run_level(
        1,
        meta,
        (inv, panel_1),
        [[(0, 0, eighth)], [(0, eighth, eighth)]],
        pairs=[(rows_of(after_1), rows_of(after_z1))],
        cost=10**10,
    )
    next_1 = [next_0, *next_1]
    next_c1 = [trade(x, 2) for x in next_1]
    after_2 = chunk(0, panel_0, rest_2, rest_y2, cost=0)
    after_z2 = trade(after_2, 1)
    next_c1[0], after_2 = after(next_c1[0], after_2)
    (last_1,) = run_level(
        2,
        meta,
        (inv, panel_2),
        [[(i, 0, x.shape[0]) for i, x in enumerate(next_1)]],
        pairs=[(rows_of(x), rows_of(y)) for x, y in zip(next_1, next_c1)],
    )
    last_w1 = trade(last_1, 3)
    tops_w = lead_w[:eighth]
    tops_wc = trade(tops_w, 2)
    tops_wy = trade(tops_w, 0)
    after_z2, tops_wy = after(after_z2, tops_wy)
    tops_wyc = trade(tops_wy, 2)
    next_2 = chunk(1, panel_1, after_2, after_z2, cost=5 * 10**9)
    last_2 = chunk(2, panel_2, next_2, trade(next_2, 2))
    last_w2 = trade(last_2, 3)
    more = lead.shape[0] - eighth
    tops = [(lead, 0, share), (others, 0, share), (lead, share, share)]
    tops += [(others, share * i, share) for i in range(1, 6)]
    tops_other = [(x, low, share) for low in (0, share) for x in (tops_w, tops_wy)]
    tops_other += [(x, low, share) for low in (0, share) for x in (tops_wc, tops_wyc)]
    out, panel_3 = run_level(
        3,
        meta,
        (inv,),
        [[("top", 0, share), (0, 0, more), (1, 0, last_1.shape[0])]],
        top=(tops, tops_other),
        pairs=[([(lead, eighth, more)], [(lead_w, eighth, more)]), (rows_of(last_1), rows_of(last_w1))],
        keeps=True,
        part=(all_rows, 0, None),
        cost=5 * 10**10,
    )
    return chunk(3, panel_3, last_2, last_w2, part=(all_rows, all_rows // quarter - 1, out))


def solution(mesh):
    return jax.shard_map(
        on_device,
        mesh=mesh,
        in_specs=(P(("tx", "ty"), None), P(), P(), P(), P()),
        out_specs=P(("tx", "ty"), None),
        check_vma=False,
    )
```

```python
import functools

import jax
import jax.numpy as jnp
from jax import lax
from jax.experimental import pallas as pl
from jax.experimental.pallas import tpu as pltpu
from jax.sharding import PartitionSpec as P

BLOCK = 128
LEVELS = 4
TILE = 2 * BLOCK
F32 = jnp.float32
BF16 = jnp.bfloat16


def stride_bit(axis, level):
    return lax.axis_size(axis).bit_length() - 2 - level // 2


def level_axis(level):
    return "tx" if level % 2 == 0 else "ty"


def trade(block, level):
    axis = level_axis(level)
    flip = 1 << stride_bit(axis, level)
    return lax.ppermute(block, axis, [(i, i ^ flip) for i in range(lax.axis_size(axis))])


def my_bit(level):
    axis = level_axis(level)
    place = lax.axis_index(axis).astype(jnp.int32)
    return jnp.bitwise_and(jnp.right_shift(place, stride_bit(axis, level)), 1)


def after(x, *others):
    return lax.optimization_barrier((x, *others))


def cut(pieces, start, rows):
    for ref, low, count in pieces:
        if start < count:
            assert start + rows <= count
            return ref, low + start
        start -= count
    raise ValueError


def segments(one, other):
    edges = {0}
    for pieces in (one, other):
        at = 0
        for _, _, count in pieces:
            at += count
            edges.add(at)
    edges = sorted(edges)
    return [(a, b - a) for a, b in zip(edges[:-1], edges[1:])]


def reorder_kernel(meta, inv, out, *, step):
    for level in range(LEVELS):
        shape = inv.shape[1:]
        row_id = lax.broadcasted_iota(jnp.int32, shape, 0)
        col_id = lax.broadcasted_iota(jnp.int32, shape, 1)
        source = jnp.bitwise_xor(col_id, meta[step * (level + 1) - 1])
        swap = jnp.where(row_id == source, 1.0, 0.0).astype(BF16)
        out[level] = jnp.dot(inv[level], swap, preferred_element_type=F32).astype(BF16)


def eliminate(meta, inv, panel, merged, top, pairs, outs, level, blocks):
    width = blocks * BLOCK
    base = level * meta.shape[0] // LEVELS

    def at(j):
        return pl.ds(pl.multiple_of(j * BLOCK, BLOCK), BLOCK)

    def read(pieces, start, rows, j):
        ref, low = cut(pieces, start, rows)
        return ref[pl.ds(low, rows), at(j)].astype(F32)

    def order(j):
        return meta[base + j]

    jobs = [job for _, dest in outs for job in dest]
    if top is not None:
        a, b = top
        half = sum(count for _, _, count in a)
        kept = [(start, start + rows) for source, start, rows in jobs if source == "top"]

        def keep(value, first, rows, j):
            for low, high in kept:
                low, high = max(low, first), min(high, first + rows)
                if low < high:
                    merged[pl.ds(low, high - low), at(j)] = value[low - first : high - first]

        def merge_block(j, carry):
            other = order(j)
            keep_a = meta[base + blocks + j].astype(F32)
            keep_b = meta[base + 2 * blocks + j].astype(F32)
            for start, rows in segments(a, b):
                from_a = read(a, start, rows, j) + read(b, start, rows, other)
                from_b = read(b, start, rows, j) + read(a, start, rows, other)
                keep(from_a, start, rows, j)
                keep(from_b, half + start, rows, j)
                panel[pl.ds(start, rows), at(j)] = (from_a * keep_a).astype(BF16)
                panel[pl.ds(half + start, rows), at(j)] = (from_b * keep_b).astype(BF16)
            return carry

        lax.fori_loop(0, blocks, merge_block, 0, unroll=8)

    def columns(job, j):
        source, start, rows = job
        if source == "top":
            return merged[pl.ds(start, rows), at(j)]
        a, b = pairs[source]
        return read(a, start, rows, j) + read(b, start, rows, order(j))

    pivots = [meta[base + 3 * blocks + i] for i in range(inv.shape[1] // BLOCK)]
    coupling = jnp.concatenate(
        [jnp.concatenate([columns(job, p) for p in pivots], axis=1).astype(BF16) for job in jobs],
        axis=0,
    )
    weights = jnp.dot(coupling, inv[level], preferred_element_type=F32).astype(BF16)

    def finish_tile(t, carry):
        lanes = pl.ds(pl.multiple_of(t * TILE, TILE), TILE)
        update = jnp.dot(weights, panel[:, lanes], preferred_element_type=F32)
        done = 0
        for out, dest in outs:
            put = 0
            for job in dest:
                rows = job[2]
                for i in range(TILE // BLOCK):
                    j = (TILE // BLOCK) * t + i
                    part = update[done : done + rows, i * BLOCK : (i + 1) * BLOCK]
                    out[pl.ds(put, rows), at(j)] = (columns(job, j) - part).astype(BF16)
                put += rows
                done += rows
        return carry

    lax.fori_loop(0, width // TILE, finish_tile, 0, unroll=8)


def level_kernel(meta, *refs, level, blocks, n_in, top, pairs, outs, n_hidden):
    ins, rest = refs[:n_in], refs[n_in + n_hidden :]
    out_refs, rest = rest[: len(outs)], rest[len(outs) :]

    def stack(spec):
        return [(ins[i], low, count) for i, low, count in spec]

    panel, merged = rest if top is not None else (ins[1], None)
    eliminate(
        meta,
        ins[0],
        panel,
        merged,
        None if top is None else tuple(stack(s) for s in top),
        [tuple(stack(s) for s in pair) for pair in pairs],
        list(zip(out_refs, outs)),
        level,
        blocks,
    )


def two_level_kernel(meta, inv, *refs, blocks, counts, first_outs, second_outs, pairs):
    n = len(counts)
    ours, theirs, near, near_x = refs[:n], refs[n : 2 * n], *refs[2 * n : 2 * n + 2]
    outs, panel, other_panel, merged, far, far_x = refs[2 * n + 2 : -5], *refs[-5:]
    stacks = tuple([(ref, 0, count) for ref, count in zip(group, counts)] for group in (ours, theirs))
    eliminate(meta, inv, other_panel, merged, stacks, [], list(zip((far, far_x), first_outs)), 0, blocks)
    held = ((near, far), (near_x, far_x))
    top = tuple([(ref, 0, ref.shape[0])] for ref in (near, far))
    stacked = [tuple([(ref, low, rows)] for ref in held[i]) for i, low, rows in pairs]
    eliminate(meta, inv, panel, merged, top, stacked, list(zip(outs, second_outs)), 1, blocks)


def run_level(level, meta, held, outs, pairs=(), top=None, keeps=False, part=None, cost=0):
    arrays = list(held)

    def spec(stack):
        named = []
        for x, low, rows in stack:
            found = [i for i, seen in enumerate(arrays) if seen is x]
            if not found:
                arrays.append(x)
            named.append((found[0] if found else len(arrays) - 1, low, rows))
        return tuple(named)

    top_spec = None if top is None else (spec(top[0]), spec(top[1]))
    pair_specs = tuple((spec(a), spec(b)) for a, b in pairs)
    n_in = len(arrays)
    width = arrays[-1].shape[1]
    size = held[0].shape[1]
    counts = [sum(job[2] for job in dest) for dest in outs]
    shapes = [jax.ShapeDtypeStruct((rows, width), BF16) for rows in counts]
    whole = pl.BlockSpec(memory_space=pltpu.VMEM)
    in_specs = [pl.BlockSpec(memory_space=pltpu.SMEM)] + [whole] * n_in
    out_specs = [whole] * len(shapes)
    aliases = {}
    hidden = []
    if part is not None:
        all_rows, block, old = part
        shapes[0] = jax.ShapeDtypeStruct((all_rows, width), BF16)
        out_specs[0] = pl.BlockSpec((counts[0], width), lambda i: (block, 0))
        if old is not None:
            hidden = [old]
            in_specs.append(pl.BlockSpec(memory_space=pl.ANY))
            aliases = {1 + n_in: 0}
    scratch = []
    if top is not None:
        if keeps:
            shapes.append(jax.ShapeDtypeStruct((size, width), BF16))
            out_specs.append(whole)
        else:
            scratch.append(pltpu.VMEM((size, width), BF16))
        scratch.append(pltpu.VMEM((size, width), F32))
    kernel = functools.partial(
        level_kernel,
        level=level,
        blocks=width // BLOCK,
        n_in=n_in,
        top=top_spec,
        pairs=pair_specs,
        outs=tuple(tuple(dest) for dest in outs),
        n_hidden=len(hidden),
    )
    return pl.pallas_call(
        kernel,
        grid=(1,) if part is not None else (),
        out_shape=shapes,
        in_specs=in_specs,
        out_specs=out_specs,
        scratch_shapes=scratch,
        input_output_aliases=aliases,
        compiler_params=pltpu.CompilerParams(vmem_limit_bytes=30 * 2**20),
        cost_estimate=pl.CostEstimate(flops=cost, bytes_accessed=0, transcendentals=0),
        name=f"level{level}_rows{sum(counts)}",
    )(meta, *arrays, *hidden)


def run_two_levels(meta, inv, ours, theirs, near, near_x, first_outs, second_outs, pairs):
    width, size = near.shape[1], inv.shape[1]
    rows = [sum(job[2] for job in dest) for dest in second_outs] + [size]
    vmem = pl.BlockSpec(memory_space=pltpu.VMEM)
    kernel = functools.partial(
        two_level_kernel,
        blocks=width // BLOCK,
        counts=tuple(x.shape[0] for x in ours),
        first_outs=first_outs,
        second_outs=second_outs,
        pairs=pairs,
    )
    return pl.pallas_call(
        kernel,
        out_shape=[jax.ShapeDtypeStruct((n, width), BF16) for n in rows],
        in_specs=[pl.BlockSpec(memory_space=pltpu.SMEM)] + [vmem] * (3 + 2 * len(ours)),
        out_specs=[vmem] * len(rows),
        scratch_shapes=[
            pltpu.VMEM((size, width), BF16),
            pltpu.VMEM((size, width), F32),
            pltpu.VMEM(near.shape, BF16),
            pltpu.VMEM(near_x.shape, BF16),
        ],
        compiler_params=pltpu.CompilerParams(vmem_limit_bytes=30 * 2**20),
        cost_estimate=pl.CostEstimate(flops=0, bytes_accessed=0, transcendentals=0),
        name="level0_level1",
    )(meta, inv, *ours, *theirs, near, near_x)


def reorder(meta, pivot_inverse):
    step = meta.shape[0] // LEVELS
    return pl.pallas_call(
        functools.partial(reorder_kernel, step=step),
        out_shape=jax.ShapeDtypeStruct(pivot_inverse.shape, BF16),
        in_specs=[pl.BlockSpec(memory_space=pltpu.SMEM), pl.BlockSpec(memory_space=pltpu.VMEM)],
        out_specs=pl.BlockSpec(memory_space=pltpu.VMEM),
        compiler_params=pltpu.CompilerParams(vmem_limit_bytes=30 * 2**20),
        cost_estimate=pl.CostEstimate(flops=0, bytes_accessed=0, transcendentals=0),
        name="reorder",
    )(meta, pivot_inverse)


def make_meta(size, block_pattern, column_order, pivot_blocks):
    blocks = column_order.shape[1]
    rank = jnp.int32(0)
    meta = []
    for level in range(LEVELS):
        bit = my_bit(level)
        rank = rank + bit * (1 << level)
        shift = rank * (size >> (level + 1))
        meta += [
            column_order[level],
            jnp.where(bit == 0, block_pattern[level, 0], block_pattern[level, 1]),
            jnp.where(bit == 0, block_pattern[level, 1], block_pattern[level, 0]),
            pivot_blocks[level],
            jnp.zeros((blocks,), jnp.int32) + shift,
        ]
    return jnp.concatenate(meta)


def on_device(schur_slab, pivot_inverse, block_pattern, column_order, pivot_blocks):
    all_rows = schur_slab.shape[0]
    size = pivot_inverse.shape[1]
    half, quarter, eighth, share = size // 2, size // 4, size // 8, size // 16
    meta = make_meta(size, block_pattern, column_order, pivot_blocks)

    def rows_of(x):
        return [(x, 0, x.shape[0])]

    def chunk(level, panel, own, other, **more):
        (out,) = run_level(
            level, meta, (inv, panel), [[(0, 0, own.shape[0])]], pairs=[(rows_of(own), rows_of(other))], **more
        )
        return out

    cut_1 = quarter + share
    cut_2 = half + quarter
    begin_1 = schur_slab[:cut_1]
    first_z1 = trade(begin_1, 1)
    begin_y1 = trade(begin_1, 0)
    slab, begin_1 = after(schur_slab, begin_1)
    begin_2, begin_3, rest_2 = slab[cut_1:half], slab[half:cut_2], slab[cut_2:]
    begin_y2, begin_y3 = trade(begin_2, 0), trade(begin_3, 0)
    inv = reorder(meta, pivot_inverse)

    first_yz1 = trade(first_z1, 0)
    first_2, first_z1 = after(begin_2, first_z1)
    first_z2 = trade(first_2, 1)
    rest_2, begin_y3 = after(rest_2, begin_y3)

    tops = [("top", 0, quarter), ("top", half, quarter)]
    begun = ((begin_1, begin_2, begin_3), (begin_y1, begin_y2, begin_y3))
    near, near_x, after_1, panel_0 = run_level(
        0,
        meta,
        (inv,),
        [tops, [("top", quarter, quarter)], [(0, 0, quarter)]],
        top=tuple(rows_of(x) + rows_of(y) for x, y, _ in begun),
        pairs=[tuple(rows_of(x) for *_, x in begun)],
        keeps=True,
    )
    first_z2, after_1 = after(first_z2, after_1)
    after_z1 = trade(after_1, 1)
    first_z2, first_yz1 = after(first_z2, first_yz1)
    first_yz2 = trade(first_z2, 0)
    rest_2, first_yz2 = after(rest_2, first_yz2)
    rest_y2 = trade(rest_2, 0)

    e, y, z, yz = (("top", low, eighth) for low in range(0, size, quarter))
    jobs = [[e, (*y[:2], share)], [("top", quarter + share, share), z], [yz]]
    jobs.append([(0, 0, eighth), (1, 0, quarter)])
    *head, next_0, panel_1 = run_two_levels(
        meta,
        inv,
        (first_z1, first_z2),
        (first_yz1, first_yz2),
        near,
        near_x,
        (tuple(tops), (("top", quarter, quarter),)),
        jobs,
        ((0, eighth, eighth), (1, 0, quarter)),
    )
    head_c = [trade(x, 2) for x in head]

    tops = [("top", low, share) for low in range(0, size, eighth)]
    lead, others, panel_2 = run_level(
        2,
        meta,
        (inv,),
        [[tops[0], tops[2], ("top", share, share)], [tops[i] for i in (1, 3, 4, 5, 6, 7)]],
        top=tuple(sum((rows_of(x) for x in group), []) for group in (head, head_c)),
        keeps=True,
    )
    lead_w = trade(lead, 3)
    after_z1, rest_y2, lead = after(after_z1, rest_y2, lead)
    next_1 = run_level(
        1,
        meta,
        (inv, panel_1),
        [[(0, 0, eighth)], [(0, eighth, eighth)]],
        pairs=[(rows_of(after_1), rows_of(after_z1))],
        cost=10**10,
    )
    next_1 = [next_0, *next_1]
    next_c1 = [trade(x, 2) for x in next_1]
    after_2 = chunk(0, panel_0, rest_2, rest_y2, cost=0)
    after_z2 = trade(after_2, 1)
    next_c1[0], after_2 = after(next_c1[0], after_2)
    (last_1,) = run_level(
        2,
        meta,
        (inv, panel_2),
        [[(i, 0, x.shape[0]) for i, x in enumerate(next_1)]],
        pairs=[(rows_of(x), rows_of(y)) for x, y in zip(next_1, next_c1)],
    )
    last_w1 = trade(last_1, 3)
    tops_w = lead_w[:eighth]
    tops_wc = trade(tops_w, 2)
    tops_wy = trade(tops_w, 0)
    after_z2, tops_wy = after(after_z2, tops_wy)
    tops_wyc = trade(tops_wy, 2)
    next_2 = chunk(1, panel_1, after_2, after_z2, cost=5 * 10**9)
    last_2 = chunk(2, panel_2, next_2, trade(next_2, 2))
    last_w2 = trade(last_2, 3)
    more = lead.shape[0] - eighth
    tops = [(lead, 0, share), (others, 0, share), (lead, share, share)]
    tops += [(others, share * i, share) for i in range(1, 6)]
    tops_other = [(x, low, share) for low in (0, share) for x in (tops_w, tops_wy)]
    tops_other += [(x, low, share) for low in (0, share) for x in (tops_wc, tops_wyc)]
    out, panel_3 = run_level(
        3,
        meta,
        (inv,),
        [[("top", 0, share), (0, 0, more), (1, 0, last_1.shape[0])]],
        top=(tops, tops_other),
        pairs=[([(lead, eighth, more)], [(lead_w, eighth, more)]), (rows_of(last_1), rows_of(last_w1))],
        keeps=True,
        part=(all_rows, 0, None),
        cost=5 * 10**10,
    )
    return chunk(3, panel_3, last_2, last_w2, part=(all_rows, all_rows // quarter - 1, out))


def solution(mesh):
    return jax.shard_map(
        on_device,
        mesh=mesh,
        in_specs=(P(("tx", "ty"), None), P(), P(), P(), P()),
        out_specs=P(("tx", "ty"), None),
        check_vma=False,
    )
```

```python
import functools

import jax
import jax.numpy as jnp
from jax import lax
from jax.experimental import pallas as pl
from jax.experimental.pallas import tpu as pltpu
from jax.sharding import PartitionSpec as P

BLOCK = 128
LEVELS = 4
TILE = 2 * BLOCK
F32 = jnp.float32
BF16 = jnp.bfloat16


def stride_bit(axis, level):
    return lax.axis_size(axis).bit_length() - 2 - level // 2


def level_axis(level):
    return "tx" if level % 2 == 0 else "ty"


def trade(block, level):
    axis = level_axis(level)
    flip = 1 << stride_bit(axis, level)
    return lax.ppermute(block, axis, [(i, i ^ flip) for i in range(lax.axis_size(axis))])


def my_bit(level):
    axis = level_axis(level)
    place = lax.axis_index(axis).astype(jnp.int32)
    return jnp.bitwise_and(jnp.right_shift(place, stride_bit(axis, level)), 1)


def after(x, *others):
    return lax.optimization_barrier((x, *others))


def cut(pieces, start, rows):
    for ref, low, count in pieces:
        if start < count:
            assert start + rows <= count
            return ref, low + start
        start -= count
    raise ValueError


def segments(one, other):
    edges = {0}
    for pieces in (one, other):
        at = 0
        for _, _, count in pieces:
            at += count
            edges.add(at)
    edges = sorted(edges)
    return [(a, b - a) for a, b in zip(edges[:-1], edges[1:])]


def reorder_kernel(meta, inv, out, *, step):
    for level in range(LEVELS):
        shape = inv.shape[1:]
        row_id = lax.broadcasted_iota(jnp.int32, shape, 0)
        col_id = lax.broadcasted_iota(jnp.int32, shape, 1)
        source = jnp.bitwise_xor(col_id, meta[step * (level + 1) - 1])
        swap = jnp.where(row_id == source, 1.0, 0.0).astype(BF16)
        out[level] = jnp.dot(inv[level], swap, preferred_element_type=F32).astype(BF16)


def eliminate(meta, inv, panel, merged, top, pairs, outs, level, blocks):
    width = blocks * BLOCK
    base = level * meta.shape[0] // LEVELS

    def at(j):
        return pl.ds(pl.multiple_of(j * BLOCK, BLOCK), BLOCK)

    def read(pieces, start, rows, j):
        ref, low = cut(pieces, start, rows)
        return ref[pl.ds(low, rows), at(j)].astype(F32)

    def order(j):
        return meta[base + j]

    jobs = [job for _, dest in outs for job in dest]
    if top is not None:
        a, b = top
        half = sum(count for _, _, count in a)
        kept = [(start, start + rows) for source, start, rows in jobs if source == "top"]

        def keep(value, first, rows, j):
            for low, high in kept:
                low, high = max(low, first), min(high, first + rows)
                if low < high:
                    merged[pl.ds(low, high - low), at(j)] = value[low - first : high - first]

        def merge_block(j, carry):
            other = order(j)
            keep_a = meta[base + blocks + j].astype(F32)
            keep_b = meta[base + 2 * blocks + j].astype(F32)
            for start, rows in segments(a, b):
                from_a = read(a, start, rows, j) + read(b, start, rows, other)
                from_b = read(b, start, rows, j) + read(a, start, rows, other)
                keep(from_a, start, rows, j)
                keep(from_b, half + start, rows, j)
                panel[pl.ds(start, rows), at(j)] = (from_a * keep_a).astype(BF16)
                panel[pl.ds(half + start, rows), at(j)] = (from_b * keep_b).astype(BF16)
            return carry

        lax.fori_loop(0, blocks, merge_block, 0, unroll=True)

    def columns(job, j):
        source, start, rows = job
        if source == "top":
            return merged[pl.ds(start, rows), at(j)]
        a, b = pairs[source]
        return read(a, start, rows, j) + read(b, start, rows, order(j))

    pivots = [meta[base + 3 * blocks + i] for i in range(inv.shape[1] // BLOCK)]
    coupling = jnp.concatenate(
        [jnp.concatenate([columns(job, p) for p in pivots], axis=1).astype(BF16) for job in jobs],
        axis=0,
    )
    weights = jnp.dot(coupling, inv[level], preferred_element_type=F32).astype(BF16)

    def finish_tile(t, carry):
        lanes = pl.ds(pl.multiple_of(t * TILE, TILE), TILE)
        update = jnp.dot(weights, panel[:, lanes], preferred_element_type=F32)
        done = 0
        for out, dest in outs:
            put = 0
            for job in dest:
                rows = job[2]
                for i in range(TILE // BLOCK):
                    j = (TILE // BLOCK) * t + i
                    part = update[done : done + rows, i * BLOCK : (i + 1) * BLOCK]
                    out[pl.ds(put, rows), at(j)] = (columns(job, j) - part).astype(BF16)
                put += rows
                done += rows
        return carry

    lax.fori_loop(0, width // TILE, finish_tile, 0, unroll=True)


def level_kernel(meta, *refs, level, blocks, n_in, top, pairs, outs, n_hidden):
    ins, rest = refs[:n_in], refs[n_in + n_hidden :]
    out_refs, rest = rest[: len(outs)], rest[len(outs) :]

    def stack(spec):
        return [(ins[i], low, count) for i, low, count in spec]

    panel, merged = rest if top is not None else (ins[1], None)
    eliminate(
        meta,
        ins[0],
        panel,
        merged,
        None if top is None else tuple(stack(s) for s in top),
        [tuple(stack(s) for s in pair) for pair in pairs],
        list(zip(out_refs, outs)),
        level,
        blocks,
    )


def two_level_kernel(meta, inv, *refs, blocks, counts, first_outs, second_outs, pairs):
    n = len(counts)
    ours, theirs, near, near_x = refs[:n], refs[n : 2 * n], *refs[2 * n : 2 * n + 2]
    outs, panel, other_panel, merged, far, far_x = refs[2 * n + 2 : -5], *refs[-5:]
    stacks = tuple([(ref, 0, count) for ref, count in zip(group, counts)] for group in (ours, theirs))
    eliminate(meta, inv, other_panel, merged, stacks, [], list(zip((far, far_x), first_outs)), 0, blocks)
    held = ((near, far), (near_x, far_x))
    top = tuple([(ref, 0, ref.shape[0])] for ref in (near, far))
    stacked = [tuple([(ref, low, rows)] for ref in held[i]) for i, low, rows in pairs]
    eliminate(meta, inv, panel, merged, top, stacked, list(zip(outs, second_outs)), 1, blocks)


def run_level(level, meta, held, outs, pairs=(), top=None, keeps=False, part=None, cost=0):
    arrays = list(held)

    def spec(stack):
        named = []
        for x, low, rows in stack:
            found = [i for i, seen in enumerate(arrays) if seen is x]
            if not found:
                arrays.append(x)
            named.append((found[0] if found else len(arrays) - 1, low, rows))
        return tuple(named)

    top_spec = None if top is None else (spec(top[0]), spec(top[1]))
    pair_specs = tuple((spec(a), spec(b)) for a, b in pairs)
    n_in = len(arrays)
    width = arrays[-1].shape[1]
    size = held[0].shape[1]
    counts = [sum(job[2] for job in dest) for dest in outs]
    shapes = [jax.ShapeDtypeStruct((rows, width), BF16) for rows in counts]
    whole = pl.BlockSpec(memory_space=pltpu.VMEM)
    in_specs = [pl.BlockSpec(memory_space=pltpu.SMEM)] + [whole] * n_in
    out_specs = [whole] * len(shapes)
    aliases = {}
    hidden = []
    if part is not None:
        all_rows, block, old = part
        shapes[0] = jax.ShapeDtypeStruct((all_rows, width), BF16)
        out_specs[0] = pl.BlockSpec((counts[0], width), lambda i: (block, 0))
        if old is not None:
            hidden = [old]
            in_specs.append(pl.BlockSpec(memory_space=pl.ANY))
            aliases = {1 + n_in: 0}
    scratch = []
    if top is not None:
        if keeps:
            shapes.append(jax.ShapeDtypeStruct((size, width), BF16))
            out_specs.append(whole)
        else:
            scratch.append(pltpu.VMEM((size, width), BF16))
        scratch.append(pltpu.VMEM((size, width), F32))
    kernel = functools.partial(
        level_kernel,
        level=level,
        blocks=width // BLOCK,
        n_in=n_in,
        top=top_spec,
        pairs=pair_specs,
        outs=tuple(tuple(dest) for dest in outs),
        n_hidden=len(hidden),
    )
    return pl.pallas_call(
        kernel,
        grid=(1,) if part is not None else (),
        out_shape=shapes,
        in_specs=in_specs,
        out_specs=out_specs,
        scratch_shapes=scratch,
        input_output_aliases=aliases,
        compiler_params=pltpu.CompilerParams(vmem_limit_bytes=30 * 2**20),
        cost_estimate=pl.CostEstimate(flops=cost, bytes_accessed=0, transcendentals=0),
        name=f"level{level}_rows{sum(counts)}",
    )(meta, *arrays, *hidden)


def run_two_levels(meta, inv, ours, theirs, near, near_x, first_outs, second_outs, pairs):
    width, size = near.shape[1], inv.shape[1]
    rows = [sum(job[2] for job in dest) for dest in second_outs] + [size]
    vmem = pl.BlockSpec(memory_space=pltpu.VMEM)
    kernel = functools.partial(
        two_level_kernel,
        blocks=width // BLOCK,
        counts=tuple(x.shape[0] for x in ours),
        first_outs=first_outs,
        second_outs=second_outs,
        pairs=pairs,
    )
    return pl.pallas_call(
        kernel,
        out_shape=[jax.ShapeDtypeStruct((n, width), BF16) for n in rows],
        in_specs=[pl.BlockSpec(memory_space=pltpu.SMEM)] + [vmem] * (3 + 2 * len(ours)),
        out_specs=[vmem] * len(rows),
        scratch_shapes=[
            pltpu.VMEM((size, width), BF16),
            pltpu.VMEM((size, width), F32),
            pltpu.VMEM(near.shape, BF16),
            pltpu.VMEM(near_x.shape, BF16),
        ],
        compiler_params=pltpu.CompilerParams(vmem_limit_bytes=30 * 2**20),
        cost_estimate=pl.CostEstimate(flops=0, bytes_accessed=0, transcendentals=0),
        name="level0_level1",
    )(meta, inv, *ours, *theirs, near, near_x)


def reorder(meta, pivot_inverse):
    step = meta.shape[0] // LEVELS
    return pl.pallas_call(
        functools.partial(reorder_kernel, step=step),
        out_shape=jax.ShapeDtypeStruct(pivot_inverse.shape, BF16),
        in_specs=[pl.BlockSpec(memory_space=pltpu.SMEM), pl.BlockSpec(memory_space=pltpu.VMEM)],
        out_specs=pl.BlockSpec(memory_space=pltpu.VMEM),
        compiler_params=pltpu.CompilerParams(vmem_limit_bytes=30 * 2**20),
        cost_estimate=pl.CostEstimate(flops=0, bytes_accessed=0, transcendentals=0),
        name="reorder",
    )(meta, pivot_inverse)


def make_meta(size, block_pattern, column_order, pivot_blocks):
    blocks = column_order.shape[1]
    rank = jnp.int32(0)
    meta = []
    for level in range(LEVELS):
        bit = my_bit(level)
        rank = rank + bit * (1 << level)
        shift = rank * (size >> (level + 1))
        meta += [
            column_order[level],
            jnp.where(bit == 0, block_pattern[level, 0], block_pattern[level, 1]),
            jnp.where(bit == 0, block_pattern[level, 1], block_pattern[level, 0]),
            pivot_blocks[level],
            jnp.zeros((blocks,), jnp.int32) + shift,
        ]
    return jnp.concatenate(meta)


def on_device(schur_slab, pivot_inverse, block_pattern, column_order, pivot_blocks):
    all_rows = schur_slab.shape[0]
    size = pivot_inverse.shape[1]
    half, quarter, eighth, share = size // 2, size // 4, size // 8, size // 16
    meta = make_meta(size, block_pattern, column_order, pivot_blocks)

    def rows_of(x):
        return [(x, 0, x.shape[0])]

    def chunk(level, panel, own, other, **more):
        (out,) = run_level(
            level, meta, (inv, panel), [[(0, 0, own.shape[0])]], pairs=[(rows_of(own), rows_of(other))], **more
        )
        return out

    cut_1 = quarter + share
    cut_2 = half + quarter
    begin_1 = schur_slab[:cut_1]
    first_z1 = trade(begin_1, 1)
    begin_y1 = trade(begin_1, 0)
    slab, begin_1 = after(schur_slab, begin_1)
    begin_2, begin_3, rest_2 = slab[cut_1:half], slab[half:cut_2], slab[cut_2:]
    begin_y2, begin_y3 = trade(begin_2, 0), trade(begin_3, 0)
    inv = reorder(meta, pivot_inverse)

    first_yz1 = trade(first_z1, 0)
    first_2, first_z1 = after(begin_2, first_z1)
    first_z2 = trade(first_2, 1)
    rest_2, begin_y3 = after(rest_2, begin_y3)

    tops = [("top", 0, quarter), ("top", half, quarter)]
    begun = ((begin_1, begin_2, begin_3), (begin_y1, begin_y2, begin_y3))
    near, near_x, after_1, panel_0 = run_level(
        0,
        meta,
        (inv,),
        [tops, [("top", quarter, quarter)], [(0, 0, quarter)]],
        top=tuple(rows_of(x) + rows_of(y) for x, y, _ in begun),
        pairs=[tuple(rows_of(x) for *_, x in begun)],
        keeps=True,
    )
    first_z2, after_1 = after(first_z2, after_1)
    after_z1 = trade(after_1, 1)
    first_z2, first_yz1 = after(first_z2, first_yz1)
    first_yz2 = trade(first_z2, 0)
    rest_2, first_yz2 = after(rest_2, first_yz2)
    rest_y2 = trade(rest_2, 0)

    e, y, z, yz = (("top", low, eighth) for low in range(0, size, quarter))
    jobs = [[e, (*y[:2], share)], [("top", quarter + share, share), z], [yz]]
    jobs.append([(0, 0, eighth), (1, 0, quarter)])
    *head, next_0, panel_1 = run_two_levels(
        meta,
        inv,
        (first_z1, first_z2),
        (first_yz1, first_yz2),
        near,
        near_x,
        (tuple(tops), (("top", quarter, quarter),)),
        jobs,
        ((0, eighth, eighth), (1, 0, quarter)),
    )
    head_c = [trade(x, 2) for x in head]

    tops = [("top", low, share) for low in range(0, size, eighth)]
    lead, others, panel_2 = run_level(
        2,
        meta,
        (inv,),
        [[tops[0], tops[2], ("top", share, share)], [tops[i] for i in (1, 3, 4, 5, 6, 7)]],
        top=tuple(sum((rows_of(x) for x in group), []) for group in (head, head_c)),
        keeps=True,
    )
    lead_w = trade(lead, 3)
    after_z1, rest_y2, lead = after(after_z1, rest_y2, lead)
    next_1 = run_level(
        1,
        meta,
        (inv, panel_1),
        [[(0, 0, eighth)], [(0, eighth, eighth)]],
        pairs=[(rows_of(after_1), rows_of(after_z1))],
        cost=10**10,
    )
    next_1 = [next_0, *next_1]
    next_c1 = [trade(x, 2) for x in next_1]
    after_2 = chunk(0, panel_0, rest_2, rest_y2, cost=0)
    after_z2 = trade(after_2, 1)
    next_c1[0], after_2 = after(next_c1[0], after_2)
    (last_1,) = run_level(
        2,
        meta,
        (inv, panel_2),
        [[(i, 0, x.shape[0]) for i, x in enumerate(next_1)]],
        pairs=[(rows_of(x), rows_of(y)) for x, y in zip(next_1, next_c1)],
    )
    last_w1 = trade(last_1, 3)
    tops_w = lead_w[:eighth]
    tops_wc = trade(tops_w, 2)
    tops_wy = trade(tops_w, 0)
    after_z2, tops_wy = after(after_z2, tops_wy)
    tops_wyc = trade(tops_wy, 2)
    next_2 = chunk(1, panel_1, after_2, after_z2, cost=5 * 10**9)
    last_2 = chunk(2, panel_2, next_2, trade(next_2, 2))
    last_w2 = trade(last_2, 3)
    more = lead.shape[0] - eighth
    tops = [(lead, 0, share), (others, 0, share), (lead, share, share)]
    tops += [(others, share * i, share) for i in range(1, 6)]
    tops_other = [(x, low, share) for low in (0, share) for x in (tops_w, tops_wy)]
    tops_other += [(x, low, share) for low in (0, share) for x in (tops_wc, tops_wyc)]
    out, panel_3 = run_level(
        3,
        meta,
        (inv,),
        [[("top", 0, share), (0, 0, more), (1, 0, last_1.shape[0])]],
        top=(tops, tops_other),
        pairs=[([(lead, eighth, more)], [(lead_w, eighth, more)]), (rows_of(last_1), rows_of(last_w1))],
        keeps=True,
        part=(all_rows, 0, None),
        cost=5 * 10**10,
    )
    return chunk(3, panel_3, last_2, last_w2, part=(all_rows, all_rows // quarter - 1, out))


def solution(mesh):
    return jax.shard_map(
        on_device,
        mesh=mesh,
        in_specs=(P(("tx", "ty"), None), P(), P(), P(), P()),
        out_specs=P(("tx", "ty"), None),
        check_vma=False,
    )
```

```python
import functools

import jax
import jax.numpy as jnp
from jax import lax
from jax.experimental import pallas as pl
from jax.experimental.pallas import tpu as pltpu
from jax.sharding import PartitionSpec as P

BLOCK = 128
LEVELS = 4
TILE = 2 * BLOCK
F32 = jnp.float32
BF16 = jnp.bfloat16


def stride_bit(axis, level):
    return lax.axis_size(axis).bit_length() - 2 - level // 2


def level_axis(level):
    return "tx" if level % 2 == 0 else "ty"


def trade(block, level):
    axis = level_axis(level)
    flip = 1 << stride_bit(axis, level)
    return lax.ppermute(block, axis, [(i, i ^ flip) for i in range(lax.axis_size(axis))])


def my_bit(level):
    axis = level_axis(level)
    place = lax.axis_index(axis).astype(jnp.int32)
    return jnp.bitwise_and(jnp.right_shift(place, stride_bit(axis, level)), 1)


def after(x, *others):
    return lax.optimization_barrier((x, *others))


def cut(pieces, start, rows):
    for ref, low, count in pieces:
        if start < count:
            assert start + rows <= count
            return ref, low + start
        start -= count
    raise ValueError


def segments(one, other):
    edges = {0}
    for pieces in (one, other):
        at = 0
        for _, _, count in pieces:
            at += count
            edges.add(at)
    edges = sorted(edges)
    return [(a, b - a) for a, b in zip(edges[:-1], edges[1:])]


def reorder_kernel(meta, inv, out, *, step):
    for level in range(LEVELS):
        shape = inv.shape[1:]
        row_id = lax.broadcasted_iota(jnp.int32, shape, 0)
        col_id = lax.broadcasted_iota(jnp.int32, shape, 1)
        source = jnp.bitwise_xor(col_id, meta[step * (level + 1) - 1])
        swap = jnp.where(row_id == source, 1.0, 0.0).astype(BF16)
        out[level] = jnp.dot(inv[level], swap, preferred_element_type=F32).astype(BF16)


def eliminate(meta, inv, panel, merged, top, pairs, outs, level, blocks):
    width = blocks * BLOCK
    base = level * meta.shape[0] // LEVELS

    def at(j):
        return pl.ds(pl.multiple_of(j * BLOCK, BLOCK), BLOCK)

    def read(pieces, start, rows, j):
        ref, low = cut(pieces, start, rows)
        return ref[pl.ds(low, rows), at(j)].astype(F32)

    def order(j):
        return meta[base + j]

    jobs = [job for _, dest in outs for job in dest]
    if top is not None:
        a, b = top
        half = sum(count for _, _, count in a)
        kept = [(start, start + rows) for source, start, rows in jobs if source == "top"]

        def keep(value, first, rows, j):
            for low, high in kept:
                low, high = max(low, first), min(high, first + rows)
                if low < high:
                    merged[pl.ds(low, high - low), at(j)] = value[low - first : high - first]

        def merge_block(j, carry):
            other = order(j)
            keep_a = meta[base + blocks + j].astype(F32)
            keep_b = meta[base + 2 * blocks + j].astype(F32)
            for start, rows in segments(a, b):
                from_a = read(a, start, rows, j) + read(b, start, rows, other)
                from_b = read(b, start, rows, j) + read(a, start, rows, other)
                keep(from_a, start, rows, j)
                keep(from_b, half + start, rows, j)
                panel[pl.ds(start, rows), at(j)] = (from_a * keep_a).astype(BF16)
                panel[pl.ds(half + start, rows), at(j)] = (from_b * keep_b).astype(BF16)
            return carry

        lax.fori_loop(0, blocks, merge_block, 0, unroll=True)

    def columns(job, j):
        source, start, rows = job
        if source == "top":
            return merged[pl.ds(start, rows), at(j)]
        a, b = pairs[source]
        return read(a, start, rows, j) + read(b, start, rows, order(j))

    pivots = [meta[base + 3 * blocks + i] for i in range(inv.shape[1] // BLOCK)]
    coupling = jnp.concatenate(
        [jnp.concatenate([columns(job, p) for p in pivots], axis=1).astype(BF16) for job in jobs],
        axis=0,
    )
    weights = jnp.dot(coupling, inv[level], preferred_element_type=F32).astype(BF16)

    def finish_tile(t, carry):
        lanes = pl.ds(pl.multiple_of(t * TILE, TILE), TILE)
        update = jnp.dot(weights, panel[:, lanes], preferred_element_type=F32)
        done = 0
        for out, dest in outs:
            put = 0
            for job in dest:
                rows = job[2]
                for i in range(TILE // BLOCK):
                    j = (TILE // BLOCK) * t + i
                    part = update[done : done + rows, i * BLOCK : (i + 1) * BLOCK]
                    out[pl.ds(put, rows), at(j)] = (columns(job, j) - part).astype(BF16)
                put += rows
                done += rows
        return carry

    lax.fori_loop(0, width // TILE, finish_tile, 0, unroll=True)


def level_kernel(meta, *refs, level, blocks, n_in, top, pairs, outs, n_hidden):
    ins, rest = refs[:n_in], refs[n_in + n_hidden :]
    out_refs, rest = rest[: len(outs)], rest[len(outs) :]

    def stack(spec):
        return [(ins[i], low, count) for i, low, count in spec]

    panel, merged = rest if top is not None else (ins[1], None)
    eliminate(
        meta,
        ins[0],
        panel,
        merged,
        None if top is None else tuple(stack(s) for s in top),
        [tuple(stack(s) for s in pair) for pair in pairs],
        list(zip(out_refs, outs)),
        level,
        blocks,
    )


def two_level_kernel(meta, inv, *refs, blocks, counts, first_outs, second_outs, pairs):
    n = len(counts)
    ours, theirs, near, near_x = refs[:n], refs[n : 2 * n], *refs[2 * n : 2 * n + 2]
    outs, panel, other_panel, merged, far, far_x = refs[2 * n + 2 : -5], *refs[-5:]
    stacks = tuple([(ref, 0, count) for ref, count in zip(group, counts)] for group in (ours, theirs))
    eliminate(meta, inv, other_panel, merged, stacks, [], list(zip((far, far_x), first_outs)), 0, blocks)
    held = ((near, far), (near_x, far_x))
    top = tuple([(ref, 0, ref.shape[0])] for ref in (near, far))
    stacked = [tuple([(ref, low, rows)] for ref in held[i]) for i, low, rows in pairs]
    eliminate(meta, inv, panel, merged, top, stacked, list(zip(outs, second_outs)), 1, blocks)


def run_level(level, meta, held, outs, pairs=(), top=None, keeps=False, part=None, cost=0):
    arrays = list(held)

    def spec(stack):
        named = []
        for x, low, rows in stack:
            found = [i for i, seen in enumerate(arrays) if seen is x]
            if not found:
                arrays.append(x)
            named.append((found[0] if found else len(arrays) - 1, low, rows))
        return tuple(named)

    top_spec = None if top is None else (spec(top[0]), spec(top[1]))
    pair_specs = tuple((spec(a), spec(b)) for a, b in pairs)
    n_in = len(arrays)
    width = arrays[-1].shape[1]
    size = held[0].shape[1]
    counts = [sum(job[2] for job in dest) for dest in outs]
    shapes = [jax.ShapeDtypeStruct((rows, width), BF16) for rows in counts]
    whole = pl.BlockSpec(memory_space=pltpu.VMEM)
    in_specs = [pl.BlockSpec(memory_space=pltpu.SMEM)] + [whole] * n_in
    out_specs = [whole] * len(shapes)
    aliases = {}
    hidden = []
    if part is not None:
        all_rows, block, old = part
        shapes[0] = jax.ShapeDtypeStruct((all_rows, width), BF16)
        out_specs[0] = pl.BlockSpec((counts[0], width), lambda i: (block, 0))
        if old is not None:
            hidden = [old]
            in_specs.append(pl.BlockSpec(memory_space=pl.ANY))
            aliases = {1 + n_in: 0}
    scratch = []
    if top is not None:
        if keeps:
            shapes.append(jax.ShapeDtypeStruct((size, width), BF16))
            out_specs.append(whole)
        else:
            scratch.append(pltpu.VMEM((size, width), BF16))
        scratch.append(pltpu.VMEM((size, width), F32))
    kernel = functools.partial(
        level_kernel,
        level=level,
        blocks=width // BLOCK,
        n_in=n_in,
        top=top_spec,
        pairs=pair_specs,
        outs=tuple(tuple(dest) for dest in outs),
        n_hidden=len(hidden),
    )
    return pl.pallas_call(
        kernel,
        grid=(1,) if part is not None else (),
        out_shape=shapes,
        in_specs=in_specs,
        out_specs=out_specs,
        scratch_shapes=scratch,
        input_output_aliases=aliases,
        compiler_params=pltpu.CompilerParams(vmem_limit_bytes=30 * 2**20),
        cost_estimate=pl.CostEstimate(flops=cost, bytes_accessed=0, transcendentals=0),
        name=f"level{level}_rows{sum(counts)}",
    )(meta, *arrays, *hidden)


def run_two_levels(meta, inv, ours, theirs, near, near_x, first_outs, second_outs, pairs):
    width, size = near.shape[1], inv.shape[1]
    rows = [sum(job[2] for job in dest) for dest in second_outs] + [size]
    vmem = pl.BlockSpec(memory_space=pltpu.VMEM)
    kernel = functools.partial(
        two_level_kernel,
        blocks=width // BLOCK,
        counts=tuple(x.shape[0] for x in ours),
        first_outs=first_outs,
        second_outs=second_outs,
        pairs=pairs,
    )
    return pl.pallas_call(
        kernel,
        out_shape=[jax.ShapeDtypeStruct((n, width), BF16) for n in rows],
        in_specs=[pl.BlockSpec(memory_space=pltpu.SMEM)] + [vmem] * (3 + 2 * len(ours)),
        out_specs=[vmem] * len(rows),
        scratch_shapes=[
            pltpu.VMEM((size, width), BF16),
            pltpu.VMEM((size, width), F32),
            pltpu.VMEM(near.shape, BF16),
            pltpu.VMEM(near_x.shape, BF16),
        ],
        compiler_params=pltpu.CompilerParams(vmem_limit_bytes=30 * 2**20),
        cost_estimate=pl.CostEstimate(flops=0, bytes_accessed=0, transcendentals=0),
        name="level0_level1",
    )(meta, inv, *ours, *theirs, near, near_x)


def reorder(meta, pivot_inverse):
    step = meta.shape[0] // LEVELS
    return pl.pallas_call(
        functools.partial(reorder_kernel, step=step),
        out_shape=jax.ShapeDtypeStruct(pivot_inverse.shape, BF16),
        in_specs=[pl.BlockSpec(memory_space=pltpu.SMEM), pl.BlockSpec(memory_space=pltpu.VMEM)],
        out_specs=pl.BlockSpec(memory_space=pltpu.VMEM),
        compiler_params=pltpu.CompilerParams(vmem_limit_bytes=30 * 2**20),
        cost_estimate=pl.CostEstimate(flops=0, bytes_accessed=0, transcendentals=0),
        name="reorder",
    )(meta, pivot_inverse)


def make_meta(size, block_pattern, column_order, pivot_blocks):
    blocks = column_order.shape[1]
    rank = jnp.int32(0)
    meta = []
    for level in range(LEVELS):
        bit = my_bit(level)
        rank = rank + bit * (1 << level)
        shift = rank * (size >> (level + 1))
        meta += [
            column_order[level],
            jnp.where(bit == 0, block_pattern[level, 0], block_pattern[level, 1]),
            jnp.where(bit == 0, block_pattern[level, 1], block_pattern[level, 0]),
            pivot_blocks[level],
            jnp.zeros((blocks,), jnp.int32) + shift,
        ]
    return jnp.concatenate(meta)


def on_device(schur_slab, pivot_inverse, block_pattern, column_order, pivot_blocks):
    all_rows = schur_slab.shape[0]
    size = pivot_inverse.shape[1]
    half, quarter, eighth, share = size // 2, size // 4, size // 8, size // 16
    meta = make_meta(size, block_pattern, column_order, pivot_blocks)

    def rows_of(x):
        return [(x, 0, x.shape[0])]

    def chunk(level, panel, own, other, **more):
        (out,) = run_level(
            level, meta, (inv, panel), [[(0, 0, own.shape[0])]], pairs=[(rows_of(own), rows_of(other))], **more
        )
        return out

    cut_1 = quarter + share
    cut_2 = half + quarter
    begin_1 = schur_slab[:cut_1]
    first_z1 = trade(begin_1, 1)
    slab, begin_1 = after(schur_slab, begin_1)
    begin_2, begin_3, rest_2 = slab[cut_1:half], slab[half:cut_2], slab[cut_2:]
    begin_1, begin_3, rest_2 = after(begin_1, begin_3, rest_2)
    begin_y1, begin_y2, begin_y3 = (trade(x, 0) for x in (begin_1, begin_2, begin_3))
    inv = reorder(meta, pivot_inverse)

    first_yz1 = trade(first_z1, 0)
    first_2, first_z1 = after(begin_2, first_z1)
    first_z2 = trade(first_2, 1)
    rest_2, begin_y3 = after(rest_2, begin_y3)

    tops = [("top", 0, quarter), ("top", half, quarter)]
    begun = ((begin_1, begin_2, begin_3), (begin_y1, begin_y2, begin_y3))
    near, near_x, after_1, panel_0 = run_level(
        0,
        meta,
        (inv,),
        [tops, [("top", quarter, quarter)], [(0, 0, quarter)]],
        top=tuple(rows_of(x) + rows_of(y) for x, y, _ in begun),
        pairs=[tuple(rows_of(x) for *_, x in begun)],
        keeps=True,
    )
    first_z2, after_1 = after(first_z2, after_1)
    after_z1 = trade(after_1, 1)
    first_z2, first_yz1 = after(first_z2, first_yz1)
    first_yz2 = trade(first_z2, 0)
    rest_2, first_yz2 = after(rest_2, first_yz2)
    rest_y2 = trade(rest_2, 0)

    e, y, z, yz = (("top", low, eighth) for low in range(0, size, quarter))
    jobs = [[e, (*y[:2], share)], [("top", quarter + share, share), z], [yz, (0, 0, share)]]
    jobs.append([(0, share, share), (1, 0, quarter)])
    *head, next_0, panel_1 = run_two_levels(
        meta,
        inv,
        (first_z1, first_z2),
        (first_yz1, first_yz2),
        near,
        near_x,
        (tuple(tops), (("top", quarter, quarter),)),
        jobs,
        ((0, eighth, eighth), (1, 0, quarter)),
    )
    head_c = [trade(x, 2) for x in head]

    tops = [("top", low, share) for low in range(0, size, eighth)]
    lead, others, panel_2 = run_level(
        2,
        meta,
        (inv,),
        [[tops[0], ("top", share, share), (0, 0, share)], tops[1:]],
        top=tuple(
            rows_of(group[0]) + rows_of(group[1]) + [(group[2], 0, eighth)] for group in (head, head_c)
        ),
        pairs=[tuple([(group[2], eighth, share)] for group in (head, head_c))],
        keeps=True,
    )
    lead_w = trade(lead, 3)
    after_z1, rest_y2, lead = after(after_z1, rest_y2, lead)
    next_1 = run_level(
        1,
        meta,
        (inv, panel_1),
        [[(0, 0, eighth)], [(0, eighth, eighth)]],
        pairs=[(rows_of(after_1), rows_of(after_z1))],
        cost=10**10,
    )
    next_1 = [next_0, *next_1]
    next_c1 = [trade(x, 2) for x in next_1]
    after_2 = chunk(0, panel_0, rest_2, rest_y2, cost=0)
    after_z2 = trade(after_2, 1)
    next_c1[0], after_2 = after(next_c1[0], after_2)
    (last_1,) = run_level(
        2,
        meta,
        (inv, panel_2),
        [[(i, 0, x.shape[0]) for i, x in enumerate(next_1)]],
        pairs=[(rows_of(x), rows_of(y)) for x, y in zip(next_1, next_c1)],
    )
    last_w1 = trade(last_1, 3)
    first_w = lead_w[:share]
    first_wy = trade(first_w, 0)
    first_wz = trade(first_w, 1)
    after_z2, first_wy = after(after_z2, first_wy)
    first_wz, after_z2 = after(first_wz, after_z2)
    first_wyz = trade(first_wz, 0)
    firsts_w = [first_w, first_wy, first_wz, first_wyz]
    firsts_w += [trade(x, 2) for x in firsts_w]
    next_2 = chunk(1, panel_1, after_2, after_z2, cost=3 * 10**9)
    last_2 = chunk(2, panel_2, next_2, trade(next_2, 2))
    last_w2 = trade(last_2, 3)
    tops = [(lead, 0, share)] + [(others, share * i, share) for i in range(7)]
    tops_other = [(x, 0, share) for x in firsts_w]
    out, panel_3 = run_level(
        3,
        meta,
        (inv,),
        [[("top", 0, share), (0, 0, eighth), (1, 0, last_1.shape[0])]],
        top=(tops, tops_other),
        pairs=[([(lead, share, eighth)], [(lead_w, share, eighth)]), (rows_of(last_1), rows_of(last_w1))],
        keeps=True,
        part=(all_rows, 0, None),
        cost=5 * 10**10,
    )
    return chunk(3, panel_3, last_2, last_w2, part=(all_rows, all_rows // quarter - 1, out))


def solution(mesh):
    return jax.shard_map(
        on_device,
        mesh=mesh,
        in_specs=(P(("tx", "ty"), None), P(), P(), P(), P()),
        out_specs=P(("tx", "ty"), None),
        check_vma=False,
    )
```

```python
import functools

import jax
import jax.numpy as jnp
from jax import lax
from jax.experimental import pallas as pl
from jax.experimental.pallas import tpu as pltpu
from jax.sharding import PartitionSpec as P

BLOCK = 128
LEVELS = 4
TILE = 2 * BLOCK
F32 = jnp.float32
BF16 = jnp.bfloat16


def stride_bit(axis, level):
    return lax.axis_size(axis).bit_length() - 2 - level // 2


def level_axis(level):
    return "tx" if level % 2 == 0 else "ty"


def trade(block, level):
    axis = level_axis(level)
    flip = 1 << stride_bit(axis, level)
    return lax.ppermute(block, axis, [(i, i ^ flip) for i in range(lax.axis_size(axis))])


def my_bit(level):
    axis = level_axis(level)
    place = lax.axis_index(axis).astype(jnp.int32)
    return jnp.bitwise_and(jnp.right_shift(place, stride_bit(axis, level)), 1)


def after(x, *others):
    return lax.optimization_barrier((x, *others))


def cut(pieces, start, rows):
    for ref, low, count in pieces:
        if start < count:
            assert start + rows <= count
            return ref, low + start
        start -= count
    raise ValueError


def segments(one, other):
    edges = {0}
    for pieces in (one, other):
        at = 0
        for _, _, count in pieces:
            at += count
            edges.add(at)
    edges = sorted(edges)
    return [(a, b - a) for a, b in zip(edges[:-1], edges[1:])]


def reorder_kernel(meta, inv, out, *, step):
    for level in range(LEVELS):
        shape = inv.shape[1:]
        row_id = lax.broadcasted_iota(jnp.int32, shape, 0)
        col_id = lax.broadcasted_iota(jnp.int32, shape, 1)
        source = jnp.bitwise_xor(col_id, meta[step * (level + 1) - 1])
        swap = jnp.where(row_id == source, 1.0, 0.0).astype(BF16)
        out[level] = jnp.dot(inv[level], swap, preferred_element_type=F32).astype(BF16)


def eliminate(meta, inv, panel, merged, top, pairs, outs, level, blocks):
    width = blocks * BLOCK
    base = level * meta.shape[0] // LEVELS

    def at(j):
        return pl.ds(pl.multiple_of(j * BLOCK, BLOCK), BLOCK)

    def read(pieces, start, rows, j):
        ref, low = cut(pieces, start, rows)
        return ref[pl.ds(low, rows), at(j)].astype(F32)

    def order(j):
        return meta[base + j]

    jobs = [job for _, dest in outs for job in dest]
    if top is not None:
        a, b = top
        half = sum(count for _, _, count in a)
        kept = [(start, start + rows) for source, start, rows in jobs if source == "top"]

        def keep(value, first, rows, j):
            for low, high in kept:
                low, high = max(low, first), min(high, first + rows)
                if low < high:
                    merged[pl.ds(low, high - low), at(j)] = value[low - first : high - first]

        def merge_block(j, carry):
            other = order(j)
            keep_a = meta[base + blocks + j].astype(F32)
            keep_b = meta[base + 2 * blocks + j].astype(F32)
            for start, rows in segments(a, b):
                from_a = read(a, start, rows, j) + read(b, start, rows, other)
                from_b = read(b, start, rows, j) + read(a, start, rows, other)
                keep(from_a, start, rows, j)
                keep(from_b, half + start, rows, j)
                panel[pl.ds(start, rows), at(j)] = (from_a * keep_a).astype(BF16)
                panel[pl.ds(half + start, rows), at(j)] = (from_b * keep_b).astype(BF16)
            return carry

        lax.fori_loop(0, blocks, merge_block, 0, unroll=True)

    def columns(job, j):
        source, start, rows = job
        if source == "top":
            return merged[pl.ds(start, rows), at(j)]
        a, b = pairs[source]
        return read(a, start, rows, j) + read(b, start, rows, order(j))

    pivots = [meta[base + 3 * blocks + i] for i in range(inv.shape[1] // BLOCK)]
    coupling = jnp.concatenate(
        [jnp.concatenate([columns(job, p) for p in pivots], axis=1).astype(BF16) for job in jobs],
        axis=0,
    )
    weights = jnp.dot(coupling, inv[level], preferred_element_type=F32).astype(BF16)

    def finish_tile(t, carry):
        lanes = pl.ds(pl.multiple_of(t * TILE, TILE), TILE)
        update = jnp.dot(weights, panel[:, lanes], preferred_element_type=F32)
        done = 0
        for out, dest in outs:
            put = 0
            for job in dest:
                rows = job[2]
                for i in range(TILE // BLOCK):
                    j = (TILE // BLOCK) * t + i
                    part = update[done : done + rows, i * BLOCK : (i + 1) * BLOCK]
                    out[pl.ds(put, rows), at(j)] = (columns(job, j) - part).astype(BF16)
                put += rows
                done += rows
        return carry

    lax.fori_loop(0, width // TILE, finish_tile, 0, unroll=True)


def level_kernel(meta, *refs, level, blocks, n_in, top, pairs, outs, n_hidden):
    ins, rest = refs[:n_in], refs[n_in + n_hidden :]
    out_refs, rest = rest[: len(outs)], rest[len(outs) :]

    def stack(spec):
        return [(ins[i], low, count) for i, low, count in spec]

    panel, merged = rest if top is not None else (ins[1], None)
    eliminate(
        meta,
        ins[0],
        panel,
        merged,
        None if top is None else tuple(stack(s) for s in top),
        [tuple(stack(s) for s in pair) for pair in pairs],
        list(zip(out_refs, outs)),
        level,
        blocks,
    )


def two_level_kernel(meta, inv, *refs, blocks, counts, first_outs, second_outs, pairs):
    n = len(counts)
    ours, theirs, near, near_x = refs[:n], refs[n : 2 * n], *refs[2 * n : 2 * n + 2]
    outs, panel, other_panel, merged, far, far_x = refs[2 * n + 2 : -5], *refs[-5:]
    stacks = tuple([(ref, 0, count) for ref, count in zip(group, counts)] for group in (ours, theirs))
    eliminate(meta, inv, other_panel, merged, stacks, [], list(zip((far, far_x), first_outs)), 0, blocks)
    held = ((near, far), (near_x, far_x))
    top = tuple([(ref, 0, ref.shape[0])] for ref in (near, far))
    stacked = [tuple([(ref, low, rows)] for ref in held[i]) for i, low, rows in pairs]
    eliminate(meta, inv, panel, merged, top, stacked, list(zip(outs, second_outs)), 1, blocks)


def run_level(level, meta, held, outs, pairs=(), top=None, keeps=False, part=None, cost=0):
    arrays = list(held)

    def spec(stack):
        named = []
        for x, low, rows in stack:
            found = [i for i, seen in enumerate(arrays) if seen is x]
            if not found:
                arrays.append(x)
            named.append((found[0] if found else len(arrays) - 1, low, rows))
        return tuple(named)

    top_spec = None if top is None else (spec(top[0]), spec(top[1]))
    pair_specs = tuple((spec(a), spec(b)) for a, b in pairs)
    n_in = len(arrays)
    width = arrays[-1].shape[1]
    size = held[0].shape[1]
    counts = [sum(job[2] for job in dest) for dest in outs]
    shapes = [jax.ShapeDtypeStruct((rows, width), BF16) for rows in counts]
    whole = pl.BlockSpec(memory_space=pltpu.VMEM)
    in_specs = [pl.BlockSpec(memory_space=pltpu.SMEM)] + [whole] * n_in
    out_specs = [whole] * len(shapes)
    aliases = {}
    hidden = []
    if part is not None:
        all_rows, block, old = part
        shapes[0] = jax.ShapeDtypeStruct((all_rows, width), BF16)
        out_specs[0] = pl.BlockSpec((counts[0], width), lambda i: (block, 0))
        if old is not None:
            hidden = [old]
            in_specs.append(pl.BlockSpec(memory_space=pl.ANY))
            aliases = {1 + n_in: 0}
    scratch = []
    if top is not None:
        if keeps:
            shapes.append(jax.ShapeDtypeStruct((size, width), BF16))
            out_specs.append(whole)
        else:
            scratch.append(pltpu.VMEM((size, width), BF16))
        scratch.append(pltpu.VMEM((size, width), F32))
    kernel = functools.partial(
        level_kernel,
        level=level,
        blocks=width // BLOCK,
        n_in=n_in,
        top=top_spec,
        pairs=pair_specs,
        outs=tuple(tuple(dest) for dest in outs),
        n_hidden=len(hidden),
    )
    return pl.pallas_call(
        kernel,
        grid=(1,) if part is not None else (),
        out_shape=shapes,
        in_specs=in_specs,
        out_specs=out_specs,
        scratch_shapes=scratch,
        input_output_aliases=aliases,
        compiler_params=pltpu.CompilerParams(vmem_limit_bytes=30 * 2**20),
        cost_estimate=pl.CostEstimate(flops=cost, bytes_accessed=0, transcendentals=0),
        name=f"level{level}_rows{sum(counts)}",
    )(meta, *arrays, *hidden)


def run_two_levels(meta, inv, ours, theirs, near, near_x, first_outs, second_outs, pairs):
    width, size = near.shape[1], inv.shape[1]
    rows = [sum(job[2] for job in dest) for dest in second_outs] + [size]
    vmem = pl.BlockSpec(memory_space=pltpu.VMEM)
    kernel = functools.partial(
        two_level_kernel,
        blocks=width // BLOCK,
        counts=tuple(x.shape[0] for x in ours),
        first_outs=first_outs,
        second_outs=second_outs,
        pairs=pairs,
    )
    return pl.pallas_call(
        kernel,
        out_shape=[jax.ShapeDtypeStruct((n, width), BF16) for n in rows],
        in_specs=[pl.BlockSpec(memory_space=pltpu.SMEM)] + [vmem] * (3 + 2 * len(ours)),
        out_specs=[vmem] * len(rows),
        scratch_shapes=[
            pltpu.VMEM((size, width), BF16),
            pltpu.VMEM((size, width), F32),
            pltpu.VMEM(near.shape, BF16),
            pltpu.VMEM(near_x.shape, BF16),
        ],
        compiler_params=pltpu.CompilerParams(vmem_limit_bytes=30 * 2**20),
        cost_estimate=pl.CostEstimate(flops=0, bytes_accessed=0, transcendentals=0),
        name="level0_level1",
    )(meta, inv, *ours, *theirs, near, near_x)


def reorder(meta, pivot_inverse, cost=0):
    step = meta.shape[0] // LEVELS
    return pl.pallas_call(
        functools.partial(reorder_kernel, step=step),
        out_shape=jax.ShapeDtypeStruct(pivot_inverse.shape, BF16),
        in_specs=[pl.BlockSpec(memory_space=pltpu.SMEM), pl.BlockSpec(memory_space=pltpu.VMEM)],
        out_specs=pl.BlockSpec(memory_space=pltpu.VMEM),
        compiler_params=pltpu.CompilerParams(vmem_limit_bytes=30 * 2**20),
        cost_estimate=pl.CostEstimate(flops=cost, bytes_accessed=0, transcendentals=0),
        name="reorder",
    )(meta, pivot_inverse)


def make_meta(size, block_pattern, column_order, pivot_blocks):
    blocks = column_order.shape[1]
    rank = jnp.int32(0)
    meta = []
    for level in range(LEVELS):
        bit = my_bit(level)
        rank = rank + bit * (1 << level)
        shift = rank * (size >> (level + 1))
        meta += [
            column_order[level],
            jnp.where(bit == 0, block_pattern[level, 0], block_pattern[level, 1]),
            jnp.where(bit == 0, block_pattern[level, 1], block_pattern[level, 0]),
            pivot_blocks[level],
            jnp.zeros((blocks,), jnp.int32) + shift,
        ]
    return jnp.concatenate(meta)


def on_device(schur_slab, pivot_inverse, block_pattern, column_order, pivot_blocks):
    all_rows = schur_slab.shape[0]
    size = pivot_inverse.shape[1]
    half, quarter, eighth, share = size // 2, size // 4, size // 8, size // 16
    meta = make_meta(size, block_pattern, column_order, pivot_blocks)

    def rows_of(x):
        return [(x, 0, x.shape[0])]

    def chunk(level, panel, own, other, **more):
        (out,) = run_level(
            level, meta, (inv, panel), [[(0, 0, own.shape[0])]], pairs=[(rows_of(own), rows_of(other))], **more
        )
        return out

    cut_1 = quarter + share
    cut_2 = half + quarter
    begin_1 = schur_slab[:cut_1]
    first_z1 = trade(begin_1, 1)
    begin_y1 = trade(begin_1, 0)
    slab, begin_1 = after(schur_slab, begin_1)
    begin_2, begin_3, rest_2 = slab[cut_1:half], slab[half:cut_2], slab[cut_2:]
    begin_y2, begin_y3 = trade(begin_2, 0), trade(begin_3, 0)
    pivot_inverse, first_z1 = after(pivot_inverse, first_z1)
    inv = reorder(meta, pivot_inverse, cost=10**9)

    first_yz1 = trade(first_z1, 0)
    first_2, first_z1 = after(begin_2, first_z1)
    first_z2 = trade(first_2, 1)
    rest_2, begin_y3 = after(rest_2, begin_y3)

    tops = [("top", 0, quarter), ("top", half, quarter)]
    begun = ((begin_1, begin_2, begin_3), (begin_y1, begin_y2, begin_y3))
    near, near_x, after_1, panel_0 = run_level(
        0,
        meta,
        (inv,),
        [tops, [("top", quarter, quarter)], [(0, 0, quarter)]],
        top=tuple(rows_of(x) + rows_of(y) for x, y, _ in begun),
        pairs=[tuple(rows_of(x) for *_, x in begun)],
        keeps=True,
    )
    first_z2, after_1 = after(first_z2, after_1)
    after_z1 = trade(after_1, 1)
    first_z2, first_yz1 = after(first_z2, first_yz1)
    first_yz2 = trade(first_z2, 0)
    rest_2, first_yz2 = after(rest_2, first_yz2)
    rest_y2 = trade(rest_2, 0)

    e, y, z, yz = (("top", low, eighth) for low in range(0, size, quarter))
    jobs = [[e, (*y[:2], share)], [("top", quarter + share, share), z], [yz]]
    jobs.append([(0, 0, eighth), (1, 0, quarter)])
    *head, next_0, panel_1 = run_two_levels(
        meta,
        inv,
        (first_z1, first_z2),
        (first_yz1, first_yz2),
        near,
        near_x,
        (tuple(tops), (("top", quarter, quarter),)),
        jobs,
        ((0, eighth, eighth), (1, 0, quarter)),
    )
    head_c = [trade(x, 2) for x in head]

    tops = [("top", low, share) for low in range(0, size, eighth)]
    lead, others, panel_2 = run_level(
        2,
        meta,
        (inv,),
        [[tops[0], tops[2], ("top", share, share)], [tops[i] for i in (1, 3, 4, 5, 6, 7)]],
        top=tuple(sum((rows_of(x) for x in group), []) for group in (head, head_c)),
        keeps=True,
    )
    lead_w = trade(lead, 3)
    after_z1, rest_y2, lead = after(after_z1, rest_y2, lead)
    next_1 = run_level(
        1,
        meta,
        (inv, panel_1),
        [[(0, 0, eighth)], [(0, eighth, eighth)]],
        pairs=[(rows_of(after_1), rows_of(after_z1))],
        cost=10**10,
    )
    next_1 = [next_0, *next_1]
    next_c1 = [trade(x, 2) for x in next_1]
    after_2 = chunk(0, panel_0, rest_2, rest_y2, cost=0)
    after_z2 = trade(after_2, 1)
    next_c1[0], after_2 = after(next_c1[0], after_2)
    (last_1,) = run_level(
        2,
        meta,
        (inv, panel_2),
        [[(i, 0, x.shape[0]) for i, x in enumerate(next_1)]],
        pairs=[(rows_of(x), rows_of(y)) for x, y in zip(next_1, next_c1)],
    )
    last_w1 = trade(last_1, 3)
    tops_w = lead_w[:eighth]
    tops_wc = trade(tops_w, 2)
    tops_wy = trade(tops_w, 0)
    after_z2, tops_wy = after(after_z2, tops_wy)
    tops_wyc = trade(tops_wy, 2)
    next_2 = chunk(1, panel_1, after_2, after_z2, cost=5 * 10**9)
    last_2 = chunk(2, panel_2, next_2, trade(next_2, 2))
    last_w2 = trade(last_2, 3)
    more = lead.shape[0] - eighth
    tops = [(lead, 0, share), (others, 0, share), (lead, share, share)]
    tops += [(others, share * i, share) for i in range(1, 6)]
    tops_other = [(x, low, share) for low in (0, share) for x in (tops_w, tops_wy)]
    tops_other += [(x, low, share) for low in (0, share) for x in (tops_wc, tops_wyc)]
    out, panel_3 = run_level(
        3,
        meta,
        (inv,),
        [[("top", 0, share), (0, 0, more), (1, 0, last_1.shape[0])]],
        top=(tops, tops_other),
        pairs=[([(lead, eighth, more)], [(lead_w, eighth, more)]), (rows_of(last_1), rows_of(last_w1))],
        keeps=True,
        part=(all_rows, 0, None),
        cost=5 * 10**10,
    )
    return chunk(3, panel_3, last_2, last_w2, part=(all_rows, all_rows // quarter - 1, out))


def solution(mesh):
    return jax.shard_map(
        on_device,
        mesh=mesh,
        in_specs=(P(("tx", "ty"), None), P(), P(), P(), P()),
        out_specs=P(("tx", "ty"), None),
        check_vma=False,
    )
```

```python
import functools

import jax
import jax.numpy as jnp
from jax import lax
from jax.experimental import pallas as pl
from jax.experimental.pallas import tpu as pltpu
from jax.sharding import PartitionSpec as P

BLOCK = 128
LEVELS = 4
TILE = 2 * BLOCK
F32 = jnp.float32
BF16 = jnp.bfloat16


def stride_bit(axis, level):
    return lax.axis_size(axis).bit_length() - 2 - level // 2


def level_axis(level):
    return "tx" if level % 2 == 0 else "ty"


def trade(block, level):
    axis = level_axis(level)
    flip = 1 << stride_bit(axis, level)
    return lax.ppermute(block, axis, [(i, i ^ flip) for i in range(lax.axis_size(axis))])


def my_bit(level):
    axis = level_axis(level)
    place = lax.axis_index(axis).astype(jnp.int32)
    return jnp.bitwise_and(jnp.right_shift(place, stride_bit(axis, level)), 1)


def after(x, *others):
    return lax.optimization_barrier((x, *others))


def cut(pieces, start, rows):
    for ref, low, count in pieces:
        if start < count:
            assert start + rows <= count
            return ref, low + start
        start -= count
    raise ValueError


def segments(one, other):
    edges = {0}
    for pieces in (one, other):
        at = 0
        for _, _, count in pieces:
            at += count
            edges.add(at)
    edges = sorted(edges)
    return [(a, b - a) for a, b in zip(edges[:-1], edges[1:])]


def reorder_kernel(meta, inv, out, *, step):
    for level in range(LEVELS):
        shape = inv.shape[1:]
        row_id = lax.broadcasted_iota(jnp.int32, shape, 0)
        col_id = lax.broadcasted_iota(jnp.int32, shape, 1)
        source = jnp.bitwise_xor(col_id, meta[step * (level + 1) - 1])
        swap = jnp.where(row_id == source, 1.0, 0.0).astype(BF16)
        out[level] = jnp.dot(inv[level], swap, preferred_element_type=F32).astype(BF16)


def eliminate(meta, inv, panel, merged, top, pairs, outs, level, blocks):
    width = blocks * BLOCK
    base = level * meta.shape[0] // LEVELS

    def at(j):
        return pl.ds(pl.multiple_of(j * BLOCK, BLOCK), BLOCK)

    def read(pieces, start, rows, j):
        ref, low = cut(pieces, start, rows)
        return ref[pl.ds(low, rows), at(j)].astype(F32)

    def order(j):
        return meta[base + j]

    jobs = [job for _, dest in outs for job in dest]
    if top is not None:
        a, b = top
        half = sum(count for _, _, count in a)
        kept = [(start, start + rows) for source, start, rows in jobs if source == "top"]

        def keep(value, first, rows, j):
            for low, high in kept:
                low, high = max(low, first), min(high, first + rows)
                if low < high:
                    merged[pl.ds(low, high - low), at(j)] = value[low - first : high - first]

        def merge_block(j, carry):
            other = order(j)
            keep_a = meta[base + blocks + j].astype(F32)
            keep_b = meta[base + 2 * blocks + j].astype(F32)
            for start, rows in segments(a, b):
                from_a = read(a, start, rows, j) + read(b, start, rows, other)
                from_b = read(b, start, rows, j) + read(a, start, rows, other)
                keep(from_a, start, rows, j)
                keep(from_b, half + start, rows, j)
                panel[pl.ds(start, rows), at(j)] = (from_a * keep_a).astype(BF16)
                panel[pl.ds(half + start, rows), at(j)] = (from_b * keep_b).astype(BF16)
            return carry

        lax.fori_loop(0, blocks, merge_block, 0, unroll=True)

    def columns(job, j):
        source, start, rows = job
        if source == "top":
            return merged[pl.ds(start, rows), at(j)]
        a, b = pairs[source]
        return read(a, start, rows, j) + read(b, start, rows, order(j))

    pivots = [meta[base + 3 * blocks + i] for i in range(inv.shape[1] // BLOCK)]
    coupling = jnp.concatenate(
        [jnp.concatenate([columns(job, p) for p in pivots], axis=1).astype(BF16) for job in jobs],
        axis=0,
    )
    weights = jnp.dot(coupling, inv[level], preferred_element_type=F32).astype(BF16)

    def finish_tile(t, carry):
        lanes = pl.ds(pl.multiple_of(t * TILE, TILE), TILE)
        update = jnp.dot(weights, panel[:, lanes], preferred_element_type=F32)
        done = 0
        for out, dest in outs:
            put = 0
            for job in dest:
                rows = job[2]
                for i in range(TILE // BLOCK):
                    j = (TILE // BLOCK) * t + i
                    part = update[done : done + rows, i * BLOCK : (i + 1) * BLOCK]
                    out[pl.ds(put, rows), at(j)] = (columns(job, j) - part).astype(BF16)
                put += rows
                done += rows
        return carry

    lax.fori_loop(0, width // TILE, finish_tile, 0, unroll=True)


def level_kernel(meta, *refs, level, blocks, n_in, top, pairs, outs, n_hidden):
    ins, rest = refs[:n_in], refs[n_in + n_hidden :]
    out_refs, rest = rest[: len(outs)], rest[len(outs) :]

    def stack(spec):
        return [(ins[i], low, count) for i, low, count in spec]

    panel, merged = rest if top is not None else (ins[1], None)
    eliminate(
        meta,
        ins[0],
        panel,
        merged,
        None if top is None else tuple(stack(s) for s in top),
        [tuple(stack(s) for s in pair) for pair in pairs],
        list(zip(out_refs, outs)),
        level,
        blocks,
    )


def two_level_kernel(meta, inv, *refs, blocks, counts, first_outs, second_outs, pairs):
    n = len(counts)
    ours, theirs, near, near_x = refs[:n], refs[n : 2 * n], *refs[2 * n : 2 * n + 2]
    outs, panel, other_panel, merged, far, far_x = refs[2 * n + 2 : -5], *refs[-5:]
    stacks = tuple([(ref, 0, count) for ref, count in zip(group, counts)] for group in (ours, theirs))
    eliminate(meta, inv, other_panel, merged, stacks, [], list(zip((far, far_x), first_outs)), 0, blocks)
    held = ((near, far), (near_x, far_x))
    top = tuple([(ref, 0, ref.shape[0])] for ref in (near, far))
    stacked = [tuple([(ref, low, rows)] for ref in held[i]) for i, low, rows in pairs]
    eliminate(meta, inv, panel, merged, top, stacked, list(zip(outs, second_outs)), 1, blocks)


def run_level(level, meta, held, outs, pairs=(), top=None, keeps=False, part=None, cost=0):
    arrays = list(held)

    def spec(stack):
        named = []
        for x, low, rows in stack:
            found = [i for i, seen in enumerate(arrays) if seen is x]
            if not found:
                arrays.append(x)
            named.append((found[0] if found else len(arrays) - 1, low, rows))
        return tuple(named)

    top_spec = None if top is None else (spec(top[0]), spec(top[1]))
    pair_specs = tuple((spec(a), spec(b)) for a, b in pairs)
    n_in = len(arrays)
    width = arrays[-1].shape[1]
    size = held[0].shape[1]
    counts = [sum(job[2] for job in dest) for dest in outs]
    shapes = [jax.ShapeDtypeStruct((rows, width), BF16) for rows in counts]
    whole = pl.BlockSpec(memory_space=pltpu.VMEM)
    in_specs = [pl.BlockSpec(memory_space=pltpu.SMEM)] + [whole] * n_in
    out_specs = [whole] * len(shapes)
    aliases = {}
    hidden = []
    if part is not None:
        all_rows, block, old = part
        shapes[0] = jax.ShapeDtypeStruct((all_rows, width), BF16)
        out_specs[0] = pl.BlockSpec((counts[0], width), lambda i: (block, 0))
        if old is not None:
            hidden = [old]
            in_specs.append(pl.BlockSpec(memory_space=pl.ANY))
            aliases = {1 + n_in: 0}
    scratch = []
    if top is not None:
        if keeps:
            shapes.append(jax.ShapeDtypeStruct((size, width), BF16))
            out_specs.append(whole)
        else:
            scratch.append(pltpu.VMEM((size, width), BF16))
        scratch.append(pltpu.VMEM((size, width), F32))
    kernel = functools.partial(
        level_kernel,
        level=level,
        blocks=width // BLOCK,
        n_in=n_in,
        top=top_spec,
        pairs=pair_specs,
        outs=tuple(tuple(dest) for dest in outs),
        n_hidden=len(hidden),
    )
    return pl.pallas_call(
        kernel,
        grid=(1,) if part is not None else (),
        out_shape=shapes,
        in_specs=in_specs,
        out_specs=out_specs,
        scratch_shapes=scratch,
        input_output_aliases=aliases,
        compiler_params=pltpu.CompilerParams(vmem_limit_bytes=30 * 2**20),
        cost_estimate=pl.CostEstimate(flops=cost, bytes_accessed=0, transcendentals=0),
        name=f"level{level}_rows{sum(counts)}",
    )(meta, *arrays, *hidden)


def run_two_levels(meta, inv, ours, theirs, near, near_x, first_outs, second_outs, pairs):
    width, size = near.shape[1], inv.shape[1]
    rows = [sum(job[2] for job in dest) for dest in second_outs] + [size]
    vmem = pl.BlockSpec(memory_space=pltpu.VMEM)
    kernel = functools.partial(
        two_level_kernel,
        blocks=width // BLOCK,
        counts=tuple(x.shape[0] for x in ours),
        first_outs=first_outs,
        second_outs=second_outs,
        pairs=pairs,
    )
    return pl.pallas_call(
        kernel,
        out_shape=[jax.ShapeDtypeStruct((n, width), BF16) for n in rows],
        in_specs=[pl.BlockSpec(memory_space=pltpu.SMEM)] + [vmem] * (3 + 2 * len(ours)),
        out_specs=[vmem] * len(rows),
        scratch_shapes=[
            pltpu.VMEM((size, width), BF16),
            pltpu.VMEM((size, width), F32),
            pltpu.VMEM(near.shape, BF16),
            pltpu.VMEM(near_x.shape, BF16),
        ],
        compiler_params=pltpu.CompilerParams(vmem_limit_bytes=30 * 2**20),
        cost_estimate=pl.CostEstimate(flops=0, bytes_accessed=0, transcendentals=0),
        name="level0_level1",
    )(meta, inv, *ours, *theirs, near, near_x)


def reorder(meta, pivot_inverse):
    step = meta.shape[0] // LEVELS
    return pl.pallas_call(
        functools.partial(reorder_kernel, step=step),
        out_shape=jax.ShapeDtypeStruct(pivot_inverse.shape, BF16),
        in_specs=[pl.BlockSpec(memory_space=pltpu.SMEM), pl.BlockSpec(memory_space=pltpu.VMEM)],
        out_specs=pl.BlockSpec(memory_space=pltpu.VMEM),
        compiler_params=pltpu.CompilerParams(vmem_limit_bytes=30 * 2**20),
        cost_estimate=pl.CostEstimate(flops=0, bytes_accessed=0, transcendentals=0),
        name="reorder",
    )(meta, pivot_inverse)


def make_meta(size, block_pattern, column_order, pivot_blocks):
    blocks = column_order.shape[1]
    rank = jnp.int32(0)
    meta = []
    for level in range(LEVELS):
        bit = my_bit(level)
        rank = rank + bit * (1 << level)
        shift = rank * (size >> (level + 1))
        meta += [
            column_order[level],
            jnp.where(bit == 0, block_pattern[level, 0], block_pattern[level, 1]),
            jnp.where(bit == 0, block_pattern[level, 1], block_pattern[level, 0]),
            pivot_blocks[level],
            jnp.zeros((blocks,), jnp.int32) + shift,
        ]
    return jnp.concatenate(meta)


def on_device(schur_slab, pivot_inverse, block_pattern, column_order, pivot_blocks):
    all_rows = schur_slab.shape[0]
    size = pivot_inverse.shape[1]
    half, quarter, eighth, share = size // 2, size // 4, size // 8, size // 16
    meta = make_meta(size, block_pattern, column_order, pivot_blocks)

    def rows_of(x):
        return [(x, 0, x.shape[0])]

    def chunk(level, panel, own, other, **more):
        (out,) = run_level(
            level, meta, (inv, panel), [[(0, 0, own.shape[0])]], pairs=[(rows_of(own), rows_of(other))], **more
        )
        return out

    cut_1 = quarter + share
    cut_2 = half + quarter
    begin_1 = schur_slab[:cut_1]
    first_z1 = trade(begin_1, 1)
    begin_y1 = trade(begin_1, 0)
    slab, begin_1 = after(schur_slab, begin_1)
    begin_2, begin_3, rest_2 = slab[cut_1:half], slab[half:cut_2], slab[cut_2:]
    begin_y2, begin_y3 = trade(begin_2, 0), trade(begin_3, 0)
    inv = reorder(meta, pivot_inverse)

    first_yz1 = trade(first_z1, 0)
    first_2, first_z1 = after(begin_2, first_z1)
    first_z2 = trade(first_2, 1)
    rest_2, begin_y3 = after(rest_2, begin_y3)

    tops = [("top", 0, quarter), ("top", half, quarter)]
    begun = ((begin_1, begin_2, begin_3), (begin_y1, begin_y2, begin_y3))
    near, near_x, after_1, panel_0 = run_level(
        0,
        meta,
        (inv,),
        [tops, [("top", quarter, quarter)], [(0, 0, quarter)]],
        top=tuple(rows_of(x) + rows_of(y) for x, y, _ in begun),
        pairs=[tuple(rows_of(x) for *_, x in begun)],
        keeps=True,
    )
    first_z2, after_1 = after(first_z2, after_1)
    after_z1 = trade(after_1, 1)
    first_z2, first_yz1 = after(first_z2, first_yz1)
    first_yz2 = trade(first_z2, 0)
    rest_2, first_yz2 = after(rest_2, first_yz2)
    rest_y2 = trade(rest_2, 0)

    e, y, z, yz = (("top", low, eighth) for low in range(0, size, quarter))
    jobs = [[e, (*y[:2], share)], [("top", quarter + share, share), z], [yz, (0, 0, share)]]
    jobs.append([(0, share, share), (1, 0, quarter)])
    *head, next_0, panel_1 = run_two_levels(
        meta,
        inv,
        (first_z1, first_z2),
        (first_yz1, first_yz2),
        near,
        near_x,
        (tuple(tops), (("top", quarter, quarter),)),
        jobs,
        ((0, eighth, eighth), (1, 0, quarter)),
    )
    head_c = [trade(x, 2) for x in head]

    tops = [("top", low, share) for low in range(0, size, eighth)]
    first, lead, others, panel_2 = run_level(
        2,
        meta,
        (inv,),
        [[tops[0]], [("top", share, share), (0, 0, share)], tops[1:]],
        top=tuple(
            rows_of(group[0]) + rows_of(group[1]) + [(group[2], 0, eighth)] for group in (head, head_c)
        ),
        pairs=[tuple([(group[2], eighth, share)] for group in (head, head_c))],
        keeps=True,
    )
    first_w, lead_w = trade(first, 3), trade(lead, 3)
    after_z1, rest_y2, lead = after(after_z1, rest_y2, lead)
    next_1 = run_level(
        1,
        meta,
        (inv, panel_1),
        [[(0, 0, eighth)], [(0, eighth, eighth)]],
        pairs=[(rows_of(after_1), rows_of(after_z1))],
        cost=10**10,
    )
    next_1 = [next_0, *next_1]
    next_c1 = [trade(x, 2) for x in next_1]
    after_2 = chunk(0, panel_0, rest_2, rest_y2, cost=0)
    after_z2 = trade(after_2, 1)
    next_c1[0], after_2 = after(next_c1[0], after_2)
    (last_1,) = run_level(
        2,
        meta,
        (inv, panel_2),
        [[(i, 0, x.shape[0]) for i, x in enumerate(next_1)]],
        pairs=[(rows_of(x), rows_of(y)) for x, y in zip(next_1, next_c1)],
    )
    last_w1 = trade(last_1, 3)
    first_wz = trade(first_w, 1)
    after_z2, first_wz, lead_w = after(after_z2, first_wz, lead_w)
    tops_w = jnp.concatenate([first_w, first_wz], axis=0)
    tops_wc = trade(tops_w, 2)
    tops_wy = trade(tops_w, 0)
    tops_wyc = trade(tops_wy, 2)
    next_2 = chunk(1, panel_1, after_2, after_z2, cost=5 * 10**9)
    last_2 = chunk(2, panel_2, next_2, trade(next_2, 2))
    last_w2 = trade(last_2, 3)
    tops = [(first, 0, share)] + [(others, share * i, share) for i in range(7)]
    tops_other = [(x, low, share) for low in (0, share) for x in (tops_w, tops_wy)]
    tops_other += [(x, low, share) for low in (0, share) for x in (tops_wc, tops_wyc)]
    out, panel_3 = run_level(
        3,
        meta,
        (inv,),
        [[("top", 0, share), (0, 0, eighth), (1, 0, last_1.shape[0])]],
        top=(tops, tops_other),
        pairs=[(rows_of(lead), rows_of(lead_w)), (rows_of(last_1), rows_of(last_w1))],
        keeps=True,
        part=(all_rows, 0, None),
        cost=5 * 10**10,
    )
    return chunk(3, panel_3, last_2, last_w2, part=(all_rows, all_rows // quarter - 1, out))


def solution(mesh):
    return jax.shard_map(
        on_device,
        mesh=mesh,
        in_specs=(P(("tx", "ty"), None), P(), P(), P(), P()),
        out_specs=P(("tx", "ty"), None),
        check_vma=False,
    )
```

```python
import functools

import jax
import jax.numpy as jnp
from jax import lax
from jax.experimental import pallas as pl
from jax.experimental.pallas import tpu as pltpu
from jax.sharding import PartitionSpec as P

BLOCK = 128
LEVELS = 4
TILE = 2 * BLOCK
F32 = jnp.float32
BF16 = jnp.bfloat16


def stride_bit(axis, level):
    return lax.axis_size(axis).bit_length() - 2 - level // 2


def level_axis(level):
    return "tx" if level % 2 == 0 else "ty"


def trade(block, level):
    axis = level_axis(level)
    flip = 1 << stride_bit(axis, level)
    return lax.ppermute(block, axis, [(i, i ^ flip) for i in range(lax.axis_size(axis))])


def my_bit(level):
    axis = level_axis(level)
    place = lax.axis_index(axis).astype(jnp.int32)
    return jnp.bitwise_and(jnp.right_shift(place, stride_bit(axis, level)), 1)


def after(x, *others):
    return lax.optimization_barrier((x, *others))


def cut(pieces, start, rows):
    for ref, low, count in pieces:
        if start < count:
            assert start + rows <= count
            return ref, low + start
        start -= count
    raise ValueError


def segments(one, other):
    edges = {0}
    for pieces in (one, other):
        at = 0
        for _, _, count in pieces:
            at += count
            edges.add(at)
    edges = sorted(edges)
    return [(a, b - a) for a, b in zip(edges[:-1], edges[1:])]


def reorder_kernel(meta, inv, out, *, step):
    for level in range(LEVELS):
        shape = inv.shape[1:]
        row_id = lax.broadcasted_iota(jnp.int32, shape, 0)
        col_id = lax.broadcasted_iota(jnp.int32, shape, 1)
        source = jnp.bitwise_xor(col_id, meta[step * (level + 1) - 1])
        swap = jnp.where(row_id == source, 1.0, 0.0).astype(BF16)
        out[level] = jnp.dot(inv[level], swap, preferred_element_type=F32).astype(BF16)


def eliminate(meta, inv, panel, merged, top, pairs, outs, level, blocks, flush=None):
    width = blocks * BLOCK
    base = level * meta.shape[0] // LEVELS

    def at(j):
        if isinstance(j, int):
            return pl.ds(j * BLOCK, BLOCK)
        return pl.ds(pl.multiple_of(j * BLOCK, BLOCK), BLOCK)

    def read(pieces, start, rows, j):
        ref, low = cut(pieces, start, rows)
        return ref[pl.ds(low, rows), at(j)].astype(F32)

    def order(j):
        return meta[base + j]

    jobs = [job for _, dest in outs for job in dest]
    if top is not None:
        a, b = top
        half = sum(count for _, _, count in a)
        kept = [(start, start + rows) for source, start, rows in jobs if source == "top"]

        def keep(value, first, rows, j):
            for low, high in kept:
                low, high = max(low, first), min(high, first + rows)
                if low < high:
                    merged[pl.ds(low, high - low), at(j)] = value[low - first : high - first]

        def merge_block(j, carry):
            other = order(j)
            keep_a = meta[base + blocks + j].astype(F32)
            keep_b = meta[base + 2 * blocks + j].astype(F32)
            for start, rows in segments(a, b):
                from_a = read(a, start, rows, j) + read(b, start, rows, other)
                from_b = read(b, start, rows, j) + read(a, start, rows, other)
                keep(from_a, start, rows, j)
                keep(from_b, half + start, rows, j)
                panel[pl.ds(start, rows), at(j)] = (from_a * keep_a).astype(BF16)
                panel[pl.ds(half + start, rows), at(j)] = (from_b * keep_b).astype(BF16)
            return carry

        lax.fori_loop(0, blocks, merge_block, 0, unroll=True)

    def columns(job, j):
        source, start, rows = job
        if source == "top":
            return merged[pl.ds(start, rows), at(j)]
        a, b = pairs[source]
        return read(a, start, rows, j) + read(b, start, rows, order(j))

    pivots = [meta[base + 3 * blocks + i] for i in range(inv.shape[1] // BLOCK)]
    coupling = jnp.concatenate(
        [jnp.concatenate([columns(job, p) for p in pivots], axis=1).astype(BF16) for job in jobs],
        axis=0,
    )
    weights = jnp.dot(coupling, inv[level], preferred_element_type=F32).astype(BF16)

    def finish_tile(t, carry):
        lanes = pl.ds(t * TILE, TILE)
        update = jnp.dot(weights, panel[:, lanes], preferred_element_type=F32)
        done = 0
        for out, dest in outs:
            put = 0
            for job in dest:
                rows = job[2]
                for i in range(TILE // BLOCK):
                    j = (TILE // BLOCK) * t + i
                    part = update[done : done + rows, i * BLOCK : (i + 1) * BLOCK]
                    out[pl.ds(put, rows), at(j)] = (columns(job, j) - part).astype(BF16)
                put += rows
                done += rows
        return carry

    for t in range(width // TILE):
        finish_tile(t, 0)
        if flush is not None:
            flush(t)


def level_kernel(meta, *refs, level, blocks, n_in, top, pairs, outs, n_hidden):
    ins, rest = refs[:n_in], refs[n_in + n_hidden :]
    out_refs, rest = rest[: len(outs)], rest[len(outs) :]

    def stack(spec):
        return [(ins[i], low, count) for i, low, count in spec]

    panel, merged = rest if top is not None else (ins[1], None)
    eliminate(
        meta,
        ins[0],
        panel,
        merged,
        None if top is None else tuple(stack(s) for s in top),
        [tuple(stack(s) for s in pair) for pair in pairs],
        list(zip(out_refs, outs)),
        level,
        blocks,
    )


def two_level_kernel(meta, inv, *refs, blocks, counts, first_outs, second_outs, pairs):
    n = len(counts)
    ours, theirs, near, near_x = refs[:n], refs[n : 2 * n], *refs[2 * n : 2 * n + 2]
    outs, panel, other_panel, merged, far, far_x = refs[2 * n + 2 : -5], *refs[-5:]
    stacks = tuple([(ref, 0, count) for ref, count in zip(group, counts)] for group in (ours, theirs))
    eliminate(meta, inv, other_panel, merged, stacks, [], list(zip((far, far_x), first_outs)), 0, blocks)
    held = ((near, far), (near_x, far_x))
    top = tuple([(ref, 0, ref.shape[0])] for ref in (near, far))
    stacked = [tuple([(ref, low, rows)] for ref in held[i]) for i, low, rows in pairs]
    eliminate(meta, inv, panel, merged, top, stacked, list(zip(outs, second_outs)), 1, blocks)


def last_kernel(meta, inv, panel, own, other, old, out, made, sems, *, level, blocks, first):
    del old
    rows, width = own.shape
    quarter = width // sems.shape[0]
    copies = [
        pltpu.make_async_copy(
            made.at[:, pl.ds(i * quarter, quarter)],
            out.at[pl.ds(first, rows), pl.ds(i * quarter, quarter)],
            sems.at[i],
        )
        for i in range(sems.shape[0])
    ]

    def flush(t):
        if (t + 1) * TILE % quarter == 0:
            copies[t * TILE // quarter].start()

    pair = ([(own, 0, rows)], [(other, 0, rows)])
    eliminate(meta, inv, panel, None, None, [pair], [(made, [(0, 0, rows)])], level, blocks, flush)
    for copy in copies:
        copy.wait()


def run_last(level, meta, inv, panel, own, other, first, old):
    rows, width = own.shape
    vmem = pl.BlockSpec(memory_space=pltpu.VMEM)
    kernel = functools.partial(last_kernel, level=level, blocks=width // BLOCK, first=first)
    return pl.pallas_call(
        kernel,
        out_shape=jax.ShapeDtypeStruct(old.shape, BF16),
        in_specs=[pl.BlockSpec(memory_space=pltpu.SMEM)] + [vmem] * 4 + [pl.BlockSpec(memory_space=pl.ANY)],
        out_specs=pl.BlockSpec(memory_space=pl.ANY),
        scratch_shapes=[pltpu.VMEM((rows, width), BF16), pltpu.SemaphoreType.DMA((4,))],
        input_output_aliases={5: 0},
        compiler_params=pltpu.CompilerParams(vmem_limit_bytes=30 * 2**20),
        cost_estimate=pl.CostEstimate(flops=0, bytes_accessed=0, transcendentals=0),
        name="last_rows",
    )(meta, inv, panel, own, other, old)


def run_level(level, meta, held, outs, pairs=(), top=None, keeps=False, part=None, cost=0):
    arrays = list(held)

    def spec(stack):
        named = []
        for x, low, rows in stack:
            found = [i for i, seen in enumerate(arrays) if seen is x]
            if not found:
                arrays.append(x)
            named.append((found[0] if found else len(arrays) - 1, low, rows))
        return tuple(named)

    top_spec = None if top is None else (spec(top[0]), spec(top[1]))
    pair_specs = tuple((spec(a), spec(b)) for a, b in pairs)
    n_in = len(arrays)
    width = arrays[-1].shape[1]
    size = held[0].shape[1]
    counts = [sum(job[2] for job in dest) for dest in outs]
    shapes = [jax.ShapeDtypeStruct((rows, width), BF16) for rows in counts]
    whole = pl.BlockSpec(memory_space=pltpu.VMEM)
    in_specs = [pl.BlockSpec(memory_space=pltpu.SMEM)] + [whole] * n_in
    out_specs = [whole] * len(shapes)
    aliases = {}
    hidden = []
    if part is not None:
        all_rows, block, old = part
        shapes[0] = jax.ShapeDtypeStruct((all_rows, width), BF16)
        out_specs[0] = pl.BlockSpec((counts[0], width), lambda i: (block, 0))
        if old is not None:
            hidden = [old]
            in_specs.append(pl.BlockSpec(memory_space=pl.ANY))
            aliases = {1 + n_in: 0}
    scratch = []
    if top is not None:
        if keeps:
            shapes.append(jax.ShapeDtypeStruct((size, width), BF16))
            out_specs.append(whole)
        else:
            scratch.append(pltpu.VMEM((size, width), BF16))
        scratch.append(pltpu.VMEM((size, width), F32))
    kernel = functools.partial(
        level_kernel,
        level=level,
        blocks=width // BLOCK,
        n_in=n_in,
        top=top_spec,
        pairs=pair_specs,
        outs=tuple(tuple(dest) for dest in outs),
        n_hidden=len(hidden),
    )
    return pl.pallas_call(
        kernel,
        grid=(1,) if part is not None else (),
        out_shape=shapes,
        in_specs=in_specs,
        out_specs=out_specs,
        scratch_shapes=scratch,
        input_output_aliases=aliases,
        compiler_params=pltpu.CompilerParams(vmem_limit_bytes=30 * 2**20),
        cost_estimate=pl.CostEstimate(flops=cost, bytes_accessed=0, transcendentals=0),
        name=f"level{level}_rows{sum(counts)}",
    )(meta, *arrays, *hidden)


def run_two_levels(meta, inv, ours, theirs, near, near_x, first_outs, second_outs, pairs):
    width, size = near.shape[1], inv.shape[1]
    rows = [sum(job[2] for job in dest) for dest in second_outs] + [size]
    vmem = pl.BlockSpec(memory_space=pltpu.VMEM)
    kernel = functools.partial(
        two_level_kernel,
        blocks=width // BLOCK,
        counts=tuple(x.shape[0] for x in ours),
        first_outs=first_outs,
        second_outs=second_outs,
        pairs=pairs,
    )
    return pl.pallas_call(
        kernel,
        out_shape=[jax.ShapeDtypeStruct((n, width), BF16) for n in rows],
        in_specs=[pl.BlockSpec(memory_space=pltpu.SMEM)] + [vmem] * (3 + 2 * len(ours)),
        out_specs=[vmem] * len(rows),
        scratch_shapes=[
            pltpu.VMEM((size, width), BF16),
            pltpu.VMEM((size, width), F32),
            pltpu.VMEM(near.shape, BF16),
            pltpu.VMEM(near_x.shape, BF16),
        ],
        compiler_params=pltpu.CompilerParams(vmem_limit_bytes=30 * 2**20),
        cost_estimate=pl.CostEstimate(flops=0, bytes_accessed=0, transcendentals=0),
        name="level0_level1",
    )(meta, inv, *ours, *theirs, near, near_x)


def reorder(meta, pivot_inverse):
    step = meta.shape[0] // LEVELS
    return pl.pallas_call(
        functools.partial(reorder_kernel, step=step),
        out_shape=jax.ShapeDtypeStruct(pivot_inverse.shape, BF16),
        in_specs=[pl.BlockSpec(memory_space=pltpu.SMEM), pl.BlockSpec(memory_space=pltpu.VMEM)],
        out_specs=pl.BlockSpec(memory_space=pltpu.VMEM),
        compiler_params=pltpu.CompilerParams(vmem_limit_bytes=30 * 2**20),
        cost_estimate=pl.CostEstimate(flops=0, bytes_accessed=0, transcendentals=0),
        name="reorder",
    )(meta, pivot_inverse)


def make_meta(size, block_pattern, column_order, pivot_blocks):
    blocks = column_order.shape[1]
    rank = jnp.int32(0)
    meta = []
    for level in range(LEVELS):
        bit = my_bit(level)
        rank = rank + bit * (1 << level)
        shift = rank * (size >> (level + 1))
        meta += [
            column_order[level],
            jnp.where(bit == 0, block_pattern[level, 0], block_pattern[level, 1]),
            jnp.where(bit == 0, block_pattern[level, 1], block_pattern[level, 0]),
            pivot_blocks[level],
            jnp.zeros((blocks,), jnp.int32) + shift,
        ]
    return jnp.concatenate(meta)


def on_device(schur_slab, pivot_inverse, block_pattern, column_order, pivot_blocks):
    all_rows = schur_slab.shape[0]
    size = pivot_inverse.shape[1]
    half, quarter, eighth, share = size // 2, size // 4, size // 8, size // 16
    meta = make_meta(size, block_pattern, column_order, pivot_blocks)

    def rows_of(x):
        return [(x, 0, x.shape[0])]

    def chunk(level, panel, own, other, **more):
        (out,) = run_level(
            level, meta, (inv, panel), [[(0, 0, own.shape[0])]], pairs=[(rows_of(own), rows_of(other))], **more
        )
        return out

    cut_1 = quarter + share
    cut_2 = half + quarter
    begin_1 = schur_slab[:cut_1]
    first_z1 = trade(begin_1, 1)
    begin_y1 = trade(begin_1, 0)
    slab, begin_1 = after(schur_slab, begin_1)
    begin_2, begin_3, rest_2 = slab[cut_1:half], slab[half:cut_2], slab[cut_2:]
    begin_y2, begin_y3 = trade(begin_2, 0), trade(begin_3, 0)
    inv = reorder(meta, pivot_inverse)

    first_yz1 = trade(first_z1, 0)
    first_2, first_z1 = after(begin_2, first_z1)
    first_z2 = trade(first_2, 1)
    rest_2, begin_y3 = after(rest_2, begin_y3)

    tops = [("top", 0, quarter), ("top", half, quarter)]
    begun = ((begin_1, begin_2, begin_3), (begin_y1, begin_y2, begin_y3))
    near, near_x, after_1, panel_0 = run_level(
        0,
        meta,
        (inv,),
        [tops, [("top", quarter, quarter)], [(0, 0, quarter)]],
        top=tuple(rows_of(x) + rows_of(y) for x, y, _ in begun),
        pairs=[tuple(rows_of(x) for *_, x in begun)],
        keeps=True,
    )
    first_z2, after_1 = after(first_z2, after_1)
    after_z1 = trade(after_1, 1)
    first_z2, first_yz1 = after(first_z2, first_yz1)
    first_yz2 = trade(first_z2, 0)
    rest_2, first_yz2 = after(rest_2, first_yz2)
    rest_y2 = trade(rest_2, 0)

    e, y, z, yz = (("top", low, eighth) for low in range(0, size, quarter))
    jobs = [[e, (*y[:2], share)], [("top", quarter + share, share), z], [yz, (0, 0, share)]]
    jobs.append([(0, share, share), (1, 0, quarter)])
    *head, next_0, panel_1 = run_two_levels(
        meta,
        inv,
        (first_z1, first_z2),
        (first_yz1, first_yz2),
        near,
        near_x,
        (tuple(tops), (("top", quarter, quarter),)),
        jobs,
        ((0, eighth, eighth), (1, 0, quarter)),
    )
    head_c = [trade(x, 2) for x in head]

    tops = [("top", low, share) for low in range(0, size, eighth)]
    first, lead, others, panel_2 = run_level(
        2,
        meta,
        (inv,),
        [[tops[0]], [("top", share, share), (0, 0, share)], tops[1:]],
        top=tuple(
            rows_of(group[0]) + rows_of(group[1]) + [(group[2], 0, eighth)] for group in (head, head_c)
        ),
        pairs=[tuple([(group[2], eighth, share)] for group in (head, head_c))],
        keeps=True,
    )
    first_w, lead_w = trade(first, 3), trade(lead, 3)
    after_z1, rest_y2, lead = after(after_z1, rest_y2, lead)
    next_1 = run_level(
        1,
        meta,
        (inv, panel_1),
        [[(0, 0, eighth)], [(0, eighth, eighth)]],
        pairs=[(rows_of(after_1), rows_of(after_z1))],
        cost=10**10,
    )
    next_1 = [next_0, *next_1]
    next_c1 = [trade(x, 2) for x in next_1]
    after_2 = chunk(0, panel_0, rest_2, rest_y2, cost=0)
    after_z2 = trade(after_2, 1)
    next_c1[0], after_2 = after(next_c1[0], after_2)
    (last_1,) = run_level(
        2,
        meta,
        (inv, panel_2),
        [[(i, 0, x.shape[0]) for i, x in enumerate(next_1)]],
        pairs=[(rows_of(x), rows_of(y)) for x, y in zip(next_1, next_c1)],
    )
    last_w1 = trade(last_1, 3)
    first_wz = trade(first_w, 1)
    after_z2, first_wz, lead_w = after(after_z2, first_wz, lead_w)
    tops_w = jnp.concatenate([first_w, first_wz], axis=0)
    tops_wc = trade(tops_w, 2)
    tops_wy = trade(tops_w, 0)
    tops_wyc = trade(tops_wy, 2)
    next_2 = chunk(1, panel_1, after_2, after_z2, cost=5 * 10**9)
    last_2 = chunk(2, panel_2, next_2, trade(next_2, 2))
    last_w2 = trade(last_2, 3)
    tops = [(first, 0, share)] + [(others, share * i, share) for i in range(7)]
    tops_other = [(x, low, share) for low in (0, share) for x in (tops_w, tops_wy)]
    tops_other += [(x, low, share) for low in (0, share) for x in (tops_wc, tops_wyc)]
    out, panel_3 = run_level(
        3,
        meta,
        (inv,),
        [[("top", 0, share), (0, 0, eighth), (1, 0, last_1.shape[0])]],
        top=(tops, tops_other),
        pairs=[(rows_of(lead), rows_of(lead_w)), (rows_of(last_1), rows_of(last_w1))],
        keeps=True,
        part=(all_rows, 0, None),
        cost=5 * 10**10,
    )
    return run_last(3, meta, inv, panel_3, last_2, last_w2, all_rows - quarter, out)


def solution(mesh):
    return jax.shard_map(
        on_device,
        mesh=mesh,
        in_specs=(P(("tx", "ty"), None), P(), P(), P(), P()),
        out_specs=P(("tx", "ty"), None),
        check_vma=False,
    )
```

```python
import functools

import jax
import jax.numpy as jnp
from jax import lax
from jax.experimental import pallas as pl
from jax.experimental.pallas import tpu as pltpu
from jax.sharding import PartitionSpec as P

BLOCK = 128
LEVELS = 4
TILE = 2 * BLOCK
F32 = jnp.float32
BF16 = jnp.bfloat16


def stride_bit(axis, level):
    return lax.axis_size(axis).bit_length() - 2 - level // 2


def level_axis(level):
    return "tx" if level % 2 == 0 else "ty"


def trade(block, level):
    axis = level_axis(level)
    flip = 1 << stride_bit(axis, level)
    return lax.ppermute(block, axis, [(i, i ^ flip) for i in range(lax.axis_size(axis))])


def my_bit(level):
    axis = level_axis(level)
    place = lax.axis_index(axis).astype(jnp.int32)
    return jnp.bitwise_and(jnp.right_shift(place, stride_bit(axis, level)), 1)


def after(x, *others):
    return lax.optimization_barrier((x, *others))


def cut(pieces, start, rows):
    for ref, low, count in pieces:
        if start < count:
            assert start + rows <= count
            return ref, low + start
        start -= count
    raise ValueError


def segments(one, other):
    edges = {0}
    for pieces in (one, other):
        at = 0
        for _, _, count in pieces:
            at += count
            edges.add(at)
    edges = sorted(edges)
    return [(a, b - a) for a, b in zip(edges[:-1], edges[1:])]


def reorder_kernel(meta, inv, out, *, step):
    for level in range(LEVELS):
        shape = inv.shape[1:]
        row_id = lax.broadcasted_iota(jnp.int32, shape, 0)
        col_id = lax.broadcasted_iota(jnp.int32, shape, 1)
        source = jnp.bitwise_xor(col_id, meta[step * (level + 1) - 1])
        swap = jnp.where(row_id == source, 1.0, 0.0).astype(BF16)
        out[level] = jnp.dot(inv[level], swap, preferred_element_type=F32).astype(BF16)


def eliminate(meta, inv, panel, merged, top, pairs, outs, level, blocks, flush=None):
    width = blocks * BLOCK
    base = level * meta.shape[0] // LEVELS

    def at(j):
        if isinstance(j, int):
            return pl.ds(j * BLOCK, BLOCK)
        return pl.ds(pl.multiple_of(j * BLOCK, BLOCK), BLOCK)

    def read(pieces, start, rows, j):
        ref, low = cut(pieces, start, rows)
        return ref[pl.ds(low, rows), at(j)].astype(F32)

    def order(j):
        return meta[base + j]

    jobs = [job for _, dest in outs for job in dest]
    if top is not None:
        a, b = top
        half = sum(count for _, _, count in a)
    pivots = [meta[base + 3 * blocks + i] for i in range(inv.shape[1] // BLOCK)]

    def pivot_columns(job, p):
        source, start, rows = job
        own, other = (a, b) if source == "top" else pairs[source]
        if source == "top" and start >= half:
            own, other, start = b, a, start - half
        parts = []
        for low, count in segments(own, other):
            first, last = max(low, start), min(low + count, start + rows)
            if first < last:
                size = last - first
                parts.append(read(own, first, size, p) + read(other, first, size, order(p)))
        return jnp.concatenate(parts, axis=0)

    coupling = jnp.concatenate(
        [jnp.concatenate([pivot_columns(job, p) for p in pivots], axis=1).astype(BF16) for job in jobs],
        axis=0,
    )
    weights = jnp.dot(coupling, inv[level], preferred_element_type=F32).astype(BF16)

    if top is not None:
        kept = [(start, start + rows) for source, start, rows in jobs if source == "top"]

        def keep(value, first, rows, j):
            for low, high in kept:
                low, high = max(low, first), min(high, first + rows)
                if low < high:
                    merged[pl.ds(low, high - low), at(j)] = value[low - first : high - first]

        def merge_block(j, carry):
            other = order(j)
            keep_a = meta[base + blocks + j].astype(F32)
            keep_b = meta[base + 2 * blocks + j].astype(F32)
            for start, rows in segments(a, b):
                from_a = read(a, start, rows, j) + read(b, start, rows, other)
                from_b = read(b, start, rows, j) + read(a, start, rows, other)
                keep(from_a, start, rows, j)
                keep(from_b, half + start, rows, j)
                panel[pl.ds(start, rows), at(j)] = (from_a * keep_a).astype(BF16)
                panel[pl.ds(half + start, rows), at(j)] = (from_b * keep_b).astype(BF16)
            return carry

        lax.fori_loop(0, blocks, merge_block, 0, unroll=True)

    def columns(job, j):
        source, start, rows = job
        if source == "top":
            return merged[pl.ds(start, rows), at(j)]
        a, b = pairs[source]
        return read(a, start, rows, j) + read(b, start, rows, order(j))

    def finish_tile(t, carry):
        lanes = pl.ds(t * TILE, TILE)
        update = jnp.dot(weights, panel[:, lanes], preferred_element_type=F32)
        done = 0
        for out, dest in outs:
            put = 0
            for job in dest:
                rows = job[2]
                for i in range(TILE // BLOCK):
                    j = (TILE // BLOCK) * t + i
                    part = update[done : done + rows, i * BLOCK : (i + 1) * BLOCK]
                    out[pl.ds(put, rows), at(j)] = (columns(job, j) - part).astype(BF16)
                put += rows
                done += rows
        return carry

    for t in range(width // TILE):
        finish_tile(t, 0)
        if flush is not None:
            flush(t)


def level_kernel(meta, *refs, level, blocks, n_in, top, pairs, outs, n_hidden):
    ins, rest = refs[:n_in], refs[n_in + n_hidden :]
    out_refs, rest = rest[: len(outs)], rest[len(outs) :]

    def stack(spec):
        return [(ins[i], low, count) for i, low, count in spec]

    panel, merged = rest if top is not None else (ins[1], None)
    eliminate(
        meta,
        ins[0],
        panel,
        merged,
        None if top is None else tuple(stack(s) for s in top),
        [tuple(stack(s) for s in pair) for pair in pairs],
        list(zip(out_refs, outs)),
        level,
        blocks,
    )


def two_level_kernel(meta, inv, *refs, blocks, counts, first_outs, second_outs, pairs):
    n = len(counts)
    ours, theirs, near, near_x = refs[:n], refs[n : 2 * n], *refs[2 * n : 2 * n + 2]
    outs, panel, other_panel, merged, far, far_x = refs[2 * n + 2 : -5], *refs[-5:]
    stacks = tuple([(ref, 0, count) for ref, count in zip(group, counts)] for group in (ours, theirs))
    eliminate(meta, inv, other_panel, merged, stacks, [], list(zip((far, far_x), first_outs)), 0, blocks)
    held = ((near, far), (near_x, far_x))
    top = tuple([(ref, 0, ref.shape[0])] for ref in (near, far))
    stacked = [tuple([(ref, low, rows)] for ref in held[i]) for i, low, rows in pairs]
    eliminate(meta, inv, panel, merged, top, stacked, list(zip(outs, second_outs)), 1, blocks)


def last_kernel(meta, inv, panel, own, other, old, out, made, sems, *, level, blocks, first):
    del old
    rows, width = own.shape
    quarter = width // sems.shape[0]
    copies = [
        pltpu.make_async_copy(
            made.at[:, pl.ds(i * quarter, quarter)],
            out.at[pl.ds(first, rows), pl.ds(i * quarter, quarter)],
            sems.at[i],
        )
        for i in range(sems.shape[0])
    ]

    def flush(t):
        if (t + 1) * TILE % quarter == 0:
            copies[t * TILE // quarter].start()

    pair = ([(own, 0, rows)], [(other, 0, rows)])
    eliminate(meta, inv, panel, None, None, [pair], [(made, [(0, 0, rows)])], level, blocks, flush)
    for copy in copies:
        copy.wait()


def run_last(level, meta, inv, panel, own, other, first, old):
    rows, width = own.shape
    vmem = pl.BlockSpec(memory_space=pltpu.VMEM)
    kernel = functools.partial(last_kernel, level=level, blocks=width // BLOCK, first=first)
    return pl.pallas_call(
        kernel,
        out_shape=jax.ShapeDtypeStruct(old.shape, BF16),
        in_specs=[pl.BlockSpec(memory_space=pltpu.SMEM)] + [vmem] * 4 + [pl.BlockSpec(memory_space=pl.ANY)],
        out_specs=pl.BlockSpec(memory_space=pl.ANY),
        scratch_shapes=[pltpu.VMEM((rows, width), BF16), pltpu.SemaphoreType.DMA((4,))],
        input_output_aliases={5: 0},
        compiler_params=pltpu.CompilerParams(vmem_limit_bytes=30 * 2**20),
        cost_estimate=pl.CostEstimate(flops=0, bytes_accessed=0, transcendentals=0),
        name="last_rows",
    )(meta, inv, panel, own, other, old)


def run_level(level, meta, held, outs, pairs=(), top=None, keeps=False, part=None, cost=0):
    arrays = list(held)

    def spec(stack):
        named = []
        for x, low, rows in stack:
            found = [i for i, seen in enumerate(arrays) if seen is x]
            if not found:
                arrays.append(x)
            named.append((found[0] if found else len(arrays) - 1, low, rows))
        return tuple(named)

    top_spec = None if top is None else (spec(top[0]), spec(top[1]))
    pair_specs = tuple((spec(a), spec(b)) for a, b in pairs)
    n_in = len(arrays)
    width = arrays[-1].shape[1]
    size = held[0].shape[1]
    counts = [sum(job[2] for job in dest) for dest in outs]
    shapes = [jax.ShapeDtypeStruct((rows, width), BF16) for rows in counts]
    whole = pl.BlockSpec(memory_space=pltpu.VMEM)
    in_specs = [pl.BlockSpec(memory_space=pltpu.SMEM)] + [whole] * n_in
    out_specs = [whole] * len(shapes)
    aliases = {}
    hidden = []
    if part is not None:
        all_rows, block, old = part
        shapes[0] = jax.ShapeDtypeStruct((all_rows, width), BF16)
        out_specs[0] = pl.BlockSpec((counts[0], width), lambda i: (block, 0))
        if old is not None:
            hidden = [old]
            in_specs.append(pl.BlockSpec(memory_space=pl.ANY))
            aliases = {1 + n_in: 0}
    scratch = []
    if top is not None:
        if keeps:
            shapes.append(jax.ShapeDtypeStruct((size, width), BF16))
            out_specs.append(whole)
        else:
            scratch.append(pltpu.VMEM((size, width), BF16))
        scratch.append(pltpu.VMEM((size, width), F32))
    kernel = functools.partial(
        level_kernel,
        level=level,
        blocks=width // BLOCK,
        n_in=n_in,
        top=top_spec,
        pairs=pair_specs,
        outs=tuple(tuple(dest) for dest in outs),
        n_hidden=len(hidden),
    )
    return pl.pallas_call(
        kernel,
        grid=(1,) if part is not None else (),
        out_shape=shapes,
        in_specs=in_specs,
        out_specs=out_specs,
        scratch_shapes=scratch,
        input_output_aliases=aliases,
        compiler_params=pltpu.CompilerParams(vmem_limit_bytes=30 * 2**20),
        cost_estimate=pl.CostEstimate(flops=cost, bytes_accessed=0, transcendentals=0),
        name=f"level{level}_rows{sum(counts)}",
    )(meta, *arrays, *hidden)


def run_two_levels(meta, inv, ours, theirs, near, near_x, first_outs, second_outs, pairs):
    width, size = near.shape[1], inv.shape[1]
    rows = [sum(job[2] for job in dest) for dest in second_outs] + [size]
    vmem = pl.BlockSpec(memory_space=pltpu.VMEM)
    kernel = functools.partial(
        two_level_kernel,
        blocks=width // BLOCK,
        counts=tuple(x.shape[0] for x in ours),
        first_outs=first_outs,
        second_outs=second_outs,
        pairs=pairs,
    )
    return pl.pallas_call(
        kernel,
        out_shape=[jax.ShapeDtypeStruct((n, width), BF16) for n in rows],
        in_specs=[pl.BlockSpec(memory_space=pltpu.SMEM)] + [vmem] * (3 + 2 * len(ours)),
        out_specs=[vmem] * len(rows),
        scratch_shapes=[
            pltpu.VMEM((size, width), BF16),
            pltpu.VMEM((size, width), F32),
            pltpu.VMEM(near.shape, BF16),
            pltpu.VMEM(near_x.shape, BF16),
        ],
        compiler_params=pltpu.CompilerParams(vmem_limit_bytes=30 * 2**20),
        cost_estimate=pl.CostEstimate(flops=0, bytes_accessed=0, transcendentals=0),
        name="level0_level1",
    )(meta, inv, *ours, *theirs, near, near_x)


def reorder(meta, pivot_inverse):
    step = meta.shape[0] // LEVELS
    return pl.pallas_call(
        functools.partial(reorder_kernel, step=step),
        out_shape=jax.ShapeDtypeStruct(pivot_inverse.shape, BF16),
        in_specs=[pl.BlockSpec(memory_space=pltpu.SMEM), pl.BlockSpec(memory_space=pltpu.VMEM)],
        out_specs=pl.BlockSpec(memory_space=pltpu.VMEM),
        compiler_params=pltpu.CompilerParams(vmem_limit_bytes=30 * 2**20),
        cost_estimate=pl.CostEstimate(flops=0, bytes_accessed=0, transcendentals=0),
        name="reorder",
    )(meta, pivot_inverse)


def make_meta(size, block_pattern, column_order, pivot_blocks):
    blocks = column_order.shape[1]
    rank = jnp.int32(0)
    meta = []
    for level in range(LEVELS):
        bit = my_bit(level)
        rank = rank + bit * (1 << level)
        shift = rank * (size >> (level + 1))
        meta += [
            column_order[level],
            jnp.where(bit == 0, block_pattern[level, 0], block_pattern[level, 1]),
            jnp.where(bit == 0, block_pattern[level, 1], block_pattern[level, 0]),
            pivot_blocks[level],
            jnp.zeros((blocks,), jnp.int32) + shift,
        ]
    return jnp.concatenate(meta)


def on_device(schur_slab, pivot_inverse, block_pattern, column_order, pivot_blocks):
    all_rows = schur_slab.shape[0]
    size = pivot_inverse.shape[1]
    half, quarter, eighth, share = size // 2, size // 4, size // 8, size // 16
    meta = make_meta(size, block_pattern, column_order, pivot_blocks)

    def rows_of(x):
        return [(x, 0, x.shape[0])]

    def chunk(level, panel, own, other, **more):
        (out,) = run_level(
            level, meta, (inv, panel), [[(0, 0, own.shape[0])]], pairs=[(rows_of(own), rows_of(other))], **more
        )
        return out

    cut_1 = quarter + share
    cut_2 = half + quarter
    begin_1 = schur_slab[:cut_1]
    first_z1 = trade(begin_1, 1)
    begin_y1 = trade(begin_1, 0)
    slab, begin_1 = after(schur_slab, begin_1)
    begin_2, begin_3, rest_2 = slab[cut_1:half], slab[half:cut_2], slab[cut_2:]
    begin_y2, begin_y3 = trade(begin_2, 0), trade(begin_3, 0)
    inv = reorder(meta, pivot_inverse)

    first_yz1 = trade(first_z1, 0)
    first_2, first_z1 = after(begin_2, first_z1)
    first_z2 = trade(first_2, 1)
    rest_2, begin_y3 = after(rest_2, begin_y3)

    tops = [("top", 0, quarter), ("top", half, quarter)]
    begun = ((begin_1, begin_2, begin_3), (begin_y1, begin_y2, begin_y3))
    near, near_x, after_1, panel_0 = run_level(
        0,
        meta,
        (inv,),
        [tops, [("top", quarter, quarter)], [(0, 0, quarter)]],
        top=tuple(rows_of(x) + rows_of(y) for x, y, _ in begun),
        pairs=[tuple(rows_of(x) for *_, x in begun)],
        keeps=True,
    )
    first_z2, after_1 = after(first_z2, after_1)
    after_z1 = trade(after_1, 1)
    first_z2, first_yz1 = after(first_z2, first_yz1)
    first_yz2 = trade(first_z2, 0)
    rest_2, first_yz2 = after(rest_2, first_yz2)
    rest_y2 = trade(rest_2, 0)

    e, y, z, yz = (("top", low, eighth) for low in range(0, size, quarter))
    jobs = [[e, (*y[:2], share)], [("top", quarter + share, share), z], [yz, (0, 0, share)]]
    jobs.append([(0, share, share), (1, 0, quarter)])
    *head, next_0, panel_1 = run_two_levels(
        meta,
        inv,
        (first_z1, first_z2),
        (first_yz1, first_yz2),
        near,
        near_x,
        (tuple(tops), (("top", quarter, quarter),)),
        jobs,
        ((0, eighth, eighth), (1, 0, quarter)),
    )
    head_c = [trade(x, 2) for x in head]

    tops = [("top", low, share) for low in range(0, size, eighth)]
    first, lead, others, panel_2 = run_level(
        2,
        meta,
        (inv,),
        [[tops[0]], [("top", share, share), (0, 0, share)], tops[1:]],
        top=tuple(
            rows_of(group[0]) + rows_of(group[1]) + [(group[2], 0, eighth)] for group in (head, head_c)
        ),
        pairs=[tuple([(group[2], eighth, share)] for group in (head, head_c))],
        keeps=True,
    )
    first_w, lead_w = trade(first, 3), trade(lead, 3)
    after_z1, rest_y2, lead = after(after_z1, rest_y2, lead)
    next_1 = run_level(
        1,
        meta,
        (inv, panel_1),
        [[(0, 0, eighth)], [(0, eighth, eighth)]],
        pairs=[(rows_of(after_1), rows_of(after_z1))],
        cost=10**10,
    )
    next_1 = [next_0, *next_1]
    next_c1 = [trade(x, 2) for x in next_1]
    after_2 = chunk(0, panel_0, rest_2, rest_y2, cost=0)
    after_z2 = trade(after_2, 1)
    next_c1[0], after_2 = after(next_c1[0], after_2)
    (last_1,) = run_level(
        2,
        meta,
        (inv, panel_2),
        [[(i, 0, x.shape[0]) for i, x in enumerate(next_1)]],
        pairs=[(rows_of(x), rows_of(y)) for x, y in zip(next_1, next_c1)],
    )
    last_w1 = trade(last_1, 3)
    first_wz = trade(first_w, 1)
    after_z2, first_wz, lead_w = after(after_z2, first_wz, lead_w)
    tops_w = jnp.concatenate([first_w, first_wz], axis=0)
    tops_wc = trade(tops_w, 2)
    tops_wy = trade(tops_w, 0)
    tops_wyc = trade(tops_wy, 2)
    next_2 = chunk(1, panel_1, after_2, after_z2, cost=5 * 10**9)
    last_2 = chunk(2, panel_2, next_2, trade(next_2, 2))
    last_w2 = trade(last_2, 3)
    tops = [(first, 0, share)] + [(others, share * i, share) for i in range(7)]
    tops_other = [(x, low, share) for low in (0, share) for x in (tops_w, tops_wy)]
    tops_other += [(x, low, share) for low in (0, share) for x in (tops_wc, tops_wyc)]
    out, panel_3 = run_level(
        3,
        meta,
        (inv,),
        [[("top", 0, share), (0, 0, eighth), (1, 0, last_1.shape[0])]],
        top=(tops, tops_other),
        pairs=[(rows_of(lead), rows_of(lead_w)), (rows_of(last_1), rows_of(last_w1))],
        keeps=True,
        part=(all_rows, 0, None),
        cost=5 * 10**10,
    )
    return run_last(3, meta, inv, panel_3, last_2, last_w2, all_rows - quarter, out)


def solution(mesh):
    return jax.shard_map(
        on_device,
        mesh=mesh,
        in_specs=(P(("tx", "ty"), None), P(), P(), P(), P()),
        out_specs=P(("tx", "ty"), None),
        check_vma=False,
    )
```

```python
import functools

import jax
import jax.numpy as jnp
from jax import lax
from jax.experimental import pallas as pl
from jax.experimental.pallas import tpu as pltpu
from jax.sharding import PartitionSpec as P

BLOCK = 128
LEVELS = 4
TILE = 2 * BLOCK
F32 = jnp.float32
BF16 = jnp.bfloat16


def stride_bit(axis, level):
    return lax.axis_size(axis).bit_length() - 2 - level // 2


def level_axis(level):
    return "tx" if level % 2 == 0 else "ty"


def trade(block, level):
    axis = level_axis(level)
    flip = 1 << stride_bit(axis, level)
    return lax.ppermute(block, axis, [(i, i ^ flip) for i in range(lax.axis_size(axis))])


def my_bit(level):
    axis = level_axis(level)
    place = lax.axis_index(axis).astype(jnp.int32)
    return jnp.bitwise_and(jnp.right_shift(place, stride_bit(axis, level)), 1)


def after(x, *others):
    return lax.optimization_barrier((x, *others))


def cut(pieces, start, rows):
    for ref, low, count in pieces:
        if start < count:
            assert start + rows <= count
            return ref, low + start
        start -= count
    raise ValueError


def segments(one, other):
    edges = {0}
    for pieces in (one, other):
        at = 0
        for _, _, count in pieces:
            at += count
            edges.add(at)
    edges = sorted(edges)
    return [(a, b - a) for a, b in zip(edges[:-1], edges[1:])]


def reorder_kernel(meta, inv, out, *, step):
    for level in range(LEVELS):
        shape = inv.shape[1:]
        row_id = lax.broadcasted_iota(jnp.int32, shape, 0)
        col_id = lax.broadcasted_iota(jnp.int32, shape, 1)
        source = jnp.bitwise_xor(col_id, meta[step * (level + 1) - 1])
        swap = jnp.where(row_id == source, 1.0, 0.0).astype(BF16)
        out[level] = jnp.dot(inv[level], swap, preferred_element_type=F32).astype(BF16)


def eliminate(meta, inv, panel, merged, top, pairs, outs, level, blocks, flush=None):
    width = blocks * BLOCK
    base = level * meta.shape[0] // LEVELS

    def at(j):
        if isinstance(j, int):
            return pl.ds(j * BLOCK, BLOCK)
        return pl.ds(pl.multiple_of(j * BLOCK, BLOCK), BLOCK)

    def read(pieces, start, rows, j):
        ref, low = cut(pieces, start, rows)
        return ref[pl.ds(low, rows), at(j)].astype(F32)

    def order(j):
        return meta[base + j]

    jobs = [job for _, dest in outs for job in dest]
    if top is not None:
        a, b = top
        half = sum(count for _, _, count in a)
    pivots = [meta[base + 3 * blocks + i] for i in range(inv.shape[1] // BLOCK)]

    def pivot_columns(job, p):
        source, start, rows = job
        own, other = (a, b) if source == "top" else pairs[source]
        if source == "top" and start >= half:
            own, other, start = b, a, start - half
        parts = []
        for low, count in segments(own, other):
            first, last = max(low, start), min(low + count, start + rows)
            if first < last:
                size = last - first
                parts.append(read(own, first, size, p) + read(other, first, size, order(p)))
        return jnp.concatenate(parts, axis=0)

    coupling = jnp.concatenate(
        [jnp.concatenate([pivot_columns(job, p) for p in pivots], axis=1).astype(BF16) for job in jobs],
        axis=0,
    )
    weights = jnp.dot(coupling, inv[level], preferred_element_type=F32).astype(BF16)

    if top is not None:
        kept = [(start, start + rows) for source, start, rows in jobs if source == "top"]

        def keep(value, first, rows, j):
            for low, high in kept:
                low, high = max(low, first), min(high, first + rows)
                if low < high:
                    merged[pl.ds(low, high - low), at(j)] = value[low - first : high - first]

        def merge_block(j, carry):
            other = order(j)
            keep_a = meta[base + blocks + j].astype(F32)
            keep_b = meta[base + 2 * blocks + j].astype(F32)
            for start, rows in segments(a, b):
                from_a = read(a, start, rows, j) + read(b, start, rows, other)
                from_b = read(b, start, rows, j) + read(a, start, rows, other)
                keep(from_a, start, rows, j)
                keep(from_b, half + start, rows, j)
                panel[pl.ds(start, rows), at(j)] = (from_a * keep_a).astype(BF16)
                panel[pl.ds(half + start, rows), at(j)] = (from_b * keep_b).astype(BF16)
            return carry

        lax.fori_loop(0, blocks, merge_block, 0, unroll=True)

    def columns(job, j):
        source, start, rows = job
        if source == "top":
            return merged[pl.ds(start, rows), at(j)]
        a, b = pairs[source]
        return read(a, start, rows, j) + read(b, start, rows, order(j))

    def finish_tile(t, carry):
        lanes = pl.ds(t * TILE, TILE)
        update = jnp.dot(weights, panel[:, lanes], preferred_element_type=F32)
        done = 0
        for out, dest in outs:
            put = 0
            for job in dest:
                rows = job[2]
                for i in range(TILE // BLOCK):
                    j = (TILE // BLOCK) * t + i
                    part = update[done : done + rows, i * BLOCK : (i + 1) * BLOCK]
                    out[pl.ds(put, rows), at(j)] = (columns(job, j) - part).astype(BF16)
                put += rows
                done += rows
        return carry

    for t in range(width // TILE):
        finish_tile(t, 0)
        if flush is not None:
            flush(t)


def level_kernel(meta, *refs, level, blocks, n_in, top, pairs, outs, n_hidden):
    ins, rest = refs[:n_in], refs[n_in + n_hidden :]
    out_refs, rest = rest[: len(outs)], rest[len(outs) :]

    def stack(spec):
        return [(ins[i], low, count) for i, low, count in spec]

    panel, merged = rest if top is not None else (ins[1], None)
    eliminate(
        meta,
        ins[0],
        panel,
        merged,
        None if top is None else tuple(stack(s) for s in top),
        [tuple(stack(s) for s in pair) for pair in pairs],
        list(zip(out_refs, outs)),
        level,
        blocks,
    )


def two_level_kernel(meta, inv, *refs, blocks, counts, first_outs, second_outs, pairs):
    n = len(counts)
    ours, theirs, near, near_x = refs[:n], refs[n : 2 * n], *refs[2 * n : 2 * n + 2]
    outs, panel, other_panel, merged, far, far_x = refs[2 * n + 2 : -5], *refs[-5:]
    stacks = tuple([(ref, 0, count) for ref, count in zip(group, counts)] for group in (ours, theirs))
    eliminate(meta, inv, other_panel, merged, stacks, [], list(zip((far, far_x), first_outs)), 0, blocks)
    held = ((near, far), (near_x, far_x))
    top = tuple([(ref, 0, ref.shape[0])] for ref in (near, far))
    stacked = [tuple([(ref, low, rows)] for ref in held[i]) for i, low, rows in pairs]
    eliminate(meta, inv, panel, merged, top, stacked, list(zip(outs, second_outs)), 1, blocks)


def last_kernel(meta, inv, panel, own, other, old, out, made, sems, *, level, blocks, first):
    del old
    rows, width = own.shape
    quarter = width // sems.shape[0]
    copies = [
        pltpu.make_async_copy(
            made.at[:, pl.ds(i * quarter, quarter)],
            out.at[pl.ds(first, rows), pl.ds(i * quarter, quarter)],
            sems.at[i],
        )
        for i in range(sems.shape[0])
    ]

    def flush(t):
        if (t + 1) * TILE % quarter == 0:
            copies[t * TILE // quarter].start()

    pair = ([(own, 0, rows)], [(other, 0, rows)])
    eliminate(meta, inv, panel, None, None, [pair], [(made, [(0, 0, rows)])], level, blocks, flush)
    for copy in copies:
        copy.wait()


def run_last(level, meta, inv, panel, own, other, first, old):
    rows, width = own.shape
    vmem = pl.BlockSpec(memory_space=pltpu.VMEM)
    kernel = functools.partial(last_kernel, level=level, blocks=width // BLOCK, first=first)
    return pl.pallas_call(
        kernel,
        out_shape=jax.ShapeDtypeStruct(old.shape, BF16),
        in_specs=[pl.BlockSpec(memory_space=pltpu.SMEM)] + [vmem] * 4 + [pl.BlockSpec(memory_space=pl.ANY)],
        out_specs=pl.BlockSpec(memory_space=pl.ANY),
        scratch_shapes=[pltpu.VMEM((rows, width), BF16), pltpu.SemaphoreType.DMA((8,))],
        input_output_aliases={5: 0},
        compiler_params=pltpu.CompilerParams(vmem_limit_bytes=30 * 2**20),
        cost_estimate=pl.CostEstimate(flops=0, bytes_accessed=0, transcendentals=0),
        name="last_rows",
    )(meta, inv, panel, own, other, old)


def run_level(level, meta, held, outs, pairs=(), top=None, keeps=False, part=None, cost=0):
    arrays = list(held)

    def spec(stack):
        named = []
        for x, low, rows in stack:
            found = [i for i, seen in enumerate(arrays) if seen is x]
            if not found:
                arrays.append(x)
            named.append((found[0] if found else len(arrays) - 1, low, rows))
        return tuple(named)

    top_spec = None if top is None else (spec(top[0]), spec(top[1]))
    pair_specs = tuple((spec(a), spec(b)) for a, b in pairs)
    n_in = len(arrays)
    width = arrays[-1].shape[1]
    size = held[0].shape[1]
    counts = [sum(job[2] for job in dest) for dest in outs]
    shapes = [jax.ShapeDtypeStruct((rows, width), BF16) for rows in counts]
    whole = pl.BlockSpec(memory_space=pltpu.VMEM)
    in_specs = [pl.BlockSpec(memory_space=pltpu.SMEM)] + [whole] * n_in
    out_specs = [whole] * len(shapes)
    aliases = {}
    hidden = []
    if part is not None:
        all_rows, block, old = part
        shapes[0] = jax.ShapeDtypeStruct((all_rows, width), BF16)
        out_specs[0] = pl.BlockSpec((counts[0], width), lambda i: (block, 0))
        if old is not None:
            hidden = [old]
            in_specs.append(pl.BlockSpec(memory_space=pl.ANY))
            aliases = {1 + n_in: 0}
    scratch = []
    if top is not None:
        if keeps:
            shapes.append(jax.ShapeDtypeStruct((size, width), BF16))
            out_specs.append(whole)
        else:
            scratch.append(pltpu.VMEM((size, width), BF16))
        scratch.append(pltpu.VMEM((size, width), F32))
    kernel = functools.partial(
        level_kernel,
        level=level,
        blocks=width // BLOCK,
        n_in=n_in,
        top=top_spec,
        pairs=pair_specs,
        outs=tuple(tuple(dest) for dest in outs),
        n_hidden=len(hidden),
    )
    return pl.pallas_call(
        kernel,
        grid=(1,) if part is not None else (),
        out_shape=shapes,
        in_specs=in_specs,
        out_specs=out_specs,
        scratch_shapes=scratch,
        input_output_aliases=aliases,
        compiler_params=pltpu.CompilerParams(vmem_limit_bytes=30 * 2**20),
        cost_estimate=pl.CostEstimate(flops=cost, bytes_accessed=0, transcendentals=0),
        name=f"level{level}_rows{sum(counts)}",
    )(meta, *arrays, *hidden)


def run_two_levels(meta, inv, ours, theirs, near, near_x, first_outs, second_outs, pairs):
    width, size = near.shape[1], inv.shape[1]
    rows = [sum(job[2] for job in dest) for dest in second_outs] + [size]
    vmem = pl.BlockSpec(memory_space=pltpu.VMEM)
    kernel = functools.partial(
        two_level_kernel,
        blocks=width // BLOCK,
        counts=tuple(x.shape[0] for x in ours),
        first_outs=first_outs,
        second_outs=second_outs,
        pairs=pairs,
    )
    return pl.pallas_call(
        kernel,
        out_shape=[jax.ShapeDtypeStruct((n, width), BF16) for n in rows],
        in_specs=[pl.BlockSpec(memory_space=pltpu.SMEM)] + [vmem] * (3 + 2 * len(ours)),
        out_specs=[vmem] * len(rows),
        scratch_shapes=[
            pltpu.VMEM((size, width), BF16),
            pltpu.VMEM((size, width), F32),
            pltpu.VMEM(near.shape, BF16),
            pltpu.VMEM(near_x.shape, BF16),
        ],
        compiler_params=pltpu.CompilerParams(vmem_limit_bytes=30 * 2**20),
        cost_estimate=pl.CostEstimate(flops=0, bytes_accessed=0, transcendentals=0),
        name="level0_level1",
    )(meta, inv, *ours, *theirs, near, near_x)


def reorder(meta, pivot_inverse):
    step = meta.shape[0] // LEVELS
    return pl.pallas_call(
        functools.partial(reorder_kernel, step=step),
        out_shape=jax.ShapeDtypeStruct(pivot_inverse.shape, BF16),
        in_specs=[pl.BlockSpec(memory_space=pltpu.SMEM), pl.BlockSpec(memory_space=pltpu.VMEM)],
        out_specs=pl.BlockSpec(memory_space=pltpu.VMEM),
        compiler_params=pltpu.CompilerParams(vmem_limit_bytes=30 * 2**20),
        cost_estimate=pl.CostEstimate(flops=0, bytes_accessed=0, transcendentals=0),
        name="reorder",
    )(meta, pivot_inverse)


def make_meta(size, block_pattern, column_order, pivot_blocks):
    blocks = column_order.shape[1]
    rank = jnp.int32(0)
    meta = []
    for level in range(LEVELS):
        bit = my_bit(level)
        rank = rank + bit * (1 << level)
        shift = rank * (size >> (level + 1))
        meta += [
            column_order[level],
            jnp.where(bit == 0, block_pattern[level, 0], block_pattern[level, 1]),
            jnp.where(bit == 0, block_pattern[level, 1], block_pattern[level, 0]),
            pivot_blocks[level],
            jnp.zeros((blocks,), jnp.int32) + shift,
        ]
    return jnp.concatenate(meta)


def on_device(schur_slab, pivot_inverse, block_pattern, column_order, pivot_blocks):
    all_rows = schur_slab.shape[0]
    size = pivot_inverse.shape[1]
    half, quarter, eighth, share = size // 2, size // 4, size // 8, size // 16
    meta = make_meta(size, block_pattern, column_order, pivot_blocks)

    def rows_of(x):
        return [(x, 0, x.shape[0])]

    def chunk(level, panel, own, other, **more):
        (out,) = run_level(
            level, meta, (inv, panel), [[(0, 0, own.shape[0])]], pairs=[(rows_of(own), rows_of(other))], **more
        )
        return out

    cut_1 = quarter + share
    cut_2 = half + quarter
    begin_1 = schur_slab[:cut_1]
    first_z1 = trade(begin_1, 1)
    begin_y1 = trade(begin_1, 0)
    slab, begin_1 = after(schur_slab, begin_1)
    begin_2, begin_3, rest_2 = slab[cut_1:half], slab[half:cut_2], slab[cut_2:]
    begin_y2, begin_y3 = trade(begin_2, 0), trade(begin_3, 0)
    inv = reorder(meta, pivot_inverse)

    first_yz1 = trade(first_z1, 0)
    first_2, first_z1 = after(begin_2, first_z1)
    first_z2 = trade(first_2, 1)
    rest_2, begin_y3 = after(rest_2, begin_y3)

    tops = [("top", 0, quarter), ("top", half, quarter)]
    begun = ((begin_1, begin_2, begin_3), (begin_y1, begin_y2, begin_y3))
    near, near_x, after_1, panel_0 = run_level(
        0,
        meta,
        (inv,),
        [tops, [("top", quarter, quarter)], [(0, 0, quarter)]],
        top=tuple(rows_of(x) + rows_of(y) for x, y, _ in begun),
        pairs=[tuple(rows_of(x) for *_, x in begun)],
        keeps=True,
    )
    first_z2, after_1 = after(first_z2, after_1)
    after_z1 = trade(after_1, 1)
    first_z2, first_yz1 = after(first_z2, first_yz1)
    first_yz2 = trade(first_z2, 0)
    rest_2, first_yz2 = after(rest_2, first_yz2)
    rest_y2 = trade(rest_2, 0)

    e, y, z, yz = (("top", low, eighth) for low in range(0, size, quarter))
    jobs = [[e, (*y[:2], share)], [("top", quarter + share, share), z], [yz, (0, 0, share)]]
    jobs.append([(0, share, share), (1, 0, quarter)])
    *head, next_0, panel_1 = run_two_levels(
        meta,
        inv,
        (first_z1, first_z2),
        (first_yz1, first_yz2),
        near,
        near_x,
        (tuple(tops), (("top", quarter, quarter),)),
        jobs,
        ((0, eighth, eighth), (1, 0, quarter)),
    )
    head_c = [trade(x, 2) for x in head]

    tops = [("top", low, share) for low in range(0, size, eighth)]
    first, lead, others, panel_2 = run_level(
        2,
        meta,
        (inv,),
        [[tops[0]], [("top", share, share), (0, 0, share)], tops[1:]],
        top=tuple(
            rows_of(group[0]) + rows_of(group[1]) + [(group[2], 0, eighth)] for group in (head, head_c)
        ),
        pairs=[tuple([(group[2], eighth, share)] for group in (head, head_c))],
        keeps=True,
    )
    first_w, lead_w = trade(first, 3), trade(lead, 3)
    after_z1, rest_y2, lead = after(after_z1, rest_y2, lead)
    next_1 = run_level(
        1,
        meta,
        (inv, panel_1),
        [[(0, 0, eighth)], [(0, eighth, eighth)]],
        pairs=[(rows_of(after_1), rows_of(after_z1))],
        cost=10**10,
    )
    next_1 = [next_0, *next_1]
    next_c1 = [trade(x, 2) for x in next_1]
    after_2 = chunk(0, panel_0, rest_2, rest_y2, cost=0)
    after_z2 = trade(after_2, 1)
    next_c1[0], after_2 = after(next_c1[0], after_2)
    (last_1,) = run_level(
        2,
        meta,
        (inv, panel_2),
        [[(i, 0, x.shape[0]) for i, x in enumerate(next_1)]],
        pairs=[(rows_of(x), rows_of(y)) for x, y in zip(next_1, next_c1)],
    )
    last_w1 = trade(last_1, 3)
    first_wz = trade(first_w, 1)
    after_z2, first_wz, lead_w = after(after_z2, first_wz, lead_w)
    tops_w = jnp.concatenate([first_w, first_wz], axis=0)
    tops_wc = trade(tops_w, 2)
    tops_wy = trade(tops_w, 0)
    tops_wyc = trade(tops_wy, 2)
    next_2 = chunk(1, panel_1, after_2, after_z2, cost=5 * 10**9)
    last_2 = chunk(2, panel_2, next_2, trade(next_2, 2))
    last_w2 = trade(last_2, 3)
    tops = [(first, 0, share)] + [(others, share * i, share) for i in range(7)]
    tops_other = [(x, low, share) for low in (0, share) for x in (tops_w, tops_wy)]
    tops_other += [(x, low, share) for low in (0, share) for x in (tops_wc, tops_wyc)]
    out, panel_3 = run_level(
        3,
        meta,
        (inv,),
        [[("top", 0, share), (0, 0, eighth), (1, 0, last_1.shape[0])]],
        top=(tops, tops_other),
        pairs=[(rows_of(lead), rows_of(lead_w)), (rows_of(last_1), rows_of(last_w1))],
        keeps=True,
        part=(all_rows, 0, None),
        cost=5 * 10**10,
    )
    return run_last(3, meta, inv, panel_3, last_2, last_w2, all_rows - quarter, out)


def solution(mesh):
    return jax.shard_map(
        on_device,
        mesh=mesh,
        in_specs=(P(("tx", "ty"), None), P(), P(), P(), P()),
        out_specs=P(("tx", "ty"), None),
        check_vma=False,
    )
```
